256 devices in a mesh: lon: 16 (over z, core), lat: 8 (over y, x_lo), tp: 2 (over x_hi).
Axes of the slice: x: 4 (x_hi: 2, x_lo: 2; x = x_hi * 2 + x_lo), y: 4, z: 8, core: 2. Of those that a mesh axis runs over, the one named last changes fastest.
Arguments:
- latent: bfloat16 [2, 48, 768, 512], P(None, 'lat', 'lon'), may hold values from -6 to 6
- pole_mask: int32 [48], replicated, may hold values from 0 to 1, as said below
- attn_gain: float32 [512], replicated, may hold values from 0.25 to 1.75
- qkv_weight: bfloat16 [512, 3, 512], P(None, None, 'tp'), may hold values from -0.44194174 to 0.44194174
- proj_weight: bfloat16 [512, 512], P('tp'), may hold values from -0.25 to 0.25
- rel_bias: float32 [8, 759], P('tp'), may hold values from -4 to 4
- merge_gain: float32 [2048], replicated, may hold values from 0.25 to 1.75
- merge_weight: bfloat16 [2048, 1024], P(None, 'tp'), may hold values from -0.125 to 0.125
- coarse_grad: bfloat16 [2, 24, 384, 1024], P(None, 'lat', 'lon', 'tp'), may hold values from -6 to 6
Outputs:
- latent_grad: bfloat16 [2, 48, 768, 512], P(None, 'lat', 'lon')
- attn_gain_grad: float32 [512], replicated
- qkv_weight_grad: float32 [512, 3, 512], P(('lon', 'lat'), None, 'tp')
- proj_weight_grad: float32 [512, 512], P('tp', ('lon', 'lat'))
- rel_bias_grad: float32 [8, 759], P('tp')
- merge_gain_grad: float32 [2048], replicated
- merge_weight_grad: float32 [2048, 1024], P(('lon', 'lat'), 'tp')
The draws below stay inside these ranges and needn't reach their ends.
Inputs may be any that keep to these rules, and one draw needn't show every extreme that they name: `pole_mask`: between 1 and 2 rows at each end of the 48 rows are 0, all others 1.
All inputs are finite; a program needn't handle non-finite values.
Results may differ from the reference program's by a relative error of at most 0.025.
Values may be sent and summed in bfloat16 or wider, within the bound.
A program may use at most 128 MiB of HBM per device.

```python
import jax
import jax.numpy as jnp
from jax import lax

D = 512
HEADS = 8
DC = 1024
LEV = 2
WLAT = 6
WLON = 12
LAT_DEV = 6
LON_DEV = 48
NLAT = 48
NLON = 768
NREL = 759


def draw_pole_mask(key, part):
    key = jax.random.fold_in(key, 7)
    padded = jax.random.randint(key, (2,), 1, 3)
    positions = jnp.arange(NLAT, dtype=jnp.int32)
    return ((positions >= padded[0]) & (positions < NLAT - padded[1])).astype(jnp.int32)


def draw_qkv_weight(key, part):
    key = jax.random.fold_in(key, 11)
    key_query = jax.random.fold_in(key, 0)
    unit = D ** (-0.5)
    limit = 10.0 * unit
    whole = jax.random.normal(key_query, (D, 3, HEADS, D // HEADS), jnp.float32) * unit
    return jnp.clip(whole, -limit, limit).reshape(D, 3, D).astype(jnp.bfloat16)


def steps_of(rng, extent, cuts, low, high):
    factor_of = 1.0
    for axis_at, shards_of in cuts:
        draws = jax.random.uniform(jax.random.fold_in(jax.random.fold_in(rng, 6), axis_at), (shards_of,), jnp.float32, low / len(cuts), high / len(cuts))
        factor_of = factor_of * jnp.repeat(jnp.exp(draws), extent[axis_at] // shards_of).reshape((-1,) + (1,) * (len(extent) - 1 - axis_at))
    return factor_of


def gaussian(stream_key, dims, width, most, pieces=(), kind=jnp.bfloat16):
    loudness = steps_of(stream_key, dims, pieces, -0.22, 0.18) if pieces else 1.0
    values = jax.random.normal(stream_key, dims, jnp.float32) * width * loudness
    return jnp.minimum(jnp.maximum(values, -most), most).astype(kind)


def setup_inputs(seed: int = 0) -> dict:
    seeds = jax.random.split(jax.random.key(seed), 10)
    latent = gaussian(seeds[0], (LEV, NLAT, NLON, D), 1.0, 6.0, ((1, 8), (2, 16)))
    pole_mask = draw_pole_mask(jax.random.fold_in(seeds[9], 71), 0)
    attn_gain = jnp.clip(1.0 + 0.15 * jax.random.normal(seeds[2], (D,), jnp.float32), 0.25, 1.75)
    qkv_weight = draw_qkv_weight(jax.random.fold_in(seeds[9], 71), 0)
    proj_weight = gaussian(seeds[4], (D, D), D ** -0.5, 0.25, ((0, 2),))
    rel_bias = gaussian(seeds[5], (HEADS, NREL), 1.0, 4.0, ((0, 2),), jnp.float32)
    merge_gain = jnp.clip(1.0 + 0.15 * jax.random.normal(seeds[6], (4 * D,), jnp.float32), 0.25, 1.75)
    merge_weight = gaussian(seeds[7], (4 * D, DC), (4 * D) ** -0.5, 0.125, ((1, 2),))
    coarse_grad = gaussian(seeds[8], (LEV, NLAT // 2, NLON // 2, DC), 1.0, 6.0, ((1, 8), (2, 16), (3, 2)))
    return dict(latent=latent, pole_mask=pole_mask, attn_gain=attn_gain, qkv_weight=qkv_weight, proj_weight=proj_weight, rel_bias=rel_bias, merge_gain=merge_gain, merge_weight=merge_weight, coarse_grad=coarse_grad)


EPS = 1e-05
NEG = -1e+30

def layer_stats(inputs):
    center = inputs - lax.optimization_barrier(jnp.mean(inputs, -1, keepdims=True))
    spread = lax.optimization_barrier(jnp.mean(center * center, -1, keepdims=True))
    inverse = lax.rsqrt(spread + EPS)
    return (center * inverse, inverse)

def norm_back(upstream, gain, normed, inverse):
    scaled = upstream * gain
    return inverse * (scaled - lax.optimization_barrier(jnp.mean(scaled, -1, keepdims=True)) - normed * lax.optimization_barrier(jnp.mean(scaled * normed, -1, keepdims=True)))

def to_windows(grid, win_lat, win_lon):
    levels, lat_rows, lon_cols, features = grid.shape
    grid = grid.reshape(levels, lat_rows // win_lat, win_lat, lon_cols // win_lon, win_lon, features)
    return grid.transpose(1, 3, 0, 2, 4, 5).reshape(-1, levels * win_lat * win_lon, features)

def from_windows(blocks, levels, lat_rows, lon_cols, win_lat, win_lon):
    features = blocks.shape[-1]
    blocks = blocks.reshape(lat_rows // win_lat, lon_cols // win_lon, levels, win_lat, win_lon, features)
    return blocks.transpose(2, 0, 3, 1, 4, 5).reshape(levels, lat_rows, lon_cols, features)

def merge_patches(grid):
    levels, lat_rows, lon_cols, features = grid.shape
    grid = grid.reshape(levels, lat_rows // 2, 2, lon_cols // 2, 2, features).transpose(0, 1, 3, 2, 4, 5)
    return grid.reshape(levels, lat_rows // 2, lon_cols // 2, 4 * features)

def split_patches(grid):
    levels, half_rows, half_cols, features = grid.shape
    grid = grid.reshape(levels, half_rows, half_cols, 2, 2, features // 4).transpose(0, 1, 3, 2, 4, 5)
    return grid.reshape(levels, 2 * half_rows, 2 * half_cols, features // 4)

def relative_index(levels, win_lat, win_lon):
    position = jnp.arange(levels * win_lat * win_lon, dtype=jnp.int32)
    level_of = position // (win_lat * win_lon)
    row_of = position // win_lon % win_lat
    col_of = position % win_lon
    level_gap = level_of[:, None] - level_of[None, :] + levels - 1
    row_gap = row_of[:, None] - row_of[None, :] + win_lat - 1
    col_gap = col_of[:, None] - col_of[None, :] + win_lon - 1
    return ((level_gap * (2 * win_lat - 1) + row_gap) * (2 * win_lon - 1) + col_gap).astype(jnp.int32)

def window_allowed(valid, side):
    return valid[:, None, :] & (side[:, :, None] == side[:, None, :])

def sublayer(latent_w, allowed, w_flat, proj_weight, bias_block, attn_gain, heads):
    groups, wtok, features = latent_w.shape
    x_float = latent_w.astype(jnp.float32)
    normed, inverse = layer_stats(x_float)
    hidden = (normed * attn_gain).astype(jnp.bfloat16)
    qkv = jnp.dot(hidden.reshape(-1, features), w_flat, preferred_element_type=jnp.float32).astype(jnp.bfloat16)
    qkv = qkv.reshape(groups, wtok, 3, heads, -1)
    query, keys, values = (qkv[:, :, 0], qkv[:, :, 1], qkv[:, :, 2])
    scale = query.shape[-1] ** (-0.5)
    scores = jnp.einsum('wqhd,wkhd->whqk', query.astype(jnp.float32), keys.astype(jnp.float32)) * scale + bias_block[None]
    scores = jnp.where(allowed[:, None], scores, NEG)
    highest = lax.optimization_barrier(jnp.max(scores, -1, keepdims=True))
    expd = jnp.exp(scores - highest)
    prob = expd / lax.optimization_barrier(jnp.sum(expd, -1, keepdims=True))
    prob_b = prob.astype(jnp.bfloat16)
    attn_o = jnp.einsum('whqk,wkhd->wqhd', prob_b.astype(jnp.float32), values.astype(jnp.float32)).astype(jnp.bfloat16)
    attn_o = attn_o.reshape(groups * wtok, features)
    result = (x_float + jnp.dot(attn_o, proj_weight, preferred_element_type=jnp.float32).reshape(x_float.shape)).astype(jnp.bfloat16)
    return (result, (normed, inverse, hidden, query, keys, values, prob, prob_b, attn_o, scale))

def sublayer_back(latent_w, allowed, grad_w, w_flat, proj_weight, bias_block, attn_gain, heads, rel, nrel):
    unused, saved = sublayer(latent_w, allowed, w_flat, proj_weight, bias_block, attn_gain, heads)
    normed, inverse, hidden, query, keys, values, prob, prob_b, attn_o, scale = saved
    groups, wtok, features = latent_w.shape
    grad_flat = grad_w.reshape(-1, features)
    d_out = jnp.dot(grad_flat, proj_weight.T, preferred_element_type=jnp.float32).astype(jnp.bfloat16)
    d_out = d_out.reshape(groups, wtok, heads, -1)
    d_proj = jnp.dot(attn_o.T, grad_flat, preferred_element_type=jnp.float32)
    d_prob = jnp.einsum('wqhd,wkhd->whqk', d_out.astype(jnp.float32), values.astype(jnp.float32))
    d_values = jnp.einsum('whqk,wqhd->wkhd', prob_b.astype(jnp.float32), d_out.astype(jnp.float32))
    d_scores = prob * (d_prob - lax.optimization_barrier(jnp.sum(d_prob * prob, -1, keepdims=True)))
    score_total = lax.optimization_barrier(jnp.sum(d_scores, 0)).reshape(heads, -1)
    d_bias = jax.ops.segment_sum(score_total.T, rel.reshape(-1), nrel).T
    d_scores_b = d_scores.astype(jnp.bfloat16).astype(jnp.float32)
    d_query = jnp.einsum('whqk,wkhd->wqhd', d_scores_b, keys.astype(jnp.float32)) * scale
    d_keys = jnp.einsum('whqk,wqhd->wkhd', d_scores_b, query.astype(jnp.float32)) * scale
    d_qkv = jnp.stack([d_query, d_keys, d_values], 2).astype(jnp.bfloat16).reshape(groups * wtok, -1)
    hidden_flat = hidden.reshape(-1, features)
    d_weight = jnp.dot(hidden_flat.T, d_qkv, preferred_element_type=jnp.float32)
    d_hidden = jnp.dot(d_qkv, w_flat.T, preferred_element_type=jnp.float32)
    normed_flat = normed.reshape(-1, features)
    d_gain = lax.optimization_barrier(jnp.sum(d_hidden * normed_flat, 0))
    branch = norm_back(d_hidden, attn_gain, normed_flat, inverse.reshape(-1, 1)).astype(jnp.bfloat16)
    return (branch.reshape(groups, wtok, features), d_weight, d_proj, d_bias, d_gain)

def reference(latent, pole_mask, attn_gain, qkv_weight, proj_weight, rel_bias, merge_gain, merge_weight, coarse_grad):
    half_lat = WLAT // 2
    half_lon = WLON // 2
    per_group = LAT_DEV // WLAT * (LON_DEV // WLON)
    rel = relative_index(LEV, WLAT, WLON)
    bias_block = jnp.take(rel_bias, rel, axis=1)
    w_flat = qkv_weight.reshape(D, 3 * D)
    rows_valid = jnp.roll(pole_mask, half_lat) > 0
    rows_side = jnp.arange(NLAT, dtype=jnp.int32) < half_lat
    grid_valid = jnp.broadcast_to(rows_valid[None, :, None, None], (LEV, NLAT, NLON, 1))
    grid_side = jnp.broadcast_to(rows_side[None, :, None, None], (LEV, NLAT, NLON, 1))
    allowed = window_allowed(to_windows(grid_valid, WLAT, WLON)[..., 0], to_windows(grid_side, WLAT, WLON)[..., 0])
    windows = allowed.shape[0]

    def grouped(blocks):
        return blocks.reshape((windows // per_group, per_group) + blocks.shape[1:])
    latent_w = to_windows(jnp.roll(latent, (half_lat, half_lon), (1, 2)), WLAT, WLON)

    def forward_group(pair):
        return sublayer(pair[0], pair[1], w_flat, proj_weight, bias_block, attn_gain, HEADS)[0]
    out_w = lax.map(forward_group, (grouped(latent_w), grouped(allowed)))
    out_grid = from_windows(out_w.reshape(latent_w.shape), LEV, NLAT, NLON, WLAT, WLON)
    out_grid = jnp.roll(out_grid, (-half_lat, -half_lon), (1, 2))
    merged = merge_patches(out_grid).astype(jnp.float32)
    merge_hat, merge_inv = layer_stats(merged)
    merge_hat = merge_hat.reshape(-1, 4 * D)
    merged_b = (merge_hat * merge_gain).astype(jnp.bfloat16)
    coarse_flat = coarse_grad.reshape(-1, DC)
    d_merged = jnp.dot(coarse_flat, merge_weight.T, preferred_element_type=jnp.float32)
    merge_weight_grad = jnp.dot(merged_b.T, coarse_flat, preferred_element_type=jnp.float32)
    merge_gain_grad = lax.optimization_barrier(jnp.sum(d_merged * merge_hat, 0))
    d_fine = norm_back(d_merged, merge_gain, merge_hat, merge_inv.reshape(-1, 1)).reshape(merged.shape)
    d_fine = split_patches(d_fine)
    grad_w = to_windows(jnp.roll(d_fine.astype(jnp.bfloat16), (half_lat, half_lon), (1, 2)), WLAT, WLON)

    def backward_group(carry, item):
        branch, d_weight, d_proj, d_bias, d_gain = sublayer_back(item[0], item[1], item[2], w_flat, proj_weight, bias_block, attn_gain, HEADS, rel, NREL)
        return ((carry[0] + d_weight, carry[1] + d_proj, carry[2] + d_bias, carry[3] + d_gain), branch)
    start = (jnp.zeros((D, 3 * D), jnp.float32), jnp.zeros((D, D), jnp.float32), jnp.zeros((HEADS, NREL), jnp.float32), jnp.zeros((D,), jnp.float32))
    totals, branch_w = lax.scan(backward_group, start, (grouped(latent_w), grouped(allowed), grouped(grad_w)))
    branch_grid = from_windows(branch_w.reshape(latent_w.shape), LEV, NLAT, NLON, WLAT, WLON)
    branch_grid = jnp.roll(branch_grid, (-half_lat, -half_lon), (1, 2))
    latent_grad = (d_fine + branch_grid.astype(jnp.float32)).astype(jnp.bfloat16)
    return (latent_grad, totals[3], totals[0].reshape(D, 3, D), totals[1], totals[2], merge_gain_grad, merge_weight_grad)
```

```python
import functools

import jax
import jax.numpy as jnp
import numpy as np
from jax import lax
from jax.experimental import pallas as pl
from jax.experimental.pallas import tpu as pltpu
from jax.sharding import PartitionSpec as P

EPS = 1e-05
NEG = -1e30
MESH = pl.DeviceIdType.MESH
BF = jnp.bfloat16
F32 = jnp.float32

LEV, ROWS, COLS, D = 2, 6, 48, 512
WLON = 12
NWIN = COLS // WLON
WTOK = LEV * ROWS * WLON
TOK = LEV * ROWS * COLS
HEADS = 4
HD = 64
DA = HEADS * HD
NREL = 759
NZ, NY = 8, 4


def onehot(rows, cols, pairs):
    out = np.zeros((rows, cols), np.float32)
    for r, c in pairs:
        out[r, c] = 1.0
    return out.astype(jnp.bfloat16)


def piece_lists(row_sets, pads):
    own_rows, next_rows = row_sets
    near, far = range(0, 42), range(42, 48)
    out, base = [], 0
    for (rows, cols), pad in zip(
        ((own_rows, near), (own_rows, far), (next_rows, near), (next_rows, far)), pads
    ):
        items = [(l, r, c) for l in range(LEV) for r in rows for c in cols]
        out.append([(base + n, it) for n, it in enumerate(items)])
        base += pad
    return out, base


@functools.lru_cache(None)
def tables():
    t = {}
    pieces, total = piece_lists((range(0, 4), range(2, 6)), (336, 48, 336, 48))
    t["Ql"] = onehot(
        total, TOK, [(p, (l * ROWS + r) * COLS + c) for pc in pieces for p, (l, r, c) in pc]
    )
    where = {}
    for n, pc in enumerate(pieces):
        for p, (l, r, c) in pc:
            rr = r + 4 if n < 2 else r - 2
            sc = c + 6 if n % 2 == 0 else c - 42
            where[(l, rr, sc)] = p

    def merge_at(l, rr, sc):
        return ((rr * 2 + sc % 2) * LEV + l) * 24 + sc // 2

    def window_at(l, rr, sc):
        return (sc // WLON) * WTOK + (l * ROWS + rr - 1) * WLON + sc % WLON

    band = [(l, rr, sc) for l in range(LEV) for rr in range(8) for sc in range(COLS)]
    inner = [k for k in band if 1 <= k[1] <= 6]
    t["PxM"] = onehot(768, total, [(merge_at(*k), where[k]) for k in band])
    t["Pxw"] = onehot(TOK, total, [(window_at(*k), where[k]) for k in inner])
    t["PwM"] = onehot(TOK, TOK, [(merge_at(*k) - 96, window_at(*k)) for k in inner])
    t["PMw"] = np.ascontiguousarray(t["PwM"].T)
    pads = (256, 48, 256, 48)
    pieces, total = piece_lists((range(0, 3), range(3, 6)), pads)
    out, back = [], []
    for n, pc in enumerate(pieces):
        for p, (l, r, c) in pc:
            rr = r + 4 if n < 2 else r - 2
            sc = c + 6 if n % 2 == 0 else c - 42
            out.append((p, window_at(l, rr, sc)))
            back.append(((l * ROWS + r) * COLS + c, p))
    t["Ppo"] = onehot(total, TOK, out)
    t["Pf"] = onehot(TOK, total, back)
    base, cpairs, cwhere = 0, [], {}
    for n, (rows, cols, pad) in enumerate(
        (
            ((0, 1), range(0, 21), 96),
            ((0, 1), range(21, 24), 16),
            ((1, 2), range(0, 21), 96),
            ((1, 2), range(21, 24), 16),
        )
    ):
        p = base
        for l in range(LEV):
            for r in rows:
                for c in cols:
                    cpairs.append((p, (l * 3 + r) * 24 + c))
                    cr = r + 2 if n < 2 else r - 1
                    cc = c + 3 if n % 2 == 0 else c - 21
                    cwhere[(cr, l, cc)] = p
                    p += 1
        base += pad
    t["Qc"] = onehot(base, 144, cpairs)
    t["Pc"] = onehot(
        192, base, [((cr * LEV + l) * 24 + cc, p) for (cr, l, cc), p in cwhere.items()]
    )
    ep = []
    for c in range(WLON):
        for j in range(WTOK):
            l2, r2, c2 = j // 72, j // 12 % 6, j % 12
            ep.append((c * WTOK + j, ((1 - l2) * 11 + 5 - r2) * 23 + c - c2 + 11))
    t["E"] = onehot(WLON * WTOK, 512, ep)
    return t


def mm(a, b):
    return lax.dot_general(a, b, (((1,), (0,)), ((), ())), preferred_element_type=F32)


def mm_nt(a, b):
    return lax.dot_general(a, b, (((1,), (1,)), ((), ())), preferred_element_type=F32)


def mm_tn(a, b):
    return lax.dot_general(a, b, (((0,), (0,)), ((), ())), preferred_element_type=F32)


def layer_stats(x):
    center = x - jnp.mean(x, -1, keepdims=True)
    inverse = lax.rsqrt(jnp.mean(center * center, -1, keepdims=True) + EPS)
    return center * inverse, inverse


def norm_back(up, gain, normed, inverse):
    s = up * gain
    return inverse * (
        s - jnp.mean(s, -1, keepdims=True) - normed * jnp.mean(s * normed, -1, keepdims=True)
    )


def head_mask(h, rows):
    lane = lax.broadcasted_iota(jnp.int32, (rows, DA), 1)
    return (lane >= h * HD) & (lane < (h + 1) * HD)


def stack_heads(x):
    zero = jnp.zeros_like(x)
    return jnp.concatenate(
        [jnp.where(head_mask(h, x.shape[0]), x, zero) for h in range(HEADS)], 0
    )


def vspec():
    return pl.BlockSpec(memory_space=pltpu.VMEM)


def call(kernel, name, ins, outs, scratch=(), cid=None, smem=0, flops=10**9):
    params = dict(vmem_limit_bytes=56 << 20)
    if cid is not None:
        params.update(collective_id=cid, has_side_effects=True)
    specs = [pl.BlockSpec(memory_space=pltpu.SMEM)] * smem + [vspec()] * (len(ins) - smem)
    return pl.pallas_call(
        kernel,
        out_shape=[jax.ShapeDtypeStruct(s, d) for s, d in outs],
        in_specs=specs,
        out_specs=[vspec()] * len(outs),
        scratch_shapes=list(scratch),
        compiler_params=pltpu.CompilerParams(**params),
        cost_estimate=pl.CostEstimate(flops=flops, bytes_accessed=8 << 20, transcendentals=0),
        name=name,
    )(*ins)


def device(dlon, dlat, dtp):
    nlon, nlat = lax.axis_size("lon"), lax.axis_size("lat")
    return (
        lax.rem(lax.axis_index("lon") + dlon + nlon, nlon),
        lax.rem(lax.axis_index("lat") + dlat + nlat, nlat),
        lax.rem(lax.axis_index("tp") + dtp, 2),
    )


def greet(partners):
    barrier = pltpu.get_barrier_semaphore()
    for d in partners:
        pl.semaphore_signal(barrier, inc=1, device_id=d, device_id_type=MESH)
    pl.semaphore_wait(barrier, len(partners))


def remote(src, dst, ss, rs, n, dev):
    return pltpu.make_async_remote_copy(
        src, dst, ss.at[n], rs.at[n], device_id=dev, device_id_type=MESH
    )


def kin(lat_ref, cg_ref, ql_ref, qc_ref, pc_ref, cc_ref, sp, sc, ss, rs):
    greet([device(s * o, s * a, 0) for s in (1, -1) for o, a in ((1, 0), (0, 1), (1, 1))])
    copies = []

    def send(n, lo, hi, clo, chi, dev):
        sp[lo:hi, :] = mm(ql_ref[lo:hi, :], lat_ref[...]).astype(BF)
        c = remote(sp.at[lo:hi], pc_ref.at[lo:hi], ss, rs, 2 * n, dev)
        c.start()
        sc[clo:chi, :] = mm(qc_ref[clo:chi, :], cg_ref[...]).astype(BF)
        k = remote(sc.at[clo:chi], cc_ref.at[clo:chi], ss, rs, 2 * n + 1, dev)
        k.start()
        copies.extend([c, k])

    send(0, 384, 720, 112, 208, device(0, 1, 0))
    send(1, 720, 768, 208, 224, device(1, 1, 0))
    send(2, 336, 384, 96, 112, device(1, 0, 0))
    pc_ref[0:336, :] = mm(ql_ref[0:336, :], lat_ref[...]).astype(BF)
    cc_ref[0:96, :] = mm(qc_ref[0:96, :], cg_ref[...]).astype(BF)
    for c in copies:
        c.wait()


def kdm(cc_ref, pc_ref, mw_ref, cm_ref, dm_ref):
    cm_ref[...] = mm(pc_ref[...], cc_ref[...]).astype(BF)
    for n in range(4):
        cols = slice(n * 512, (n + 1) * 512)
        dm_ref[:, cols] = mm_nt(cm_ref[...], mw_ref[cols, :]).astype(BF)


def kfwd(
    pole_ref, pc_ref, gain_ref, w_ref, proj_ref, tab_ref, e_ref, pxw_ref, pwm_ref,
    z_ref, qkv_ref, p_ref, hn_ref, ao_ref, bm, u, wide,
):
    for l in range(LEV):
        for r in range(ROWS):
            shift = (l * 11 + r) * 23
            row = tab_ref[...]
            if shift:
                row = pltpu.roll(row, 768 - shift, 1)
            for h in range(HEADS):
                n = h * 12 + l * ROWS + r
                u[n : n + 1, :] = row[h : h + 1, :512]
    t0 = u[...]
    hi = t0.astype(BF)
    rest = t0 - hi.astype(F32)
    mid = rest.astype(BF)
    low = (rest - mid.astype(F32)).astype(BF)
    split = jnp.concatenate([hi, mid, low], 0)
    for c in range(WLON):
        y = mm_nt(split, e_ref[c * WTOK : (c + 1) * WTOK, :])
        y = y[0:48] + y[48:96] + y[96:144]
        wide[0, pl.ds(c, 48, stride=WLON), :] = y[:, 0:128]
        wide[1, pl.ds(c, 48, stride=WLON), :] = jnp.concatenate(
            [y[:, 128:WTOK], jnp.zeros((48, 256 - WTOK), F32)], 1
        )
    band = lax.axis_index("lat")
    nrows = pole_ref.shape[0]
    i = lax.broadcasted_iota(jnp.int32, (WTOK, WTOK), 0)
    j = lax.broadcasted_iota(jnp.int32, (WTOK, WTOK), 1)
    ri, rj = lax.rem(lax.div(i, WLON), ROWS), lax.rem(lax.div(j, WLON), ROWS)
    valid = jnp.zeros((WTOK, WTOK), jnp.int32)
    for r in range(ROWS):
        flag = pole_ref[lax.rem(band * ROWS + (r - 3 + nrows), nrows)]
        valid = jnp.where(rj == r, flag, valid)
    cut = jnp.where(band == 0, 3, 0)
    same = jnp.where(ri < cut, 1, 0) == jnp.where(rj < cut, 1, 0)
    allowed = (valid > 0) & same
    for h in range(HEADS):
        rows = slice(h * WTOK, (h + 1) * WTOK)
        both = jnp.concatenate([wide[0, rows, :], wide[1, rows, 0 : WTOK - 128]], 1)
        bm[rows, :] = jnp.where(allowed, both, NEG)

    normed, _ = layer_stats(mm(pxw_ref[...], pc_ref[...]))
    hn_ref[...] = (normed * gain_ref[...]).astype(BF)
    qkv_ref[...] = mm(hn_ref[...], w_ref[...]).astype(BF)

    def window(w, carry):
        rows = pl.ds(pl.multiple_of(w * WTOK, 16), WTOK)
        q = qkv_ref[rows, 0:DA]
        k = qkv_ref[rows, DA : 2 * DA]
        v = qkv_ref[rows, 2 * DA : 3 * DA]
        s = mm_nt(stack_heads(q), k) * (HD**-0.5) + bm[...]
        e = jnp.exp(s - jnp.max(s, -1, keepdims=True))
        p = e / jnp.sum(e, -1, keepdims=True)
        p_ref[w] = p
        pb = p.astype(BF)
        vs = stack_heads(v)
        o = jnp.zeros((WTOK, DA), F32)
        for h in range(HEADS):
            at = slice(h * WTOK, (h + 1) * WTOK)
            o = o + mm(pb[at], vs[at])
        ao_ref[rows, :] = o.astype(BF)
        return carry

    lax.fori_loop(0, NWIN, window, 0)
    z_ref[...] = mm(mm(pwm_ref[...], ao_ref[...]).astype(BF), proj_ref[...]).astype(BF)


def kyx(z_ref, zp_ref, zh_ref, ss, rs):
    greet([device(0, 0, 1)] + [device(0, a, t) for a in (1, -1) for t in (0, 1)])
    copies = [
        remote(z_ref.at[480:576], zh_ref.at[0], ss, rs, 0, device(0, 1, 0)),
        remote(z_ref.at[480:576], zh_ref.at[1], ss, rs, 1, device(0, 1, 1)),
        remote(z_ref.at[0:96], zh_ref.at[2], ss, rs, 2, device(0, -1, 0)),
        remote(z_ref.at[0:96], zh_ref.at[3], ss, rs, 3, device(0, -1, 1)),
        remote(z_ref, zp_ref, ss, rs, 4, device(0, 0, 1)),
    ]
    for c in copies:
        c.start()
    for c in copies:
        c.wait()


def kmerge(
    pc_ref, pxm_ref, z_ref, zp_ref, zh_ref, dmo_ref, dmp_ref, cm_ref, gain_ref,
    dy_ref, gm_ref, mg_ref, y, mb,
):
    def total(lo, hi, a, b):
        x = mm(pxm_ref[lo:hi, :], pc_ref[...])
        y[lo:hi, :] = (x + (a.astype(F32) + b.astype(F32))).astype(BF)

    total(0, 96, zh_ref[0], zh_ref[1])
    total(96, 672, z_ref[...], zp_ref[...])
    total(672, 768, zh_ref[2], zh_ref[3])
    gain = gain_ref[...]
    acc = jnp.zeros((1, 4 * D), F32)
    for cr in range(4):
        slabs = [
            y[(2 * cr + rp) * 96 + cp * 48 : (2 * cr + rp) * 96 + cp * 48 + 48, :]
            for rp in (0, 1)
            for cp in (0, 1)
        ]
        hat, inv = layer_stats(jnp.concatenate(slabs, 1).astype(F32))
        at = slice(cr * 48, (cr + 1) * 48)
        dm = dmo_ref[at, :].astype(F32) + dmp_ref[at, :].astype(F32)
        if cr > 0:
            acc = acc + jnp.sum(dm * hat, 0, keepdims=True)
            mb[(cr - 1) * 48 : cr * 48, :] = (hat * gain).astype(BF)
        dy = norm_back(dm, gain, hat, inv).astype(BF)
        for q in range(4):
            r = 2 * cr + q // 2
            if 1 <= r <= 6:
                lo = (r - 1) * 96 + (q % 2) * 48
                dy_ref[lo : lo + 48, :] = dy[:, q * D : (q + 1) * D]
    mg_ref[...] = acc
    for n in range(4):
        at = slice(n * 512, (n + 1) * 512)
        gm_ref[at, :] = mm_tn(mb[:, at], cm_ref[48:192, :])


def kbwd(
    dy_ref, pmw_ref, proj_ref, w_ref, qkv_ref, p_ref, hn_ref, ao_ref, e_ref, ppo_ref,
    dhp_ref, dyp_ref, gq_ref, bias_ref, dyw, do, dqkv, dst, t, wide,
):
    scale = HD**-0.5
    dyw[...] = mm(pmw_ref[...], dy_ref[...]).astype(BF)
    do[...] = mm_nt(dyw[...], proj_ref[...]).astype(BF)
    dst[...] = jnp.zeros_like(dst)

    def window(w, carry):
        rows = pl.ds(pl.multiple_of(w * WTOK, 16), WTOK)
        q = qkv_ref[rows, 0:DA]
        k = qkv_ref[rows, DA : 2 * DA]
        v = qkv_ref[rows, 2 * DA : 3 * DA]
        p = p_ref[w]
        dos = stack_heads(do[rows, :])
        dp = mm_nt(dos, v)
        dv = mm_tn(p.astype(BF), dos)
        ds = p * (dp - jnp.sum(dp * p, -1, keepdims=True))
        dst[...] = dst[...] + ds
        dsb = ds.astype(BF)
        dk = mm_tn(dsb, stack_heads(q)) * scale
        ks = stack_heads(k)
        dq = jnp.zeros((WTOK, DA), F32)
        for h in range(HEADS):
            at = slice(h * WTOK, (h + 1) * WTOK)
            dq = dq + mm(dsb[at], ks[at])
        dqkv[rows, 0:DA] = (dq * scale).astype(BF)
        dqkv[rows, DA : 2 * DA] = dk.astype(BF)
        dqkv[rows, 2 * DA : 3 * DA] = dv.astype(BF)
        return carry

    lax.fori_loop(0, NWIN, window, 0)
    dh = mm_nt(dqkv[...], w_ref[...]).astype(BF)
    dhp_ref[...] = mm(ppo_ref[...], dh).astype(BF)
    dyp_ref[...] = mm(ppo_ref[...], dyw[...]).astype(BF)
    gq_ref[:, 0 : 3 * DA] = mm_tn(hn_ref[...], dqkv[...])
    gq_ref[:, 3 * DA :] = mm_tn(dyw[...], ao_ref[...])
    acc = jnp.zeros((48, 512), F32)
    wide[0] = dst[:, 0:128]
    wide[1, :, 0 : WTOK - 128] = dst[:, 128:WTOK]
    for c in range(WLON):
        rows = pl.ds(c, 48, stride=WLON)
        x = jnp.concatenate([wide[0, rows, :], wide[1, rows, :][:, 0 : WTOK - 128]], 1)
        hi = x.astype(BF)
        low = (x - hi.astype(F32)).astype(BF)
        y = mm(jnp.concatenate([hi, low], 0), e_ref[c * WTOK : (c + 1) * WTOK, :])
        acc = acc + y[0:48] + y[48:96]
    t[:, 0:512] = acc
    t[:, 512:768] = jnp.zeros((48, 256), F32)
    for h in range(HEADS):
        out = jnp.zeros((1, 768), F32)
        for g in range(12):
            row = t[h * 12 + g : h * 12 + g + 1, :]
            shift = (g // ROWS * 11 + g % ROWS) * 23
            out = out + (pltpu.roll(row, shift, 1) if shift else row)
        bias_ref[h : h + 1, :] = out


OUT = ((0, 256), (256, 304), (304, 560), (560, 608))
OUT_TO = ((0, 0), (-1, 0), (0, -1), (-1, -1))


def kout(dh_ref, dy_ref, dhr_ref, dyr_ref, ss, rs):
    greet(
        [device(0, 0, 1)]
        + [device(s * o, s * a, t) for s in (1, -1) for o, a in OUT_TO[1:] for t in (0, 1)]
    )
    copies = []
    for n in (2, 0, 3, 1):
        lo, hi = OUT[n]
        o, a = OUT_TO[n]
        at = slice(lo, hi)
        copies.append(
            remote(dh_ref.at[at], dhr_ref.at[1, at], ss, rs, n, device(o, a, 1))
        )
        if n:
            copies.append(
                remote(dh_ref.at[at], dhr_ref.at[0, at], ss, rs, 4 + n, device(o, a, 0))
            )
            copies.append(remote(dy_ref.at[at], dyr_ref.at[at], ss, rs, 8 + n, device(o, a, 0)))
    for c in copies:
        c.start()
    dhr_ref[0, 0:256, :] = dh_ref[0:256, :]
    dyr_ref[0:256, :] = dy_ref[0:256, :]
    for c in copies:
        c.wait()


def kfin(lat_ref, gain_ref, pf_ref, dhr_ref, dyr_ref, lg_ref, ag_ref):
    pf = pf_ref[...]
    normed, inv = layer_stats(lat_ref[...].astype(F32))
    dh = mm(pf, dhr_ref[0]) + mm(pf, dhr_ref[1])
    ag_ref[...] = jnp.sum(dh * normed, 0, keepdims=True)
    branch = norm_back(dh, gain_ref[...], normed, inv).astype(BF)
    lg_ref[...] = (mm(pf, dyr_ref[...]) + branch.astype(F32)).astype(BF)


def krs(
    gm_ref, gq_ref, sv_ref, om_ref, oq_ref, ov_ref,
    sm1, sq1, rm1, rq1, sv1,
    am, aq, sm2, sq2, rm2, rq2, sv2,
    bmm, bq, sm3, rm3, rq3, sv3,
    cm, cq, rm4, rq4, sv4, ss, rs,
):
    lon, lat, tp = lax.axis_index("lon"), lax.axis_index("lat"), lax.axis_index("tp")
    z, core = lax.div(lon, 2), lax.rem(lon, 2)
    yy, xx = lax.div(lat, 2), lax.rem(lat, 2)
    core_dev = (z * 2 + 1 - core, lat, tp)
    x_dev = (lon, yy * 2 + 1 - xx, tp)
    y_devs = [(lon, lax.rem(yy + k, NY) * 2 + xx, tp) for k in range(1, NY)]
    z_devs = [(lax.rem(z + k, NZ) * 2 + core, lat, tp) for k in range(1, NZ)]
    greet([core_dev, x_dev] + y_devs + z_devs)

    for iy in range(NY):
        for iz in range(NZ):
            sm1[iy, iz] = gm_ref[iz, 1 - core, iy].astype(BF)
        for iz in range(0, NZ, 2):
            pair = jnp.concatenate([gq_ref[iz, 1 - core, iy], gq_ref[iz + 1, 1 - core, iy]], 0)
            sq1[iy, iz * 8 : iz * 8 + 16, :] = pair.astype(BF)
    sv1[core] = sv_ref[...]
    copies = [
        remote(sm1, rm1, ss, rs, 0, core_dev),
        remote(sq1, rq1, ss, rs, 1, core_dev),
        remote(sv1.at[core], sv1.at[core], ss, rs, 2, core_dev),
    ]
    for c in copies:
        c.start()
    for c in copies:
        c.wait()
    sv2[yy] = sv1[0] + sv1[1]

    copies = []
    for k in range(1, NY):
        iy = lax.rem(yy + k, NY)
        for iz in range(NZ):
            sm2[k - 1, iz] = (gm_ref[iz, core, iy] + rm1[iy, iz].astype(F32)).astype(BF)
        for iz in range(0, NZ, 2):
            pair = jnp.concatenate([gq_ref[iz, core, iy], gq_ref[iz + 1, core, iy]], 0)
            at = slice(iz * 8, iz * 8 + 16)
            sq2[k - 1, at, :] = (pair + rq1[iy, at, :].astype(F32)).astype(BF)
        n = 3 * k
        for c in (
            remote(sm2.at[k - 1], rm2.at[k - 1], ss, rs, n, y_devs[k - 1]),
            remote(sq2.at[k - 1], rq2.at[k - 1], ss, rs, n + 1, y_devs[k - 1]),
            remote(sv2.at[yy], sv2.at[yy], ss, rs, n + 2, y_devs[k - 1]),
        ):
            c.start()
            copies.append(c)
    for iz in range(NZ):
        am[iz] = gm_ref[iz, core, yy] + rm1[yy, iz].astype(F32)
    for iz in range(0, NZ, 2):
        pair = jnp.concatenate([gq_ref[iz, core, yy], gq_ref[iz + 1, core, yy]], 0)
        at = slice(iz * 8, iz * 8 + 16)
        aq[at, :] = pair + rq1[yy, at, :].astype(F32)
    for c in copies:
        c.wait()
    sv3[z] = sv2[0] + sv2[1] + sv2[2] + sv2[3]
    for iz in range(NZ):
        acc = am[iz]
        for k in range(NY - 1):
            acc = acc + rm2[k, iz].astype(F32)
        bmm[iz] = acc
    acc = aq[...]
    for k in range(NY - 1):
        acc = acc + rq2[k].astype(F32)
    for iz in range(NZ):
        bq[iz] = acc[iz * 8 : iz * 8 + 8]

    copies = []
    for k in range(1, NZ):
        iz = lax.rem(z + k, NZ)
        sm3[k - 1] = bmm[iz].astype(BF)
        n = 9 + 3 * k
        for c in (
            remote(sm3.at[k - 1], rm3.at[k - 1], ss, rs, n, z_devs[k - 1]),
            remote(bq.at[iz], rq3.at[k - 1], ss, rs, n + 1, z_devs[k - 1]),
            remote(sv3.at[z], sv3.at[z], ss, rs, n + 2, z_devs[k - 1]),
        ):
            c.start()
            copies.append(c)
    for c in copies:
        c.wait()
    acc = sv3[0]
    for k in range(1, NZ):
        acc = acc + sv3[k]
    sv4[xx] = acc
    acc, accq = bmm[z], bq[z]
    for k in range(NZ - 1):
        acc = acc + rm3[k].astype(F32)
        accq = accq + rq3[k]
    cm[0] = acc[0:16]
    cm[1] = acc[16:32]
    cq[...] = accq

    copies = [
        remote(cm.at[1 - xx], rm4, ss, rs, 33, x_dev),
        remote(cq, rq4, ss, rs, 34, x_dev),
        remote(sv4.at[xx], sv4.at[xx], ss, rs, 35, x_dev),
    ]
    for c in copies:
        c.start()
    for c in copies:
        c.wait()
    om_ref[...] = cm[xx] + rm4[...]
    both = cq[...] + rq4[...]
    oq_ref[...] = jnp.where(xx == 0, both[0:4], both[4:8])
    ov_ref[...] = sv4[0] + sv4[1]


def reduce_weights(gm, gq, sv):
    nv = sv.shape
    scratch = [
        pltpu.VMEM((NY, NZ, 32, 512), BF), pltpu.VMEM((NY, 64, 1024), BF),
        pltpu.VMEM((NY, NZ, 32, 512), BF), pltpu.VMEM((NY, 64, 1024), BF),
        pltpu.VMEM((2,) + nv, F32),
        pltpu.VMEM((NZ, 32, 512), F32), pltpu.VMEM((64, 1024), F32),
        pltpu.VMEM((NY - 1, NZ, 32, 512), BF), pltpu.VMEM((NY - 1, 64, 1024), BF),
        pltpu.VMEM((NY - 1, NZ, 32, 512), BF), pltpu.VMEM((NY - 1, 64, 1024), BF),
        pltpu.VMEM((NY,) + nv, F32),
        pltpu.VMEM((NZ, 32, 512), F32), pltpu.VMEM((NZ, 8, 1024), F32),
        pltpu.VMEM((NZ - 1, 32, 512), BF), pltpu.VMEM((NZ - 1, 32, 512), BF),
        pltpu.VMEM((NZ - 1, 8, 1024), F32), pltpu.VMEM((NZ,) + nv, F32),
        pltpu.VMEM((2, 16, 512), F32), pltpu.VMEM((8, 1024), F32),
        pltpu.VMEM((16, 512), F32), pltpu.VMEM((8, 1024), F32), pltpu.VMEM((2,) + nv, F32),
        pltpu.SemaphoreType.DMA((36,)), pltpu.SemaphoreType.DMA((36,)),
    ]
    return call(
        krs, "weight_sums",
        [gm.reshape(NZ, 2, NY, 32, 512), gq.reshape(NZ, 2, NY, 8, 1024), sv],
        [((16, 512), F32), ((4, 1024), F32), (nv, F32)],
        scratch, cid=4,
    )


def local(
    latent, pole_mask, attn_gain, qkv_weight, proj_weight, rel_bias, merge_gain, merge_weight,
    coarse_grad,
):
    t = {k: jnp.asarray(v) for k, v in tables().items()}
    dma = pltpu.SemaphoreType.DMA
    lat = latent.reshape(TOK, D)
    w = qkv_weight.reshape(D, 3 * DA)
    gain = attn_gain.reshape(1, D)
    tab = jnp.pad(rel_bias, ((0, 0), (0, 768 - NREL)))

    pc, cc = call(
        kin, "way_in", [lat, coarse_grad.reshape(144, 512), t["Ql"], t["Qc"]],
        [((768, D), BF), ((224, 512), BF)],
        [pltpu.VMEM((768, D), BF), pltpu.VMEM((224, 512), BF), dma((6,)), dma((6,))], cid=1,
    )
    cm, dmo = call(
        kdm, "coarse_cotangent", [cc, t["Pc"], merge_weight],
        [((192, 512), BF), ((192, 4 * D), BF)],
    )
    dmp = lax.ppermute(dmo, "tp", [(0, 1), (1, 0)])
    z, qkv, p, hn, ao = call(
        kfwd, "attention_forward",
        [pole_mask, pc, gain, w, proj_weight, tab, t["E"], t["Pxw"], t["PwM"]],
        [
            ((TOK, D), BF), ((TOK, 3 * DA), BF), ((NWIN, HEADS * WTOK, WTOK), F32),
            ((TOK, D), BF), ((TOK, DA), BF),
        ],
        [
            pltpu.VMEM((HEADS * WTOK, WTOK), F32), pltpu.VMEM((48, 512), F32),
            pltpu.VMEM((2, HEADS * WTOK, 128), F32),
        ],
        smem=1, flops=4 * 10**9,
    )
    zp, zh = call(
        kyx, "attention_sums", [z], [((TOK, D), BF), ((4, 96, D), BF)], [dma((5,)), dma((5,))],
        cid=2,
    )
    dy, gm, mg = call(
        kmerge, "patch_merge",
        [pc, t["PxM"], z, zp, zh, dmo, dmp, cm, merge_gain.reshape(1, 4 * D)],
        [((TOK, D), BF), ((4 * D, 512), F32), ((1, 4 * D), F32)],
        [pltpu.VMEM((768, D), BF), pltpu.VMEM((144, 4 * D), BF)],
    )
    dhp, dyp, gq, bias = call(
        kbwd, "attention_backward",
        [dy, t["PMw"], proj_weight, w, qkv, p, hn, ao, t["E"], t["Ppo"]],
        [((608, D), BF), ((608, D), BF), ((D, 1024), F32), ((HEADS, 768), F32)],
        [
            pltpu.VMEM((TOK, D), BF), pltpu.VMEM((TOK, DA), BF), pltpu.VMEM((TOK, 3 * DA), BF),
            pltpu.VMEM((HEADS * WTOK, WTOK), F32), pltpu.VMEM((48, 768), F32),
            pltpu.VMEM((2, HEADS * WTOK, 128), F32),
        ],
    )
    dhr, dyr = call(
        kout, "way_out", [dhp, dyp], [((2, 608, D), BF), ((608, D), BF)], [dma((12,)), dma((12,))],
        cid=3,
    )
    lg, ag = call(
        kfin, "latent_cotangent", [lat, gain, t["Pf"], dhr, dyr],
        [((TOK, D), BF), ((1, D), F32)],
    )
    sv = jnp.concatenate([ag, mg, bias.reshape(1, HEADS * 768)], 1).reshape(44, 128)
    om, oq, ov = reduce_weights(gm, gq, jnp.pad(sv, ((0, 4), (0, 0))))
    ov = ov.reshape(-1)
    return (
        lg.reshape(latent.shape),
        ov[0:D],
        oq[:, 0 : 3 * DA].reshape(4, 3, DA),
        oq[:, 3 * DA :].T,
        ov[5 * D : 5 * D + HEADS * 768].reshape(HEADS, 768)[:, :NREL],
        ov[D : 5 * D],
        om,
    )


def solution(mesh):
    placed = (
        P(None, "lat", "lon", None),
        P(),
        P(),
        P(None, None, "tp"),
        P("tp", None),
        P("tp", None),
        P(),
        P(None, "tp"),
        P(None, "lat", "lon", "tp"),
    )
    return jax.shard_map(
        local,
        mesh=mesh,
        in_specs=placed,
        out_specs=(
            P(None, "lat", "lon", None),
            P(),
            P(("lon", "lat"), None, "tp"),
            P("tp", ("lon", "lat")),
            P("tp", None),
            P(),
            P(("lon", "lat"), "tp"),
        ),
        check_vma=False,
    )
```

```python
import functools

import jax
import jax.numpy as jnp
import numpy as np
from jax import lax
from jax.experimental import pallas as pl
from jax.experimental.pallas import tpu as pltpu
from jax.sharding import PartitionSpec as P

EPS = 1e-05
NEG = -1e30
MESH = pl.DeviceIdType.MESH
BF = jnp.bfloat16
F32 = jnp.float32

LEV, ROWS, COLS, D = 2, 6, 48, 512
WLON = 12
NWIN = COLS // WLON
WTOK = LEV * ROWS * WLON
TOK = LEV * ROWS * COLS
HEADS = 4
HD = 64
DA = HEADS * HD
NREL = 759
NZ, NY = 8, 4


(QL, QL2, QC, QC2, PC, PXM, PXW, PWM, PMW, PPO, PF, E0) = range(12)
MAPW = 768
IN_PADS = (336, 48, 336, 48)
OUT_PADS = (256, 48, 256, 48)
COARSE_PADS = (96, 16, 96, 16)


def pieces(row_sets, near, far, pads):
    base, out = 0, []
    parts = ((row_sets[0], near), (row_sets[0], far), (row_sets[1], near), (row_sets[1], far))
    for n, ((rows, cols), pad) in enumerate(zip(parts, pads)):
        p = base
        for l in range(LEV):
            for r in rows:
                for c in cols:
                    out.append((p, n, l, r, c))
                    p += 1
        base += pad
    return out


@functools.lru_cache(None)
def index_maps():
    t = np.full((24, MAPW), -1, np.int32)
    near, far = range(0, 42), range(42, 48)

    def merge_at(l, rr, sc):
        return ((rr * 2 + sc % 2) * LEV + l) * 24 + sc // 2

    def window_at(l, rr, sc):
        return (sc // WLON) * WTOK + (l * ROWS + rr - 1) * WLON + sc % WLON

    def seen(n, r, c):
        return (r + 4 if n < 2 else r - 2), (c + 6 if n % 2 == 0 else c - 42)

    for p, n, l, r, c in pieces((range(0, 4), range(2, 6)), near, far, IN_PADS):
        t[QL if n < 2 else QL2, (l * ROWS + r) * COLS + c] = p
        rr, sc = seen(n, r, c)
        t[PXM, p] = merge_at(l, rr, sc)
        if 1 <= rr <= 6:
            t[PXW, p] = window_at(l, rr, sc)
    for l in range(LEV):
        for rr in range(1, 7):
            for sc in range(COLS):
                t[PWM, window_at(l, rr, sc)] = merge_at(l, rr, sc) - 96
                t[PMW, merge_at(l, rr, sc) - 96] = window_at(l, rr, sc)
    for p, n, l, r, c in pieces((range(0, 3), range(3, 6)), near, far, OUT_PADS):
        rr, sc = seen(n, r, c)
        t[PPO, window_at(l, rr, sc)] = p
        t[PF, p] = (l * ROWS + r) * COLS + c
    for p, n, l, r, c in pieces((range(0, 2), range(1, 3)), range(0, 21), range(21, 24), COARSE_PADS):
        t[QC if n < 2 else QC2, (l * 3 + r) * 24 + c] = p
        cr = r + 2 if n < 2 else r - 1
        cc = c + 3 if n % 2 == 0 else c - 21
        t[PC, p] = (cr * LEV + l) * 24 + cc
    for c in range(WLON):
        for j in range(WTOK):
            l2, r2, c2 = j // 72, j // 12 % 6, j % 12
            t[E0 + c, ((1 - l2) * 11 + 5 - r2) * 23 + c - c2 + 11] = j
    return t


def pick(maps, n, rows, cols, base=0):
    at = lax.broadcasted_iota(jnp.int32, (rows, cols), 0) + base
    return jnp.where(at == maps[n : n + 1, 0:cols], 1.0, 0.0).astype(BF)


def mm(a, b):
    return lax.dot_general(a, b, (((1,), (0,)), ((), ())), preferred_element_type=F32)


def mm_nt(a, b):
    return lax.dot_general(a, b, (((1,), (1,)), ((), ())), preferred_element_type=F32)


def mm_tn(a, b):
    return lax.dot_general(a, b, (((0,), (0,)), ((), ())), preferred_element_type=F32)


def layer_stats(x):
    center = x - jnp.mean(x, -1, keepdims=True)
    inverse = lax.rsqrt(jnp.mean(center * center, -1, keepdims=True) + EPS)
    return center * inverse, inverse


def norm_back(up, gain, normed, inverse):
    s = up * gain
    return inverse * (
        s - jnp.mean(s, -1, keepdims=True) - normed * jnp.mean(s * normed, -1, keepdims=True)
    )


def head_mask(h, rows):
    lane = lax.broadcasted_iota(jnp.int32, (rows, DA), 1)
    return (lane >= h * HD) & (lane < (h + 1) * HD)


def stack_heads(x):
    zero = jnp.zeros_like(x)
    return jnp.concatenate(
        [jnp.where(head_mask(h, x.shape[0]), x, zero) for h in range(HEADS)], 0
    )


def vspec():
    return pl.BlockSpec(memory_space=pltpu.VMEM)


def call(kernel, name, ins, outs, scratch=(), cid=None, smem=0, flops=10**9, mib=16):
    params = dict(vmem_limit_bytes=mib << 20)
    if cid is not None:
        params.update(collective_id=cid, has_side_effects=True)
    specs = [pl.BlockSpec(memory_space=pltpu.SMEM)] * smem + [vspec()] * (len(ins) - smem)
    return pl.pallas_call(
        kernel,
        out_shape=[jax.ShapeDtypeStruct(s, d) for s, d in outs],
        in_specs=specs,
        out_specs=[vspec()] * len(outs),
        scratch_shapes=list(scratch),
        compiler_params=pltpu.CompilerParams(**params),
        cost_estimate=pl.CostEstimate(flops=flops, bytes_accessed=8 << 20, transcendentals=0),
        name=name,
    )(*ins)


def device(dlon, dlat, dtp):
    nlon, nlat = lax.axis_size("lon"), lax.axis_size("lat")
    return (
        lax.rem(lax.axis_index("lon") + dlon + nlon, nlon),
        lax.rem(lax.axis_index("lat") + dlat + nlat, nlat),
        lax.rem(lax.axis_index("tp") + dtp, 2),
    )


def greet(partners):
    barrier = pltpu.get_barrier_semaphore()
    for d in partners:
        pl.semaphore_signal(barrier, inc=1, device_id=d, device_id_type=MESH)
    pl.semaphore_wait(barrier, len(partners))


def remote(src, dst, ss, rs, n, dev):
    return pltpu.make_async_remote_copy(
        src, dst, ss.at[n], rs.at[n], device_id=dev, device_id_type=MESH
    )


def kin(
    maps, lat_ref, cg_ref, w_ref, proj_ref, tab_ref,
    pc_ref, cc_ref, wf, pf, tabs, sp, sc, ss, rs, ws, wr,
):
    tp, yy = lax.axis_index("tp"), lax.div(lax.axis_index("lat"), 2)
    peer = device(0, 0, 1)
    y_devs = [device(0, 2 * k, 0) for k in range(1, NY)]
    tabs[tp] = jnp.zeros((8, 768), F32)
    tabs[tp, 0:HEADS, 0:NREL] = tab_ref[...]
    greet(
        [peer]
        + y_devs
        + [device(s * o, s * a, 0) for s in (1, -1) for o, a in ((1, 0), (0, 1), (1, 1))]
    )
    at = pl.ds(pl.multiple_of(yy * 128, 128), 128)
    pat = pl.ds(pl.multiple_of(yy * 64, 64), 64)
    first = [
        remote(w_ref.at[:, at], wf.at[tp, :, at], ws, wr, 0, peer),
        remote(proj_ref.at[pat], pf.at[tp, pat], ws, wr, 1, peer),
        remote(tabs.at[tp], tabs.at[tp], ws, wr, 2, peer),
    ]
    for c in first:
        c.start()
    copies = []

    def send(n, m, k, lo, hi, clo, chi, dev):
        sp[lo:hi, :] = mm(pick(maps, m, hi - lo, TOK, lo), lat_ref[...]).astype(BF)
        c = remote(sp.at[lo:hi], pc_ref.at[lo:hi], ss, rs, 2 * n, dev)
        c.start()
        sc[clo:chi, :] = mm(pick(maps, k, chi - clo, 144, clo), cg_ref[...]).astype(BF)
        d = remote(sc.at[clo:chi], cc_ref.at[clo:chi], ss, rs, 2 * n + 1, dev)
        d.start()
        copies.extend([c, d])

    send(0, QL2, QC2, 384, 720, 112, 208, device(0, 1, 0))
    send(1, QL2, QC2, 720, 768, 208, 224, device(1, 1, 0))
    send(2, QL, QC, 336, 384, 96, 112, device(1, 0, 0))
    first[0].wait()
    first[1].wait()
    for k in range(1, NY):
        for n, ref in ((0, wf.at[1 - tp, :, at]), (1, pf.at[1 - tp, pat])):
            c = remote(ref, ref, ws, wr, 3 + 2 * (k - 1) + n, y_devs[k - 1])
            c.start()
            copies.append(c)
    pc_ref[0:336, :] = mm(pick(maps, QL, 336, TOK), lat_ref[...]).astype(BF)
    cc_ref[0:96, :] = mm(pick(maps, QC, 96, 144), cg_ref[...]).astype(BF)
    for n in range(3):
        wf[tp, n] = w_ref[n]
    pf[tp] = proj_ref[...]
    first[2].wait()
    for c in copies:
        c.wait()


def kdm(maps, cc_ref, mw_ref, cm_ref, dm_ref):
    cm_ref[...] = mm(pick(maps, PC, 192, 224), cc_ref[...]).astype(BF)
    for n in range(4):
        cols = slice(n * 512, (n + 1) * 512)
        dm_ref[:, cols] = mm_nt(cm_ref[...], mw_ref[cols, :]).astype(BF)


def kfwd(
    pole_ref, maps, pc_ref, gain_ref, wf, pf, tabs,
    y_ref, qkv_ref, p_ref, hn_ref, ao_ref, xw_ref, bm, u, wide,
):
    band = lax.axis_index("lat")
    nrows = pole_ref.shape[0]
    i = lax.broadcasted_iota(jnp.int32, (WTOK, WTOK), 0)
    j = lax.broadcasted_iota(jnp.int32, (WTOK, WTOK), 1)
    ri, rj = lax.rem(lax.div(i, WLON), ROWS), lax.rem(lax.div(j, WLON), ROWS)
    valid = jnp.zeros((WTOK, WTOK), jnp.int32)
    for r in range(ROWS):
        flag = pole_ref[lax.rem(band * ROWS + (r - 3 + nrows), nrows)]
        valid = jnp.where(rj == r, flag, valid)
    cut = jnp.where(band == 0, 3, 0)
    same = jnp.where(ri < cut, 1, 0) == jnp.where(rj < cut, 1, 0)
    allowed = (valid > 0) & same

    for g in range(2):
        for l in range(LEV):
            for r in range(ROWS):
                shift = (l * 11 + r) * 23
                row = tabs[g]
                if shift:
                    row = pltpu.roll(row, 768 - shift, 1)
                for h in range(HEADS):
                    n = (g * HEADS + h) * 12 + l * ROWS + r
                    u[n : n + 1, :] = row[h : h + 1, :512]
    t0 = u[...]
    hi = t0.astype(BF)
    rest = t0 - hi.astype(F32)
    mid = rest.astype(BF)
    low = (rest - mid.astype(F32)).astype(BF)
    split = jnp.concatenate([hi, mid, low], 0)
    for c in range(WLON):
        y = mm_nt(split, pick(maps, E0 + c, WTOK, 512))
        y = y[0:96] + y[96:192] + y[192:288]
        wide[0, pl.ds(c, 96, stride=WLON), :] = y[:, 0:128]
        wide[1, pl.ds(c, 96, stride=WLON), :] = jnp.concatenate(
            [y[:, 128:WTOK], jnp.zeros((96, 256 - WTOK), F32)], 1
        )
    for h in range(2 * HEADS):
        rows = slice(h * WTOK, (h + 1) * WTOK)
        both = jnp.concatenate([wide[0, rows, :], wide[1, rows, 0 : WTOK - 128]], 1)
        bm[h // HEADS, (h % HEADS) * WTOK : (h % HEADS + 1) * WTOK, :] = jnp.where(
            allowed, both, NEG
        )

    x = mm(pick(maps, PXW, TOK, 768), pc_ref[...])
    xw_ref[...] = x.astype(BF)
    normed, _ = layer_stats(x)
    hn_ref[...] = (normed * gain_ref[...]).astype(BF)
    for g in range(2):
        for n in range(3):
            qkv_ref[g, :, n * DA : (n + 1) * DA] = mm(hn_ref[...], wf[g, n]).astype(BF)

    def window(n, carry):
        g, w = lax.div(n, NWIN), lax.rem(n, NWIN)
        rows = pl.ds(pl.multiple_of(w * WTOK, 16), WTOK)
        q = qkv_ref[g, rows, 0:DA]
        k = qkv_ref[g, rows, DA : 2 * DA]
        v = qkv_ref[g, rows, 2 * DA : 3 * DA]
        s = mm_nt(stack_heads(q), k) * (HD**-0.5) + bm[g]
        e = jnp.exp(s - jnp.max(s, -1, keepdims=True))
        p = e / jnp.sum(e, -1, keepdims=True)
        p_ref[g, w] = p
        pb = p.astype(BF)
        vs = stack_heads(v)
        o = jnp.zeros((WTOK, DA), F32)
        for h in range(HEADS):
            at = slice(h * WTOK, (h + 1) * WTOK)
            o = o + mm(pb[at], vs[at])
        ao_ref[g, rows, :] = o.astype(BF)
        return carry

    lax.fori_loop(0, 2 * NWIN, window, 0)
    to_merge = pick(maps, PWM, TOK, TOK)
    y = mm(pick(maps, PXM, TOK, 768, 96), pc_ref[...])
    for g in range(2):
        y = y + mm(mm(to_merge, ao_ref[g]).astype(BF), pf[g])
    y_ref[...] = y.astype(BF)


def kmerge(
    y_ref, dmo_ref, dmp_ref, cm_ref, gain_ref, dy_ref, gm_ref, mg_ref, yh, mb, ss, rs
):
    nxt, prev = device(0, 1, 0), device(0, -1, 0)
    greet([nxt, prev])
    copies = [
        remote(y_ref.at[480:576], yh.at[0], ss, rs, 0, nxt),
        remote(y_ref.at[0:96], yh.at[1], ss, rs, 1, prev),
    ]
    for c in copies:
        c.start()
    gain = gain_ref[...]
    acc = jnp.zeros((1, 4 * D), F32)

    def slab(r, cp):
        lo = cp * 48
        if r == 0:
            return yh[0, lo : lo + 48, :]
        if r == 7:
            return yh[1, lo : lo + 48, :]
        lo += (r - 1) * 96
        return y_ref[lo : lo + 48, :]

    for cr in (1, 2, 0, 3):
        if cr == 0:
            for c in copies:
                c.wait()
        slabs = [slab(2 * cr + rp, cp) for rp in (0, 1) for cp in (0, 1)]
        hat, inv = layer_stats(jnp.concatenate(slabs, 1).astype(F32))
        at = slice(cr * 48, (cr + 1) * 48)
        dm = dmo_ref[at, :].astype(F32) + dmp_ref[at, :].astype(F32)
        if cr > 0:
            acc = acc + jnp.sum(dm * hat, 0, keepdims=True)
            mb[(cr - 1) * 48 : cr * 48, :] = (hat * gain).astype(BF)
        dy = norm_back(dm, gain, hat, inv).astype(BF)
        for q in range(4):
            r = 2 * cr + q // 2
            if 1 <= r <= 6:
                lo = (r - 1) * 96 + (q % 2) * 48
                dy_ref[lo : lo + 48, :] = dy[:, q * D : (q + 1) * D]
    mg_ref[...] = acc
    for n in range(4):
        at = slice(n * 512, (n + 1) * 512)
        gm_ref[at, :] = mm_tn(mb[:, at], cm_ref[48:192, :])


def ktail(
    maps, dy_ref, gain_ref, wf, pf, qkv_ref, p_ref, hn_ref, ao_ref, xw_ref, gm_ref, mg_ref,
    rp_ref, om_ref, oq_ref, ov_ref,
    dyw, do, dqkv, dst, t, wide, gq, lp, sv,
    sm1, sq1, rm1, rq1, sv1,
    am, aq, sm2, sq2, rm2, rq2, sv2,
    bmm, bq, sm3, rm3, rq3, sv3,
    cm, cq, rm4, rq4, sv4, ss, rs,
):
    lon, lat, tp = lax.axis_index("lon"), lax.axis_index("lat"), lax.axis_index("tp")
    z, core = lax.div(lon, 2), lax.rem(lon, 2)
    yy, xx = lax.div(lat, 2), lax.rem(lat, 2)
    core_dev = (z * 2 + 1 - core, lat, tp)
    x_dev = (lon, yy * 2 + 1 - xx, tp)
    y_devs = [(lon, lax.rem(yy + k, NY) * 2 + xx, tp) for k in range(1, NY)]
    z_devs = [(lax.rem(z + k, NZ) * 2 + core, lat, tp) for k in range(1, NZ)]
    outward = ((-1, 0), (0, -1), (-1, -1))
    greet(
        [core_dev, x_dev]
        + y_devs
        + z_devs
        + [device(s * o, s * a, 0) for s in (1, -1) for o, a in outward]
    )
    scale = HD**-0.5

    def start(copies):
        for c in copies:
            c.start()
        return copies

    def wait(copies):
        for c in copies:
            c.wait()

    for iy in range(NY):
        for iz in range(NZ):
            sm1[iy, iz] = gm_ref[iz, 1 - core, iy].astype(BF)
    m1 = start([remote(sm1, rm1, ss, rs, 0, core_dev)])

    dyw[...] = mm(pick(maps, PMW, TOK, TOK), dy_ref[...]).astype(BF)
    for g in range(2):
        do[g] = mm_nt(dyw[...], pf[g]).astype(BF)
    dst[...] = jnp.zeros_like(dst)

    def window(n, carry):
        g, w = lax.div(n, NWIN), lax.rem(n, NWIN)
        rows = pl.ds(pl.multiple_of(w * WTOK, 16), WTOK)
        q = qkv_ref[g, rows, 0:DA]
        k = qkv_ref[g, rows, DA : 2 * DA]
        v = qkv_ref[g, rows, 2 * DA : 3 * DA]
        p = p_ref[g, w]
        dos = stack_heads(do[g, rows, :])
        dp = mm_nt(dos, v)
        dv = mm_tn(p.astype(BF), dos)
        ds = p * (dp - jnp.sum(dp * p, -1, keepdims=True))
        dst[g] = dst[g] + ds
        dsb = ds.astype(BF)
        dk = mm_tn(dsb, stack_heads(q)) * scale
        ks = stack_heads(k)
        dq = jnp.zeros((WTOK, DA), F32)
        for h in range(HEADS):
            at = slice(h * WTOK, (h + 1) * WTOK)
            dq = dq + mm(dsb[at], ks[at])
        dqkv[g, 0, rows, :] = (dq * scale).astype(BF)
        dqkv[g, 1, rows, :] = dk.astype(BF)
        dqkv[g, 2, rows, :] = dv.astype(BF)
        return carry

    lax.fori_loop(0, NWIN, window, 0)

    wait(m1)
    m2 = []
    for k in range(1, NY):
        iy = lax.rem(yy + k, NY)
        for iz in range(NZ):
            sm2[k - 1, iz] = (gm_ref[iz, core, iy] + rm1[iy, iz].astype(F32)).astype(BF)
        m2 += start([remote(sm2.at[k - 1], rm2.at[k - 1], ss, rs, k, y_devs[k - 1])])
    for iz in range(NZ):
        am[iz] = gm_ref[iz, core, yy] + rm1[yy, iz].astype(F32)

    lax.fori_loop(NWIN, 2 * NWIN, window, 0)

    for n in range(3):
        part = mm_tn(hn_ref[...], dqkv[tp, n])
        for iz in range(NZ):
            for ic in range(2):
                for iy in range(NY):
                    lo = ((iz * 2 + ic) * NY + iy) * 8
                    gq[iz, ic, iy, :, n * DA : (n + 1) * DA] = part[lo : lo + 8, :]
    part = mm_tn(dyw[...], ao_ref[tp])
    for iz in range(NZ):
        for ic in range(2):
            for iy in range(NY):
                lo = ((iz * 2 + ic) * NY + iy) * 8
                gq[iz, ic, iy, :, 3 * DA :] = part[lo : lo + 8, :]
    for iy in range(NY):
        for iz in range(0, NZ, 2):
            pair = jnp.concatenate([gq[iz, 1 - core, iy], gq[iz + 1, 1 - core, iy]], 0)
            sq1[iy, iz * 8 : iz * 8 + 16, :] = pair.astype(BF)
    q1 = start([remote(sq1, rq1, ss, rs, 12, core_dev)])

    dh = jnp.zeros((TOK, D), F32)
    for g in range(2):
        for n in range(3):
            dh = dh + mm_nt(dqkv[g, n], wf[g, n])
    normed, inv = layer_stats(xw_ref[...].astype(F32))
    ag = jnp.sum(dh * normed, 0, keepdims=True)
    branch = norm_back(dh, gain_ref[...], normed, inv).astype(BF)
    lg = (dyw[...].astype(F32) + branch.astype(F32)).astype(BF)
    lp[...] = mm(pick(maps, PPO, 608, TOK), lg).astype(BF)
    ro = []
    for n, (lo, hi) in enumerate(((256, 304), (304, 560), (560, 608))):
        dev = device(outward[n][0], outward[n][1], 0)
        ro += start([remote(lp.at[lo:hi], rp_ref.at[lo:hi], ss, rs, 13 + n, dev)])
    rp_ref[0:256, :] = lp[0:256, :]

    wide[0] = dst[tp, :, 0:128]
    wide[1, :, 0 : WTOK - 128] = dst[tp, :, 128:WTOK]
    acc = jnp.zeros((48, 512), F32)
    for c in range(WLON):
        rows = pl.ds(c, 48, stride=WLON)
        x = jnp.concatenate([wide[0, rows, :], wide[1, rows, :][:, 0 : WTOK - 128]], 1)
        hi = x.astype(BF)
        low = (x - hi.astype(F32)).astype(BF)
        y = mm(jnp.concatenate([hi, low], 0), pick(maps, E0 + c, WTOK, 512))
        acc = acc + y[0:48] + y[48:96]
    t[:, 0:512] = acc
    t[:, 512:768] = jnp.zeros((48, 256), F32)
    for h in range(HEADS):
        out = jnp.zeros((1, 768), F32)
        for g in range(12):
            row = t[h * 12 + g : h * 12 + g + 1, :]
            shift = (g // ROWS * 11 + g % ROWS) * 23
            out = out + (pltpu.roll(row, shift, 1) if shift else row)
        sv[h : h + 1, :] = out
    sv[4:5, :] = mg_ref[:, 0:768]
    sv[5:6, :] = mg_ref[:, 768:1536]
    sv[6:7, 0:512] = mg_ref[:, 1536:2048]
    sv[6:7, 512:768] = jnp.zeros((1, 256), F32)
    sv[7:8, 0:512] = ag
    sv[7:8, 512:768] = jnp.zeros((1, 256), F32)
    sv1[core] = sv[...]
    v1 = start([remote(sv1.at[core], sv1.at[core], ss, rs, 16, core_dev)])

    wait(m2)
    for iz in range(NZ):
        acc = am[iz]
        for k in range(NY - 1):
            acc = acc + rm2[k, iz].astype(F32)
        bmm[iz] = acc
    m3 = []
    for k in range(1, NZ):
        sm3[k - 1] = bmm[lax.rem(z + k, NZ)].astype(BF)
        m3 += start([remote(sm3.at[k - 1], rm3.at[k - 1], ss, rs, 16 + k, z_devs[k - 1])])

    wait(q1)
    q2 = []
    for k in range(1, NY):
        iy = lax.rem(yy + k, NY)
        for iz in range(0, NZ, 2):
            pair = jnp.concatenate([gq[iz, core, iy], gq[iz + 1, core, iy]], 0)
            at = slice(iz * 8, iz * 8 + 16)
            sq2[k - 1, at, :] = (pair + rq1[iy, at, :].astype(F32)).astype(BF)
        q2 += start([remote(sq2.at[k - 1], rq2.at[k - 1], ss, rs, 23 + k, y_devs[k - 1])])
    for iz in range(0, NZ, 2):
        pair = jnp.concatenate([gq[iz, core, yy], gq[iz + 1, core, yy]], 0)
        at = slice(iz * 8, iz * 8 + 16)
        aq[at, :] = pair + rq1[yy, at, :].astype(F32)
    wait(v1)
    sv2[yy] = sv1[0] + sv1[1]
    v2 = start(
        [
            remote(sv2.at[yy], sv2.at[yy], ss, rs, 26 + k, y_devs[k - 1])
            for k in range(1, NY)
        ]
    )

    wait(m3)
    acc = bmm[z]
    for k in range(NZ - 1):
        acc = acc + rm3[k].astype(F32)
    cm[0] = acc[0:16]
    cm[1] = acc[16:32]
    m4 = start([remote(cm.at[1 - xx], rm4, ss, rs, 30, x_dev)])

    wait(q2)
    acc = aq[...]
    for k in range(NY - 1):
        acc = acc + rq2[k].astype(F32)
    for iz in range(NZ):
        bq[iz] = acc[iz * 8 : iz * 8 + 8]
    q3 = start(
        [
            remote(bq.at[lax.rem(z + k, NZ)], rq3.at[k - 1], ss, rs, 30 + k, z_devs[k - 1])
            for k in range(1, NZ)
        ]
    )
    wait(v2)
    sv3[z] = sv2[0] + sv2[1] + sv2[2] + sv2[3]
    v3 = start(
        [
            remote(sv3.at[z], sv3.at[z], ss, rs, 37 + k, z_devs[k - 1])
            for k in range(1, NZ)
        ]
    )
    wait(q3)
    acc = bq[z]
    for k in range(NZ - 1):
        acc = acc + rq3[k]
    cq[...] = acc
    q4 = start([remote(cq, rq4, ss, rs, 45, x_dev)])
    wait(v3)
    acc = sv3[0]
    for k in range(1, NZ):
        acc = acc + sv3[k]
    sv4[xx] = acc
    v4 = start([remote(sv4.at[xx], sv4.at[xx], ss, rs, 46, x_dev)])
    wait(m4)
    om_ref[...] = cm[xx] + rm4[...]
    wait(q4)
    oq_ref[...] = cq[...] + rq4[...]
    wait(v4)
    ov_ref[...] = sv4[0] + sv4[1]
    wait(ro)


def kend(
    maps, rp_ref, om_ref, oq_ref, ov_ref, lg_ref, ag_ref, gw_ref, gp_ref, gb_ref, mg_ref, gm_ref
):
    xx = lax.rem(lax.axis_index("lat"), 2)
    lg_ref[...] = mm(pick(maps, PF, TOK, 608), rp_ref[...]).astype(BF)
    gm_ref[...] = om_ref[...]
    mine = jnp.where(xx == 0, oq_ref[0:4, :], oq_ref[4:8, :])
    for n in range(3):
        gw_ref[n] = mine[:, n * DA : (n + 1) * DA]
    gp_ref[...] = mine[:, 3 * DA :]
    gb_ref[...] = ov_ref[0:HEADS, 0:NREL]
    mg_ref[:, 0:768] = ov_ref[4:5, :]
    mg_ref[:, 768:1536] = ov_ref[5:6, :]
    mg_ref[:, 1536:2048] = ov_ref[6:7, 0:512]
    ag_ref[...] = ov_ref[7:8, 0:512]


def local(
    latent, pole_mask, attn_gain, qkv_weight, proj_weight, rel_bias, merge_gain, merge_weight,
    coarse_grad,
):
    maps = jnp.asarray(index_maps())
    dma = pltpu.SemaphoreType.DMA
    lat = latent.reshape(TOK, D)
    gain = attn_gain.reshape(1, D)
    vm = pltpu.VMEM

    pc, cc, wf, pf, tabs = call(
        kin, "way_in",
        [maps, lat, coarse_grad.reshape(144, 512), qkv_weight.transpose(1, 0, 2), proj_weight, rel_bias],
        [
            ((768, D), BF), ((224, 512), BF), ((2, 3, D, DA), BF), ((2, DA, D), BF),
            ((2, 8, 768), F32),
        ],
        [vm((768, D), BF), vm((224, 512), BF), dma((6,)), dma((6,)), dma((9,)), dma((9,))],
        cid=1, mib=16,
    )
    cm, dmo = call(
        kdm, "coarse_cotangent", [maps, cc, merge_weight],
        [((192, 512), BF), ((192, 4 * D), BF)], mib=10,
    )
    dmp = lax.ppermute(dmo, "tp", [(0, 1), (1, 0)])
    nb = HEADS * WTOK
    y, qkv, p, hn, ao, xw = call(
        kfwd, "attention_forward", [pole_mask, maps, pc, gain, wf, pf, tabs],
        [
            ((TOK, D), BF), ((2, TOK, 3 * DA), BF), ((2, NWIN, nb, WTOK), F32),
            ((TOK, D), BF), ((2, TOK, DA), BF), ((TOK, D), BF),
        ],
        [vm((2, nb, WTOK), F32), vm((96, 512), F32), vm((2, 2 * nb, 128), F32)],
        smem=1, flops=8 * 10**9, mib=28,
    )
    dy, gm, mg = call(
        kmerge, "patch_merge", [y, dmo, dmp, cm, merge_gain.reshape(1, 4 * D)],
        [((TOK, D), BF), ((4 * D, 512), F32), ((1, 4 * D), F32)],
        [vm((2, 96, D), BF), vm((144, 4 * D), BF), dma((2,)), dma((2,))],
        cid=2, mib=20,
    )
    nv = (8, 768)
    rp, om, oq, ov = call(
        ktail, "attention_backward",
        [maps, dy, gain, wf, pf, qkv, p, hn, ao, xw, gm.reshape(NZ, 2, NY, 32, 512), mg],
        [((608, D), BF), ((16, 512), F32), ((8, 1024), F32), (nv, F32)],
        [
            vm((TOK, D), BF), vm((2, TOK, DA), BF), vm((2, 3, TOK, DA), BF),
            vm((2, nb, WTOK), F32), vm((48, 768), F32), vm((2, nb, 128), F32),
            vm((NZ, 2, NY, 8, 1024), F32), vm((608, D), BF), vm(nv, F32),
            vm((NY, NZ, 32, 512), BF), vm((NY, 64, 1024), BF),
            vm((NY, NZ, 32, 512), BF), vm((NY, 64, 1024), BF), vm((2,) + nv, F32),
            vm((NZ, 32, 512), F32), vm((64, 1024), F32),
            vm((NY - 1, NZ, 32, 512), BF), vm((NY - 1, 64, 1024), BF),
            vm((NY - 1, NZ, 32, 512), BF), vm((NY - 1, 64, 1024), BF), vm((NY,) + nv, F32),
            vm((NZ, 32, 512), F32), vm((NZ, 8, 1024), F32),
            vm((NZ - 1, 32, 512), BF), vm((NZ - 1, 32, 512), BF),
            vm((NZ - 1, 8, 1024), F32), vm((NZ,) + nv, F32),
            vm((2, 16, 512), F32), vm((8, 1024), F32),
            vm((16, 512), F32), vm((8, 1024), F32), vm((2,) + nv, F32),
            dma((48,)), dma((48,)),
        ],
        cid=3, mib=44,
    )
    lg, ag, gw, gp, gb, mgg, gmm = call(
        kend, "finish", [maps, rp, om, oq, ov],
        [
            ((TOK, D), BF), ((1, D), F32), ((3, 4, DA), F32), ((4, DA), F32),
            ((HEADS, NREL), F32), ((1, 4 * D), F32), ((16, 512), F32),
        ],
        mib=8,
    )
    return (
        lg.reshape(latent.shape),
        ag.reshape(D),
        gw.transpose(1, 0, 2),
        gp.T,
        gb,
        mgg.reshape(4 * D),
        gmm,
    )


def solution(mesh):
    placed = (
        P(None, "lat", "lon", None),
        P(),
        P(),
        P(None, None, "tp"),
        P("tp", None),
        P("tp", None),
        P(),
        P(None, "tp"),
        P(None, "lat", "lon", "tp"),
    )
    return jax.shard_map(
        local,
        mesh=mesh,
        in_specs=placed,
        out_specs=(
            P(None, "lat", "lon", None),
            P(),
            P(("lon", "lat"), None, "tp"),
            P("tp", ("lon", "lat")),
            P("tp", None),
            P(),
            P(("lon", "lat"), "tp"),
        ),
        check_vma=False,
    )
```

```python
import functools

import jax
import jax.numpy as jnp
import numpy as np
from jax import lax
from jax.experimental import pallas as pl
from jax.experimental.pallas import tpu as pltpu
from jax.sharding import PartitionSpec as P

EPS = 1e-05
NEG = -1e30
MESH = pl.DeviceIdType.MESH
BF = jnp.bfloat16
F32 = jnp.float32

LEV, ROWS, COLS, D = 2, 6, 48, 512
WLON = 12
NWIN = COLS // WLON
WTOK = LEV * ROWS * WLON
TOK = LEV * ROWS * COLS
HEADS = 4
HD = 64
DA = HEADS * HD
NREL = 759
NZ, NY = 8, 4


(QL, QL2, QC, QC2, PC, PXM, PXW, PWM, PMW, PPO, PF, E0) = range(12)
MAPW = 768
IN_PADS = (336, 48, 336, 48)
OUT_PADS = (256, 48, 256, 48)
COARSE_PADS = (96, 16, 96, 16)


def pieces(row_sets, near, far, pads):
    base, out = 0, []
    parts = ((row_sets[0], near), (row_sets[0], far), (row_sets[1], near), (row_sets[1], far))
    for n, ((rows, cols), pad) in enumerate(zip(parts, pads)):
        p = base
        for l in range(LEV):
            for r in rows:
                for c in cols:
                    out.append((p, n, l, r, c))
                    p += 1
        base += pad
    return out


@functools.lru_cache(None)
def index_maps():
    t = np.full((24, MAPW), -1, np.int32)
    near, far = range(0, 42), range(42, 48)

    def merge_at(l, rr, sc):
        return ((rr * 2 + sc % 2) * LEV + l) * 24 + sc // 2

    def window_at(l, rr, sc):
        return (sc // WLON) * WTOK + (l * ROWS + rr - 1) * WLON + sc % WLON

    def seen(n, r, c):
        return (r + 4 if n < 2 else r - 2), (c + 6 if n % 2 == 0 else c - 42)

    for p, n, l, r, c in pieces((range(0, 4), range(2, 6)), near, far, IN_PADS):
        t[QL if n < 2 else QL2, (l * ROWS + r) * COLS + c] = p
        rr, sc = seen(n, r, c)
        t[PXM, p] = merge_at(l, rr, sc)
        if 1 <= rr <= 6:
            t[PXW, p] = window_at(l, rr, sc)
    for l in range(LEV):
        for rr in range(1, 7):
            for sc in range(COLS):
                t[PWM, window_at(l, rr, sc)] = merge_at(l, rr, sc) - 96
                t[PMW, merge_at(l, rr, sc) - 96] = window_at(l, rr, sc)
    for p, n, l, r, c in pieces((range(0, 3), range(3, 6)), near, far, OUT_PADS):
        rr, sc = seen(n, r, c)
        t[PPO, window_at(l, rr, sc)] = p
        t[PF, p] = (l * ROWS + r) * COLS + c
    for p, n, l, r, c in pieces((range(0, 2), range(1, 3)), range(0, 21), range(21, 24), COARSE_PADS):
        t[QC if n < 2 else QC2, (l * 3 + r) * 24 + c] = p
        cr = r + 2 if n < 2 else r - 1
        cc = c + 3 if n % 2 == 0 else c - 21
        t[PC, p] = (cr * LEV + l) * 24 + cc
    for c in range(WLON):
        for j in range(WTOK):
            l2, r2, c2 = j // 72, j // 12 % 6, j % 12
            t[E0 + c, ((1 - l2) * 11 + 5 - r2) * 23 + c - c2 + 11] = j
    return t


def pick(maps, n, rows, cols, base=0):
    at = lax.broadcasted_iota(jnp.int32, (rows, cols), 0) + base
    return jnp.where(at == maps[n : n + 1, 0:cols], 1.0, 0.0).astype(BF)


def mm(a, b):
    return lax.dot_general(a, b, (((1,), (0,)), ((), ())), preferred_element_type=F32)


def mm_nt(a, b):
    return lax.dot_general(a, b, (((1,), (1,)), ((), ())), preferred_element_type=F32)


def mm_tn(a, b):
    return lax.dot_general(a, b, (((0,), (0,)), ((), ())), preferred_element_type=F32)


def layer_stats(x):
    center = x - jnp.mean(x, -1, keepdims=True)
    inverse = lax.rsqrt(jnp.mean(center * center, -1, keepdims=True) + EPS)
    return center * inverse, inverse


def norm_back(up, gain, normed, inverse):
    s = up * gain
    return inverse * (
        s - jnp.mean(s, -1, keepdims=True) - normed * jnp.mean(s * normed, -1, keepdims=True)
    )


def head_mask(h, rows):
    lane = lax.broadcasted_iota(jnp.int32, (rows, DA), 1)
    return (lane >= h * HD) & (lane < (h + 1) * HD)


def stack_heads(x):
    zero = jnp.zeros_like(x)
    return jnp.concatenate(
        [jnp.where(head_mask(h, x.shape[0]), x, zero) for h in range(HEADS)], 0
    )


def vspec():
    return pl.BlockSpec(memory_space=pltpu.VMEM)


def call(kernel, name, ins, outs, scratch=(), cid=None, smem=0, hbm=0, mib=16):
    params = dict(vmem_limit_bytes=mib << 20)
    if cid is not None:
        params.update(collective_id=cid, has_side_effects=True)
    specs = [pl.BlockSpec(memory_space=pltpu.SMEM)] * smem
    specs += [vspec()] * (len(ins) - smem - hbm) + [pl.BlockSpec(memory_space=pl.ANY)] * hbm
    return pl.pallas_call(
        kernel,
        out_shape=[jax.ShapeDtypeStruct(s, d) for s, d in outs],
        in_specs=specs,
        out_specs=[vspec()] * len(outs),
        scratch_shapes=list(scratch),
        compiler_params=pltpu.CompilerParams(**params),
        name=name,
    )(*ins)


def device(dlon, dlat, dtp):
    nlon, nlat = lax.axis_size("lon"), lax.axis_size("lat")
    return (
        lax.rem(lax.axis_index("lon") + dlon + nlon, nlon),
        lax.rem(lax.axis_index("lat") + dlat + nlat, nlat),
        lax.rem(lax.axis_index("tp") + dtp, 2),
    )


def remote(src, dst, ss, rs, n, dev):
    return pltpu.make_async_remote_copy(
        src, dst, ss.at[n], rs.at[n], device_id=dev, device_id_type=MESH
    )


class Links:
    def __init__(self, ss, rs):
        self.ss, self.rs, self.n = ss, rs, 0

    def send(self, src, dst, dev):
        c = remote(src, dst, self.ss, self.rs, self.n, dev)
        self.n += 1
        c.start()
        return c


def wait(copies):
    for c in copies:
        c.wait()


def kmain(
    pole_ref, maps, tab_ref, gain_ref, mgain_ref, lat_hbm, cg_hbm, w_hbm, proj_hbm, mw_hbm,
    rp_ref, om_ref, oq_ref, ov_ref, oa_ref,
    lat, cg, mw, wf, pf, tabs, et, bm, u, wide,
    sp, sc, pc, cc, cmt, dmo, dmp,
    xw, hn, qkv, pr, ao, y, yh, mb, dyt, mg,
    gm, dyw, do, dqkv, dst, t, gq, lp, sv, av,
    sm1, sq1, rm1, rq1, sv1, av1,
    am, aq, sm2, sq2, rm2, rq2, sv2, av2,
    bmm, bq, sm3, rm3, rq3, sv3, av3,
    cm, cq, rm4, rq4, sv4, av4, ls, ss, rs,
):
    lon, band, tp = lax.axis_index("lon"), lax.axis_index("lat"), lax.axis_index("tp")
    z, core = lax.div(lon, 2), lax.rem(lon, 2)
    yy, xx = lax.div(band, 2), lax.rem(band, 2)
    peer = device(0, 0, 1)
    core_dev = (z * 2 + 1 - core, band, tp)
    x_dev = (lon, yy * 2 + 1 - xx, tp)
    y_devs = [(lon, lax.rem(yy + k, NY) * 2 + xx, tp) for k in range(1, NY)]
    z_devs = [(lax.rem(z + k, NZ) * 2 + core, band, tp) for k in range(1, NZ)]
    near = [device(s * o, s * a, 0) for s in (1, -1) for o, a in ((1, 0), (0, 1), (1, 1))]
    partners = [peer, core_dev, x_dev] + y_devs + z_devs + near
    barrier = pltpu.get_barrier_semaphore()
    for dev in partners:
        pl.semaphore_signal(barrier, inc=1, device_id=dev, device_id_type=MESH)
    links = Links(ss, rs)
    scale = HD**-0.5
    other = 1 - tp

    loads = []
    for n, (src, into) in enumerate(
        ((lat_hbm, lat), (cg_hbm, cg), (w_hbm, wf.at[tp]), (proj_hbm, pf.at[tp]), (mw_hbm, mw))
    ):
        loads.append(pltpu.make_async_copy(src, into, ls.at[n]))
        loads[-1].start()

    nrows = pole_ref.shape[0]
    i = lax.broadcasted_iota(jnp.int32, (WTOK, WTOK), 0)
    j = lax.broadcasted_iota(jnp.int32, (WTOK, WTOK), 1)
    ri, rj = lax.rem(lax.div(i, WLON), ROWS), lax.rem(lax.div(j, WLON), ROWS)
    valid = jnp.zeros((WTOK, WTOK), jnp.int32)
    for r in range(ROWS):
        flag = pole_ref[lax.rem(band * ROWS + (r - 3 + nrows), nrows)]
        valid = jnp.where(rj == r, flag, valid)
    cut = jnp.where(band == 0, 3, 0)
    same = jnp.where(ri < cut, 1, 0) == jnp.where(rj < cut, 1, 0)
    allowed = (valid > 0) & same

    def build_bias(g):
        for l in range(LEV):
            for r in range(ROWS):
                shift = (l * 11 + r) * 23
                row = tabs[g]
                if shift:
                    row = pltpu.roll(row, 768 - shift, 1)
                for h in range(HEADS):
                    n = h * 12 + l * ROWS + r
                    u[n : n + 1, :] = row[h : h + 1, :512]
        t0 = u[...]
        hi = t0.astype(BF)
        rest = t0 - hi.astype(F32)
        mid = rest.astype(BF)
        low = (rest - mid.astype(F32)).astype(BF)
        split = jnp.concatenate([hi, mid, low], 0)
        for c in range(WLON):
            v = mm_nt(split, et[c * WTOK : (c + 1) * WTOK, :])
            v = v[0:48] + v[48:96] + v[96:144]
            wide[0, pl.ds(c, 48, stride=WLON), :] = v[:, 0:128]
            wide[1, pl.ds(c, 48, stride=WLON), :] = jnp.concatenate(
                [v[:, 128:WTOK], jnp.zeros((48, 256 - WTOK), F32)], 1
            )
        for h in range(HEADS):
            rows = slice(h * WTOK, (h + 1) * WTOK)
            both = jnp.concatenate([wide[0, rows, :], wide[1, rows, 0 : WTOK - 128]], 1)
            bm[g, rows, :] = jnp.where(allowed, both, NEG)

    tabs[tp] = jnp.zeros((8, 768), F32)
    tabs[tp, 0:HEADS, 0:NREL] = tab_ref[...]
    for c in range(WLON):
        et[c * WTOK : (c + 1) * WTOK, :] = pick(maps, E0 + c, WTOK, 512)
    build_bias(tp)

    loads[0].wait()
    loads[1].wait()
    for m, lo, hi in ((QL2, 384, 768), (QL, 336, 384)):
        sp[lo:hi, :] = mm(pick(maps, m, hi - lo, TOK, lo), lat[...]).astype(BF)
    for m, lo, hi in ((QC2, 112, 224), (QC, 96, 112)):
        sc[lo:hi, :] = mm(pick(maps, m, hi - lo, 144, lo), cg[...]).astype(BF)
    loads[2].wait()
    loads[3].wait()
    at = pl.ds(pl.multiple_of(yy * 128, 128), 128)
    pat = pl.ds(pl.multiple_of(yy * 64, 64), 64)
    pl.semaphore_wait(barrier, len(partners))
    halo = [links.send(sp.at[384:720], pc.at[384:720], device(0, 1, 0))]
    chalo = [links.send(sc.at[112:208], cc.at[112:208], device(0, 1, 0))]
    first = [
        links.send(wf.at[tp, :, at], wf.at[tp, :, at], peer),
        links.send(pf.at[tp, pat], pf.at[tp, pat], peer),
    ]
    tabc = [links.send(tabs.at[tp], tabs.at[tp], peer)]
    halo.append(links.send(sp.at[720:768], pc.at[720:768], device(1, 1, 0)))
    halo.append(links.send(sp.at[336:384], pc.at[336:384], device(1, 0, 0)))
    chalo.append(links.send(sc.at[208:224], cc.at[208:224], device(1, 1, 0)))
    chalo.append(links.send(sc.at[96:112], cc.at[96:112], device(1, 0, 0)))
    pc[0:336, :] = mm(pick(maps, QL, 336, TOK), lat[...]).astype(BF)
    cc[0:96, :] = mm(pick(maps, QC, 96, 144), cg[...]).astype(BF)
    loads[4].wait()
    wait(chalo)
    cmt[...] = mm(pick(maps, PC, 192, 224), cc[...]).astype(BF)
    for n in range(4):
        cols = slice(n * 512, (n + 1) * 512)
        dmo[:, cols] = mm_nt(cmt[...], mw[cols, :]).astype(BF)
    wait(first)
    ring = []
    for dev in y_devs:
        for ref in (wf.at[other, :, at], pf.at[other, pat]):
            ring.append(links.send(ref, ref, dev))
    wait(halo)
    dmc = [links.send(dmo, dmp, peer)]

    x = mm(pick(maps, PXW, TOK, 768), pc[...])
    xw[...] = x.astype(BF)
    normed, _ = layer_stats(x)
    hn[...] = (normed * gain_ref[...]).astype(BF)

    def forward(g):
        for n in range(3):
            qkv[g, :, n * DA : (n + 1) * DA] = mm(hn[...], wf[g, n]).astype(BF)

        def window(w, carry):
            rows = pl.ds(pl.multiple_of(w * WTOK, 16), WTOK)
            q = qkv[g, rows, 0:DA]
            k = qkv[g, rows, DA : 2 * DA]
            v = qkv[g, rows, 2 * DA : 3 * DA]
            s = mm_nt(stack_heads(q), k) * scale + bm[g]
            e = jnp.exp(s - jnp.max(s, -1, keepdims=True))
            p = e / jnp.sum(e, -1, keepdims=True)
            pr[g, w] = p
            pb = p.astype(BF)
            vs = stack_heads(v)
            o = jnp.zeros((WTOK, DA), F32)
            for h in range(HEADS):
                hs = slice(h * WTOK, (h + 1) * WTOK)
                o = o + mm(pb[hs], vs[hs])
            ao[g, rows, :] = o.astype(BF)
            return carry

        lax.fori_loop(0, NWIN, window, 0)

    forward(tp)
    wait(tabc)
    build_bias(other)
    wait(ring)
    forward(other)
    to_merge = pick(maps, PWM, TOK, TOK)
    x = mm(pick(maps, PXM, TOK, 768, 96), pc[...])
    for g in range(2):
        x = x + mm(mm(to_merge, ao[g]).astype(BF), pf[g])
    y[...] = x.astype(BF)
    yhc = [
        links.send(y.at[480:576], yh.at[0], device(0, 1, 0)),
        links.send(y.at[0:96], yh.at[1], device(0, -1, 0)),
    ]

    wait(dmc)
    mgain = mgain_ref[...]
    acc = jnp.zeros((1, 4 * D), F32)

    def slab(r, cp):
        lo = cp * 48
        if r == 0:
            return yh[0, lo : lo + 48, :]
        if r == 7:
            return yh[1, lo : lo + 48, :]
        lo += (r - 1) * 96
        return y[lo : lo + 48, :]

    for cr in (1, 2, 0, 3):
        if cr == 0:
            wait(yhc)
        slabs = [slab(2 * cr + rp, cp) for rp in (0, 1) for cp in (0, 1)]
        hat, inv = layer_stats(jnp.concatenate(slabs, 1).astype(F32))
        rows = slice(cr * 48, (cr + 1) * 48)
        dm = dmo[rows, :].astype(F32) + dmp[rows, :].astype(F32)
        if cr > 0:
            acc = acc + jnp.sum(dm * hat, 0, keepdims=True)
            mb[(cr - 1) * 48 : cr * 48, :] = (hat * mgain).astype(BF)
        dy = norm_back(dm, mgain, hat, inv).astype(BF)
        for q in range(4):
            r = 2 * cr + q // 2
            if 1 <= r <= 6:
                lo = (r - 1) * 96 + (q % 2) * 48
                dyt[lo : lo + 48, :] = dy[:, q * D : (q + 1) * D]
    mg[...] = acc

    for iz in range(NZ):
        part = mm_tn(mb[:, iz * 256 : (iz + 1) * 256], cmt[48:192, :])
        gm[iz] = part.reshape(2, NY, 32, 512)
        for iy in range(NY):
            sm1[iy, iz] = gm[iz, 1 - core, iy].astype(BF)
    m1 = [links.send(sm1, rm1, core_dev)]

    dyw[...] = mm(pick(maps, PMW, TOK, TOK), dyt[...]).astype(BF)
    for g in range(2):
        do[g] = mm_nt(dyw[...], pf[g]).astype(BF)
    dst[...] = jnp.zeros_like(dst)

    def backward(g, mine):
        def window(w, carry):
            rows = pl.ds(pl.multiple_of(w * WTOK, 16), WTOK)
            q = qkv[g, rows, 0:DA]
            k = qkv[g, rows, DA : 2 * DA]
            v = qkv[g, rows, 2 * DA : 3 * DA]
            p = pr[g, w]
            dos = stack_heads(do[g, rows, :])
            dp = mm_nt(dos, v)
            dv = mm_tn(p.astype(BF), dos)
            ds = p * (dp - jnp.sum(dp * p, -1, keepdims=True))
            if mine:
                dst[...] = dst[...] + ds
            dsb = ds.astype(BF)
            dk = mm_tn(dsb, stack_heads(q)) * scale
            ks = stack_heads(k)
            dq = jnp.zeros((WTOK, DA), F32)
            for h in range(HEADS):
                hs = slice(h * WTOK, (h + 1) * WTOK)
                dq = dq + mm(dsb[hs], ks[hs])
            dqkv[g, 0, rows, :] = (dq * scale).astype(BF)
            dqkv[g, 1, rows, :] = dk.astype(BF)
            dqkv[g, 2, rows, :] = dv.astype(BF)
            return carry

        lax.fori_loop(0, NWIN, window, 0)

    backward(tp, True)

    wait(m1)
    m2 = []
    for k in range(1, NY):
        iy = lax.rem(yy + k, NY)
        for iz in range(NZ):
            sm2[k - 1, iz] = (gm[iz, core, iy] + rm1[iy, iz].astype(F32)).astype(BF)
        m2.append(links.send(sm2.at[k - 1], rm2.at[k - 1], y_devs[k - 1]))

    for n in range(4):
        part = mm_tn(hn[...], dqkv[tp, n]) if n < 3 else mm_tn(dyw[...], ao[tp])
        gq[:, :, :, :, n * DA : (n + 1) * DA] = part.reshape(NZ, 2, NY, 8, DA)
    for iy in range(NY):
        for iz in range(0, NZ, 2):
            pair = jnp.concatenate([gq[iz, 1 - core, iy], gq[iz + 1, 1 - core, iy]], 0)
            sq1[iy, iz * 8 : iz * 8 + 16, :] = pair.astype(BF)
    q1 = [links.send(sq1, rq1, core_dev)]
    for iz in range(NZ):
        am[iz] = gm[iz, core, yy] + rm1[yy, iz].astype(F32)

    wide[0] = dst[:, 0:128]
    wide[1, :, 0 : WTOK - 128] = dst[:, 128:WTOK]
    acc = jnp.zeros((48, 512), F32)
    for c in range(WLON):
        rows = pl.ds(c, 48, stride=WLON)
        x = jnp.concatenate([wide[0, rows, :], wide[1, rows, :][:, 0 : WTOK - 128]], 1)
        hi = x.astype(BF)
        low = (x - hi.astype(F32)).astype(BF)
        v = mm(jnp.concatenate([hi, low], 0), et[c * WTOK : (c + 1) * WTOK, :])
        acc = acc + v[0:48] + v[48:96]
    t[:, 0:512] = acc
    t[:, 512:768] = jnp.zeros((48, 256), F32)
    for h in range(HEADS):
        out = jnp.zeros((1, 768), F32)
        for g in range(12):
            row = t[h * 12 + g : h * 12 + g + 1, :]
            shift = (g // ROWS * 11 + g % ROWS) * 23
            out = out + (pltpu.roll(row, shift, 1) if shift else row)
        sv[h : h + 1, :] = out
    sv[4:5, :] = mg[:, 0:768]
    sv[5:6, :] = mg[:, 768:1536]
    sv[6:7, 0:512] = mg[:, 1536:2048]
    sv[6:7, 512:768] = jnp.zeros((1, 256), F32)
    sv[7:8, :] = jnp.zeros((1, 768), F32)
    sv1[core] = sv[...]
    v1 = [links.send(sv1.at[core], sv1.at[core], core_dev)]

    backward(other, False)

    wait(q1)
    q2 = []
    for k in range(1, NY):
        iy = lax.rem(yy + k, NY)
        for iz in range(0, NZ, 2):
            pair = jnp.concatenate([gq[iz, core, iy], gq[iz + 1, core, iy]], 0)
            rows = slice(iz * 8, iz * 8 + 16)
            sq2[k - 1, rows, :] = (pair + rq1[iy, rows, :].astype(F32)).astype(BF)
        q2.append(links.send(sq2.at[k - 1], rq2.at[k - 1], y_devs[k - 1]))
    wait(v1)
    sv2[yy] = sv1[0] + sv1[1]
    v2 = [links.send(sv2.at[yy], sv2.at[yy], dev) for dev in y_devs]

    dh = jnp.zeros((TOK, D), F32)
    for g in range(2):
        for n in range(3):
            dh = dh + mm_nt(dqkv[g, n], wf[g, n])
    normed, inv = layer_stats(xw[...].astype(F32))
    av[...] = jnp.sum(dh * normed, 0, keepdims=True)
    av1[core] = av[...]
    a1 = [links.send(av1.at[core], av1.at[core], core_dev)]
    branch = norm_back(dh, gain_ref[...], normed, inv).astype(BF)
    lg = (dyw[...].astype(F32) + branch.astype(F32)).astype(BF)
    lp[...] = mm(pick(maps, PPO, 608, TOK), lg).astype(BF)
    ro = [
        links.send(lp.at[304:560], rp_ref.at[304:560], device(0, -1, 0)),
        links.send(lp.at[256:304], rp_ref.at[256:304], device(-1, 0, 0)),
        links.send(lp.at[560:608], rp_ref.at[560:608], device(-1, -1, 0)),
    ]
    wait(a1)
    av2[yy] = av1[0] + av1[1]
    a2 = [links.send(av2.at[yy], av2.at[yy], dev) for dev in y_devs]
    rp_ref[0:256, :] = lp[0:256, :]

    wait(m2)
    for iz in range(NZ):
        acc = am[iz]
        for k in range(NY - 1):
            acc = acc + rm2[k, iz].astype(F32)
        bmm[iz] = acc
    m3 = []
    for k in range(1, NZ):
        sm3[k - 1] = bmm[lax.rem(z + k, NZ)].astype(BF)
        m3.append(links.send(sm3.at[k - 1], rm3.at[k - 1], z_devs[k - 1]))

    for iz in range(0, NZ, 2):
        pair = jnp.concatenate([gq[iz, core, yy], gq[iz + 1, core, yy]], 0)
        rows = slice(iz * 8, iz * 8 + 16)
        aq[rows, :] = pair + rq1[yy, rows, :].astype(F32)
    wait(q2)
    acc = aq[...]
    for k in range(NY - 1):
        acc = acc + rq2[k].astype(F32)
    for iz in range(NZ):
        bq[iz] = acc[iz * 8 : iz * 8 + 8]
    q3 = [
        links.send(bq.at[lax.rem(z + k, NZ)], rq3.at[k - 1], z_devs[k - 1])
        for k in range(1, NZ)
    ]
    wait(v2)
    sv3[z] = sv2[0] + sv2[1] + sv2[2] + sv2[3]
    v3 = [links.send(sv3.at[z], sv3.at[z], dev) for dev in z_devs]
    wait(a2)
    av3[z] = av2[0] + av2[1] + av2[2] + av2[3]
    a3 = [links.send(av3.at[z], av3.at[z], dev) for dev in z_devs]

    wait(m3)
    acc = bmm[z]
    for k in range(NZ - 1):
        acc = acc + rm3[k].astype(F32)
    cm[0] = acc[0:16]
    cm[1] = acc[16:32]
    m4 = [links.send(cm.at[1 - xx], rm4, x_dev)]
    wait(q3)
    acc = bq[z]
    for k in range(NZ - 1):
        acc = acc + rq3[k]
    cq[...] = acc
    q4 = [links.send(cq, rq4, x_dev)]
    wait(v3)
    acc = sv3[0]
    for k in range(1, NZ):
        acc = acc + sv3[k]
    sv4[xx] = acc
    v4 = [links.send(sv4.at[xx], sv4.at[xx], x_dev)]
    wait(a3)
    acc = av3[0]
    for k in range(1, NZ):
        acc = acc + av3[k]
    av4[xx] = acc
    v4.append(links.send(av4.at[xx], av4.at[xx], x_dev))
    wait(m4)
    om_ref[...] = cm[xx] + rm4[...]
    wait(q4)
    oq_ref[...] = cq[...] + rq4[...]
    wait(v4)
    ov_ref[...] = sv4[0] + sv4[1]
    oa_ref[...] = av4[0] + av4[1]
    wait(ro)


def kend(
    maps, rp_ref, om_ref, oq_ref, ov_ref, oa_ref, lg_ref, ag_ref, gw_ref, gp_ref, gb_ref, mg_ref,
    gm_ref,
):
    xx = lax.rem(lax.axis_index("lat"), 2)
    lg_ref[...] = mm(pick(maps, PF, TOK, 608), rp_ref[...]).astype(BF)
    gm_ref[...] = om_ref[...]
    mine = jnp.where(xx == 0, oq_ref[0:4, :], oq_ref[4:8, :])
    for n in range(3):
        gw_ref[n] = mine[:, n * DA : (n + 1) * DA]
    gp_ref[...] = mine[:, 3 * DA :]
    gb_ref[...] = ov_ref[0:HEADS, 0:NREL]
    mg_ref[:, 0:768] = ov_ref[4:5, :]
    mg_ref[:, 768:1536] = ov_ref[5:6, :]
    mg_ref[:, 1536:2048] = ov_ref[6:7, 0:512]
    ag_ref[...] = oa_ref[...]


def local(
    latent, pole_mask, attn_gain, qkv_weight, proj_weight, rel_bias, merge_gain, merge_weight,
    coarse_grad,
):
    maps = jnp.asarray(index_maps())
    dma = pltpu.SemaphoreType.DMA
    vm = pltpu.VMEM
    nb = HEADS * WTOK
    nv, na = (8, 768), (1, D)
    sends = 80
    rp, om, oq, ov, oa = call(
        kmain, "sublayer_backward",
        [
            pole_mask, maps, rel_bias, attn_gain.reshape(1, D), merge_gain.reshape(1, 4 * D),
            latent.reshape(TOK, D), coarse_grad.reshape(144, 512), qkv_weight.transpose(1, 0, 2),
            proj_weight, merge_weight,
        ],
        [((608, D), BF), ((16, 512), F32), ((8, 1024), F32), (nv, F32), (na, F32)],
        [
            vm((TOK, D), BF), vm((144, 512), BF), vm((4 * D, 512), BF), vm((2, 3, D, DA), BF),
            vm((2, DA, D), BF), vm((2, 8, 768), F32), vm((WLON * WTOK, 512), BF),
            vm((2, nb, WTOK), F32), vm((48, 512), F32), vm((2, nb, 128), F32),
            vm((768, D), BF), vm((224, 512), BF), vm((768, D), BF), vm((224, 512), BF),
            vm((192, 512), BF), vm((192, 4 * D), BF), vm((192, 4 * D), BF),
            vm((TOK, D), BF), vm((TOK, D), BF), vm((2, TOK, 3 * DA), BF),
            vm((2, NWIN, nb, WTOK), F32), vm((2, TOK, DA), BF), vm((TOK, D), BF),
            vm((2, 96, D), BF), vm((144, 4 * D), BF), vm((TOK, D), BF), vm((1, 4 * D), F32),
            vm((NZ, 2, NY, 32, 512), F32), vm((TOK, D), BF), vm((2, TOK, DA), BF),
            vm((2, 3, TOK, DA), BF), vm((nb, WTOK), F32), vm((48, 768), F32),
            vm((NZ, 2, NY, 8, 1024), F32), vm((608, D), BF), vm(nv, F32), vm(na, F32),
            vm((NY, NZ, 32, 512), BF), vm((NY, 64, 1024), BF),
            vm((NY, NZ, 32, 512), BF), vm((NY, 64, 1024), BF), vm((2,) + nv, F32),
            vm((2,) + na, F32),
            vm((NZ, 32, 512), F32), vm((64, 1024), F32),
            vm((NY - 1, NZ, 32, 512), BF), vm((NY - 1, 64, 1024), BF),
            vm((NY - 1, NZ, 32, 512), BF), vm((NY - 1, 64, 1024), BF), vm((NY,) + nv, F32),
            vm((NY,) + na, F32),
            vm((NZ, 32, 512), F32), vm((NZ, 8, 1024), F32),
            vm((NZ - 1, 32, 512), BF), vm((NZ - 1, 32, 512), BF),
            vm((NZ - 1, 8, 1024), F32), vm((NZ,) + nv, F32), vm((NZ,) + na, F32),
            vm((2, 16, 512), F32), vm((8, 1024), F32),
            vm((16, 512), F32), vm((8, 1024), F32), vm((2,) + nv, F32), vm((2,) + na, F32),
            dma((5,)), dma((sends,)), dma((sends,)),
        ],
        cid=1, mib=58, smem=1, hbm=5,
    )
    lg, ag, gw, gp, gb, mgg, gmm = call(
        kend, "finish", [maps, rp, om, oq, ov, oa],
        [
            ((TOK, D), BF), ((1, D), F32), ((3, 4, DA), F32), ((4, DA), F32),
            ((HEADS, NREL), F32), ((1, 4 * D), F32), ((16, 512), F32),
        ],
        mib=8,
    )
    return (
        lg.reshape(latent.shape),
        ag.reshape(D),
        gw.transpose(1, 0, 2),
        gp.T,
        gb,
        mgg.reshape(4 * D),
        gmm,
    )


def solution(mesh):
    placed = (
        P(None, "lat", "lon", None),
        P(),
        P(),
        P(None, None, "tp"),
        P("tp", None),
        P("tp", None),
        P(),
        P(None, "tp"),
        P(None, "lat", "lon", "tp"),
    )
    return jax.shard_map(
        local,
        mesh=mesh,
        in_specs=placed,
        out_specs=(
            P(None, "lat", "lon", None),
            P(),
            P(("lon", "lat"), None, "tp"),
            P("tp", ("lon", "lat")),
            P("tp", None),
            P(),
            P(("lon", "lat"), "tp"),
        ),
        check_vma=False,
    )
```

```python
import functools

import jax
import jax.numpy as jnp
import numpy as np
from jax import lax
from jax.experimental import pallas as pl
from jax.experimental.pallas import tpu as pltpu
from jax.sharding import PartitionSpec as P

EPS = 1e-05
NEG = -1e30
MESH = pl.DeviceIdType.MESH
BF = jnp.bfloat16
F32 = jnp.float32

LEV, ROWS, COLS, D = 2, 6, 48, 512
WLON = 12
NWIN = COLS // WLON
WTOK = LEV * ROWS * WLON
TOK = LEV * ROWS * COLS
HEADS = 4
HD = 64
DA = HEADS * HD
NREL = 759
NZ, NY = 8, 4


(QL, QL2, QC, QC2, PC, PXM, PXW, PWM, PMW, PPO, PF, FP, E0) = range(13)
MAPW = 768
OUT_PADS = (256, 48, 256, 48)
COARSE_PADS = (96, 16, 96, 16)


def pieces(row_sets, near, far, pads):
    base, out = 0, []
    parts = ((row_sets[0], near), (row_sets[0], far), (row_sets[1], near), (row_sets[1], far))
    for n, ((rows, cols), pad) in enumerate(zip(parts, pads)):
        p = base
        for l in range(LEV):
            for r in rows:
                for c in cols:
                    out.append((p, n, l, r, c))
                    p += 1
        base += pad
    return out


@functools.lru_cache(None)
def index_maps():
    t = np.full((32, MAPW), -1, np.int32)
    near, far = range(0, 42), range(42, 48)

    def merge_at(l, rr, sc):
        return ((rr * 2 + sc % 2) * LEV + l) * 24 + sc // 2

    def window_at(l, rr, sc):
        return (sc // WLON) * WTOK + (l * ROWS + rr - 1) * WLON + sc % WLON

    def seen(n, r, c):
        return (r + 4 if n < 2 else r - 2), (c + 6 if n % 2 == 0 else c - 42)

    for l in range(LEV):
        for rr in range(1, 7):
            for sc in range(COLS):
                t[PWM, window_at(l, rr, sc)] = merge_at(l, rr, sc) - 96
                t[PMW, merge_at(l, rr, sc) - 96] = window_at(l, rr, sc)
    for p, n, l, r, c in pieces((range(0, 3), range(3, 6)), near, far, OUT_PADS):
        rr, sc = seen(n, r, c)
        t[QL if n < 2 else QL2, (l * ROWS + r) * COLS + c] = p
        t[PXM, p] = merge_at(l, rr, sc) - 96
        t[PXW, p] = window_at(l, rr, sc)
        t[PPO, window_at(l, rr, sc)] = p
        t[PF, p] = (l * ROWS + r) * COLS + c
    for p, n, l, r, c in pieces((range(0, 2), range(1, 3)), range(0, 21), range(21, 24), COARSE_PADS):
        t[QC if n < 2 else QC2, (l * 3 + r) * 24 + c] = p
        cr = r + 2 if n < 2 else r - 1
        cc = c + 3 if n % 2 == 0 else c - 21
        t[PC, p] = (cr * LEV + l) * 24 + cc
    order = np.arange(D).reshape(NZ, 2, NY, 2, 4).transpose(1, 3, 2, 0, 4)
    t[FP, 0:D] = order.reshape(-1)
    for c in range(WLON):
        for j in range(WTOK):
            l2, r2, c2 = j // 72, j // 12 % 6, j % 12
            t[E0 + c, ((1 - l2) * 11 + 5 - r2) * 23 + c - c2 + 11] = j
    return t


def pick(maps, n, rows, cols, base=0):
    at = lax.broadcasted_iota(jnp.int32, (rows, cols), 0) + base
    return jnp.where(at == maps[n : n + 1, 0:cols], 1.0, 0.0).astype(BF)


def mm(a, b):
    return lax.dot_general(a, b, (((1,), (0,)), ((), ())), preferred_element_type=F32)


def mm_nt(a, b):
    return lax.dot_general(a, b, (((1,), (1,)), ((), ())), preferred_element_type=F32)


def mm_tn(a, b):
    return lax.dot_general(a, b, (((0,), (0,)), ((), ())), preferred_element_type=F32)


def layer_stats(x):
    center = x - jnp.mean(x, -1, keepdims=True)
    inverse = lax.rsqrt(jnp.mean(center * center, -1, keepdims=True) + EPS)
    return center * inverse, inverse


def norm_back(up, gain, normed, inverse):
    s = up * gain
    return inverse * (
        s - jnp.mean(s, -1, keepdims=True) - normed * jnp.mean(s * normed, -1, keepdims=True)
    )


def head_mask(h, rows):
    lane = lax.broadcasted_iota(jnp.int32, (rows, DA), 1)
    return (lane >= h * HD) & (lane < (h + 1) * HD)


def stack_heads(x):
    zero = jnp.zeros_like(x)
    return jnp.concatenate(
        [jnp.where(head_mask(h, x.shape[0]), x, zero) for h in range(HEADS)], 0
    )


def vspec():
    return pl.BlockSpec(memory_space=pltpu.VMEM)


def call(kernel, name, ins, outs, scratch=(), cid=None, smem=0, hbm=0, mib=16):
    params = dict(vmem_limit_bytes=mib << 20)
    if cid is not None:
        params.update(collective_id=cid, has_side_effects=True)
    specs = [pl.BlockSpec(memory_space=pltpu.SMEM)] * smem
    specs += [vspec()] * (len(ins) - smem - hbm) + [pl.BlockSpec(memory_space=pl.ANY)] * hbm
    return pl.pallas_call(
        kernel,
        out_shape=[jax.ShapeDtypeStruct(s, d) for s, d in outs],
        in_specs=specs,
        out_specs=[vspec()] * len(outs),
        scratch_shapes=list(scratch),
        compiler_params=pltpu.CompilerParams(**params),
        name=name,
    )(*ins)


def device(dlon, dlat, dtp):
    nlon, nlat = lax.axis_size("lon"), lax.axis_size("lat")
    return (
        lax.rem(lax.axis_index("lon") + dlon + nlon, nlon),
        lax.rem(lax.axis_index("lat") + dlat + nlat, nlat),
        lax.rem(lax.axis_index("tp") + dtp, 2),
    )


def remote(src, dst, ss, rs, n, dev):
    return pltpu.make_async_remote_copy(
        src, dst, ss.at[n], rs.at[n], device_id=dev, device_id_type=MESH
    )


class Links:
    def __init__(self, ss, rs):
        self.ss, self.rs, self.n = ss, rs, 0

    def send(self, src, dst, dev):
        c = remote(src, dst, self.ss, self.rs, self.n, dev)
        self.n += 1
        c.start()
        return c


def wait(copies):
    for c in copies:
        c.wait()


def kmain(
    pole_ref, maps, tab_ref, gain_ref, mgain_ref, lat_hbm, cg_hbm, w_hbm, proj_hbm, mw_hbm,
    rp_ref, om_ref, oq_ref, ov_ref, oa_ref,
    lat, cg, mw, wf, pf, tabs, et, bm, u, wide,
    sp, sc, pc, cc, cmt, dmo, dmp,
    xw, hn, hnp, qkv, pr, ao, y, yh, mb, dyt, mg,
    gm, dyw, dyp, do, dqkv, dst, t, gq, lp, sv, av,
    sm1, sq1, rm1, rq1, sv1, av1,
    am, sm2, rm2, bmm, sm3, rm3, cm, rm4,
    aq, sq2, rq2, bq, sq3, rq3, cq, rq4,
    sv2, av2, sv3, av3, sv4, av4, ls, ss, rs,
):
    lon, band, tp = lax.axis_index("lon"), lax.axis_index("lat"), lax.axis_index("tp")
    z, core = lax.div(lon, 2), lax.rem(lon, 2)
    yy, xx = lax.div(band, 2), lax.rem(band, 2)
    peer = device(0, 0, 1)
    core_dev = (z * 2 + 1 - core, band, tp)
    x_dev = (lon, yy * 2 + 1 - xx, tp)
    y_devs = [(lon, lax.rem(yy + k, NY) * 2 + xx, tp) for k in range(1, NY)]
    z_devs = [(lax.rem(z + k, NZ) * 2 + core, band, tp) for k in range(1, NZ)]
    near = [device(s * o, s * a, 0) for s in (1, -1) for o, a in ((1, 0), (0, 1), (1, 1))]
    partners = [peer, core_dev, x_dev] + y_devs + z_devs + near
    barrier = pltpu.get_barrier_semaphore()
    for dev in partners:
        pl.semaphore_signal(barrier, inc=1, device_id=dev, device_id_type=MESH)
    links = Links(ss, rs)
    scale = HD**-0.5
    other = 1 - tp

    loads = []
    for n, (src, into) in enumerate(
        ((lat_hbm, lat), (cg_hbm, cg), (w_hbm, wf.at[tp]), (proj_hbm, pf.at[tp]), (mw_hbm, mw))
    ):
        loads.append(pltpu.make_async_copy(src, into, ls.at[n]))
        loads[-1].start()

    nrows = pole_ref.shape[0]
    i = lax.broadcasted_iota(jnp.int32, (WTOK, WTOK), 0)
    j = lax.broadcasted_iota(jnp.int32, (WTOK, WTOK), 1)
    ri, rj = lax.rem(lax.div(i, WLON), ROWS), lax.rem(lax.div(j, WLON), ROWS)
    valid = jnp.zeros((WTOK, WTOK), jnp.int32)
    for r in range(ROWS):
        flag = pole_ref[lax.rem(band * ROWS + (r - 3 + nrows), nrows)]
        valid = jnp.where(rj == r, flag, valid)
    cut = jnp.where(band == 0, 3, 0)
    same = jnp.where(ri < cut, 1, 0) == jnp.where(rj < cut, 1, 0)
    allowed = (valid > 0) & same

    def build_bias(g):
        for l in range(LEV):
            for r in range(ROWS):
                shift = (l * 11 + r) * 23
                row = tabs[g]
                if shift:
                    row = pltpu.roll(row, 768 - shift, 1)
                for h in range(HEADS):
                    n = h * 12 + l * ROWS + r
                    u[n : n + 1, :] = row[h : h + 1, :512]
        t0 = u[...]
        hi = t0.astype(BF)
        rest = t0 - hi.astype(F32)
        mid = rest.astype(BF)
        low = (rest - mid.astype(F32)).astype(BF)
        split = jnp.concatenate([hi, mid, low], 0)
        for c in range(WLON):
            v = mm_nt(split, et[c * WTOK : (c + 1) * WTOK, :])
            v = v[0:48] + v[48:96] + v[96:144]
            wide[0, pl.ds(c, 48, stride=WLON), :] = v[:, 0:128]
            wide[1, pl.ds(c, 48, stride=WLON), :] = jnp.concatenate(
                [v[:, 128:WTOK], jnp.zeros((48, 256 - WTOK), F32)], 1
            )
        for h in range(HEADS):
            rows = slice(h * WTOK, (h + 1) * WTOK)
            both = jnp.concatenate([wide[0, rows, :], wide[1, rows, 0 : WTOK - 128]], 1)
            bm[g, rows, :] = jnp.where(allowed, both, NEG)

    tabs[tp] = jnp.zeros((8, 768), F32)
    tabs[tp, 0:HEADS, 0:NREL] = tab_ref[...]
    loads[0].wait()
    loads[1].wait()
    for m, lo, hi in ((QL2, 304, 608), (QL, 256, 304)):
        sp[lo:hi, :] = mm(pick(maps, m, hi - lo, TOK, lo), lat[...]).astype(BF)
    for m, lo, hi in ((QC2, 112, 224), (QC, 96, 112)):
        sc[lo:hi, :] = mm(pick(maps, m, hi - lo, 144, lo), cg[...]).astype(BF)
    loads[2].wait()
    loads[3].wait()
    at = pl.ds(pl.multiple_of(core * 256 + yy * 64, 64), 64)
    pat = pl.ds(pl.multiple_of(core * 128 + yy * 32, 32), 32)
    half = pl.ds(pl.multiple_of(core * 256, 256), 256)
    phalf = pl.ds(pl.multiple_of(core * 128, 128), 128)
    pl.semaphore_wait(barrier, len(partners))
    chalo = [links.send(sc.at[112:208], cc.at[112:208], device(0, 1, 0))]
    halo = [links.send(sp.at[304:560], pc.at[304:560], device(0, 1, 0))]
    chalo.append(links.send(sc.at[208:224], cc.at[208:224], device(1, 1, 0)))
    chalo.append(links.send(sc.at[96:112], cc.at[96:112], device(1, 0, 0)))
    first = [
        links.send(wf.at[tp, :, at], wf.at[tp, :, at], peer),
        links.send(pf.at[tp, pat], pf.at[tp, pat], peer),
    ]
    halo.append(links.send(sp.at[560:608], pc.at[560:608], device(1, 1, 0)))
    halo.append(links.send(sp.at[256:304], pc.at[256:304], device(1, 0, 0)))
    tabc = [links.send(tabs.at[tp], tabs.at[tp], peer)]
    pc[0:256, :] = mm(pick(maps, QL, 256, TOK), lat[...]).astype(BF)
    cc[0:96, :] = mm(pick(maps, QC, 96, 144), cg[...]).astype(BF)
    for c in range(WLON):
        et[c * WTOK : (c + 1) * WTOK, :] = pick(maps, E0 + c, WTOK, 512)
    loads[4].wait()
    wait(chalo)
    cmt[...] = mm(pick(maps, PC, 192, 224), cc[...]).astype(BF)
    for n in range(4):
        cols = slice(n * 512, (n + 1) * 512)
        dmo[:, cols] = mm_nt(cmt[...], mw[cols, :]).astype(BF)
    dmc = [links.send(dmo.at[48:144], dmp.at[48:144], peer)]
    dmh = [
        links.send(dmo.at[0:48], dmp.at[0:48], peer),
        links.send(dmo.at[144:192], dmp.at[144:192], peer),
    ]
    wait(first)
    ring = []
    for dev in y_devs:
        for ref in (wf.at[other, :, at], pf.at[other, pat]):
            ring.append(links.send(ref, ref, dev))
    build_bias(tp)
    wait(halo)

    x = mm(pick(maps, PXW, TOK, 608), pc[...])
    xw[...] = x.astype(BF)
    normed, _ = layer_stats(x)
    hn[...] = (normed * gain_ref[...]).astype(BF)

    def forward(g):
        for n in range(3):
            qkv[g, :, n * DA : (n + 1) * DA] = mm(hn[...], wf[g, n]).astype(BF)

        def window(w, carry):
            rows = pl.ds(pl.multiple_of(w * WTOK, 16), WTOK)
            q = qkv[g, rows, 0:DA]
            k = qkv[g, rows, DA : 2 * DA]
            v = qkv[g, rows, 2 * DA : 3 * DA]
            s = mm_nt(stack_heads(q), k) * scale + bm[g]
            e = jnp.exp(s - jnp.max(s, -1, keepdims=True))
            p = e / jnp.sum(e, -1, keepdims=True)
            pr[g, w] = p
            pb = p.astype(BF)
            vs = stack_heads(v)
            o = jnp.zeros((WTOK, DA), F32)
            for h in range(HEADS):
                hs = slice(h * WTOK, (h + 1) * WTOK)
                o = o + mm(pb[hs], vs[hs])
            ao[g, rows, :] = o.astype(BF)
            return carry

        lax.fori_loop(0, NWIN, window, 0)

    forward(tp)
    features = pick(maps, FP, D, D)
    hnp[...] = mm(hn[...], features).astype(BF)
    wait(ring)
    pair = [links.send(r, r, core_dev) for r in (wf.at[other, :, half], pf.at[other, phalf])]
    wait(tabc)
    build_bias(other)
    wait(pair)
    forward(other)
    to_merge = pick(maps, PWM, TOK, TOK)
    x = mm(pick(maps, PXM, TOK, 608), pc[...])
    for g in range(2):
        x = x + mm(mm(to_merge, ao[g]).astype(BF), pf[g])
    y[...] = x.astype(BF)
    yhc = [
        links.send(y.at[480:576], yh.at[0], device(0, 1, 0)),
        links.send(y.at[0:96], yh.at[1], device(0, -1, 0)),
    ]

    wait(dmc)
    mgain = mgain_ref[...]
    acc = jnp.zeros((1, 4 * D), F32)

    def slab(r, cp):
        lo = cp * 48
        if r == 0:
            return yh[0, lo : lo + 48, :]
        if r == 7:
            return yh[1, lo : lo + 48, :]
        lo += (r - 1) * 96
        return y[lo : lo + 48, :]

    for cr in (1, 2, 0, 3):
        if cr == 0:
            wait(yhc)
            wait(dmh)
        slabs = [slab(2 * cr + rp, cp) for rp in (0, 1) for cp in (0, 1)]
        hat, inv = layer_stats(jnp.concatenate(slabs, 1).astype(F32))
        rows = slice(cr * 48, (cr + 1) * 48)
        dm = dmo[rows, :].astype(F32) + dmp[rows, :].astype(F32)
        if cr > 0:
            acc = acc + jnp.sum(dm * hat, 0, keepdims=True)
            mb[(cr - 1) * 48 : cr * 48, :] = (hat * mgain).astype(BF)
        dy = norm_back(dm, mgain, hat, inv).astype(BF)
        for q in range(4):
            r = 2 * cr + q // 2
            if 1 <= r <= 6:
                lo = (r - 1) * 96 + (q % 2) * 48
                dyt[lo : lo + 48, :] = dy[:, q * D : (q + 1) * D]
    mg[...] = acc

    for iz in range(NZ):
        part = mm_tn(mb[:, iz * 256 : (iz + 1) * 256], cmt[48:192, :])
        gm[iz] = part.reshape(2, NY, 32, 512)
        for iy in range(NY):
            sm1[iy, iz] = gm[iz, 1 - core, iy].astype(BF)
    m1 = [links.send(sm1, rm1, core_dev)]

    dyw[...] = mm(pick(maps, PMW, TOK, TOK), dyt[...]).astype(BF)
    for g in range(2):
        do[g] = mm_nt(dyw[...], pf[g]).astype(BF)
    dst[...] = jnp.zeros_like(dst)

    def backward(g, mine, lo=0, hi=NWIN):
        def window(w, carry):
            rows = pl.ds(pl.multiple_of(w * WTOK, 16), WTOK)
            q = qkv[g, rows, 0:DA]
            k = qkv[g, rows, DA : 2 * DA]
            v = qkv[g, rows, 2 * DA : 3 * DA]
            p = pr[g, w]
            dos = stack_heads(do[g, rows, :])
            dp = mm_nt(dos, v)
            dv = mm_tn(p.astype(BF), dos)
            ds = p * (dp - jnp.sum(dp * p, -1, keepdims=True))
            if mine:
                dst[...] = dst[...] + ds
            dsb = ds.astype(BF)
            dk = mm_tn(dsb, stack_heads(q)) * scale
            ks = stack_heads(k)
            dq = jnp.zeros((WTOK, DA), F32)
            for h in range(HEADS):
                hs = slice(h * WTOK, (h + 1) * WTOK)
                dq = dq + mm(dsb[hs], ks[hs])
            dqkv[g, 0, rows, :] = (dq * scale).astype(BF)
            dqkv[g, 1, rows, :] = dk.astype(BF)
            dqkv[g, 2, rows, :] = dv.astype(BF)
            return carry

        lax.fori_loop(lo, hi, window, 0)

    backward(tp, True, 0, 1)

    wait(m1)
    m2 = []
    for k in range(1, NY):
        iy = lax.rem(yy + k, NY)
        for iz in range(NZ):
            sm2[k - 1, iz] = (gm[iz, core, iy] + rm1[iy, iz].astype(F32)).astype(BF)
        m2.append(links.send(sm2.at[k - 1], rm2.at[k - 1], y_devs[k - 1]))

    backward(tp, True, 1)

    dyp[...] = mm(dyw[...], features).astype(BF)
    for n in range(4):
        part = mm_tn(hnp[...], dqkv[tp, n]) if n < 3 else mm_tn(dyp[...], ao[tp])
        gq[:, :, :, :, n * DA : (n + 1) * DA] = part.reshape(2, 2, NY, 32, DA)
    sq1[...] = gq[1 - core].astype(BF)
    q1 = [links.send(sq1, rq1, core_dev)]
    for iz in range(NZ):
        am[iz] = gm[iz, core, yy] + rm1[yy, iz].astype(F32)

    wide[0] = dst[:, 0:128]
    wide[1, :, 0 : WTOK - 128] = dst[:, 128:WTOK]
    acc = jnp.zeros((48, 512), F32)
    for c in range(WLON):
        rows = pl.ds(c, 48, stride=WLON)
        x = jnp.concatenate([wide[0, rows, :], wide[1, rows, :][:, 0 : WTOK - 128]], 1)
        hi = x.astype(BF)
        low = (x - hi.astype(F32)).astype(BF)
        v = mm(jnp.concatenate([hi, low], 0), et[c * WTOK : (c + 1) * WTOK, :])
        acc = acc + v[0:48] + v[48:96]
    t[:, 0:512] = acc
    t[:, 512:768] = jnp.zeros((48, 256), F32)
    for h in range(HEADS):
        out = jnp.zeros((1, 768), F32)
        for g in range(12):
            row = t[h * 12 + g : h * 12 + g + 1, :]
            shift = (g // ROWS * 11 + g % ROWS) * 23
            out = out + (pltpu.roll(row, shift, 1) if shift else row)
        sv[h : h + 1, :] = out
    sv[4:5, :] = mg[:, 0:768]
    sv[5:6, :] = mg[:, 768:1536]
    sv[6:7, 0:512] = mg[:, 1536:2048]
    sv[6:7, 512:768] = jnp.zeros((1, 256), F32)
    sv[7:8, :] = jnp.zeros((1, 768), F32)
    sv1[core] = sv[...]
    v1 = [links.send(sv1.at[core], sv1.at[core], core_dev)]

    wait(q1)
    sq2[...] = (gq[core, 1 - xx] + rq1[1 - xx].astype(F32)).astype(BF)
    q2 = [links.send(sq2, rq2, x_dev)]
    aq[...] = gq[core, xx] + rq1[xx].astype(F32)
    wait(v1)
    sv2[z] = sv1[0] + sv1[1]
    v2 = [links.send(sv2.at[z], sv2.at[z], dev) for dev in z_devs]

    backward(other, False)

    wait(q2)
    q3 = []
    for k in range(1, NY):
        iy = lax.rem(yy + k, NY)
        sq3[k - 1] = (aq[iy] + rq2[iy].astype(F32)).astype(BF)
        q3.append(links.send(sq3.at[k - 1], rq3.at[k - 1], y_devs[k - 1]))
    bq[...] = aq[yy] + rq2[yy].astype(F32)

    wait(m2)
    for iz in range(NZ):
        acc = am[iz]
        for k in range(NY - 1):
            acc = acc + rm2[k, iz].astype(F32)
        bmm[iz] = acc
    m3 = []
    for k in range(1, NZ):
        sm3[k - 1] = bmm[lax.rem(z + k, NZ)].astype(BF)
        m3.append(links.send(sm3.at[k - 1], rm3.at[k - 1], z_devs[k - 1]))

    dh = jnp.zeros((TOK, D), F32)
    for g in range(2):
        for n in range(3):
            dh = dh + mm_nt(dqkv[g, n], wf[g, n])
    normed, inv = layer_stats(xw[...].astype(F32))
    av[...] = jnp.sum(dh * normed, 0, keepdims=True)
    av1[core] = av[...]
    a1 = [links.send(av1.at[core], av1.at[core], core_dev)]
    branch = norm_back(dh, gain_ref[...], normed, inv).astype(BF)
    lg = (dyw[...].astype(F32) + branch.astype(F32)).astype(BF)
    lp[...] = mm(pick(maps, PPO, 608, TOK), lg).astype(BF)
    ro = [
        links.send(lp.at[304:560], rp_ref.at[304:560], device(0, -1, 0)),
        links.send(lp.at[256:304], rp_ref.at[256:304], device(-1, 0, 0)),
        links.send(lp.at[560:608], rp_ref.at[560:608], device(-1, -1, 0)),
    ]
    rp_ref[0:256, :] = lp[0:256, :]
    wait(v2)
    acc = sv2[0]
    for k in range(1, NZ):
        acc = acc + sv2[k]
    sv3[xx] = acc
    v3 = [links.send(sv3.at[xx], sv3.at[xx], x_dev)]
    wait(a1)
    av2[xx] = av1[0] + av1[1]
    a2 = [links.send(av2.at[xx], av2.at[xx], x_dev)]

    wait(q3)
    acc = bq[...]
    for k in range(NY - 1):
        acc = acc + rq3[k].astype(F32)
    for iz in range(NZ):
        rows = slice(iz * 4, iz * 4 + 4)
        cq[iz] = jnp.concatenate([acc[rows, 0:512], acc[rows, 512:1024]], 0)
    q4 = []
    for k in range(1, NZ):
        q4.append(links.send(cq.at[lax.rem(z + k, NZ)], rq4.at[k - 1], z_devs[k - 1]))

    wait(a2)
    av3[yy] = av2[0] + av2[1]
    a3 = [links.send(av3.at[yy], av3.at[yy], dev) for dev in y_devs]
    wait(v3)
    sv4[yy] = sv3[0] + sv3[1]
    v4 = [links.send(sv4.at[yy], sv4.at[yy], dev) for dev in y_devs]

    wait(m3)
    acc = bmm[z]
    for k in range(NZ - 1):
        acc = acc + rm3[k].astype(F32)
    cm[0] = acc[0:16]
    cm[1] = acc[16:32]
    m4 = [links.send(cm.at[1 - xx], rm4, x_dev)]
    wait(a3)
    av4[z] = av3[0] + av3[1] + av3[2] + av3[3]
    a4 = [links.send(av4.at[z], av4.at[z], dev) for dev in z_devs]
    wait(m4)
    om_ref[...] = cm[xx] + rm4[...]
    wait(q4)
    acc = cq[z]
    for k in range(NZ - 1):
        acc = acc + rq4[k]
    oq_ref[...] = acc
    wait(v4)
    ov_ref[...] = sv4[0] + sv4[1] + sv4[2] + sv4[3]
    wait(a4)
    acc = av4[0]
    for k in range(1, NZ):
        acc = acc + av4[k]
    oa_ref[...] = acc
    wait(ro)


def kend(
    maps, rp_ref, om_ref, oq_ref, ov_ref, oa_ref, lg_ref, ag_ref, gw_ref, gp_ref, gb_ref, mg_ref,
    gm_ref,
):
    lg_ref[...] = mm(pick(maps, PF, TOK, 608), rp_ref[...]).astype(BF)
    gm_ref[...] = om_ref[...]
    gw_ref[0] = oq_ref[0:4, 0:DA]
    gw_ref[1] = oq_ref[0:4, DA : 2 * DA]
    gw_ref[2] = oq_ref[4:8, 0:DA]
    gp_ref[...] = oq_ref[4:8, DA : 2 * DA]
    gb_ref[...] = ov_ref[0:HEADS, 0:NREL]
    mg_ref[:, 0:768] = ov_ref[4:5, :]
    mg_ref[:, 768:1536] = ov_ref[5:6, :]
    mg_ref[:, 1536:2048] = ov_ref[6:7, 0:512]
    ag_ref[...] = oa_ref[...]


def local(
    latent, pole_mask, attn_gain, qkv_weight, proj_weight, rel_bias, merge_gain, merge_weight,
    coarse_grad,
):
    maps = jnp.asarray(index_maps())
    dma = pltpu.SemaphoreType.DMA
    vm = pltpu.VMEM
    nb = HEADS * WTOK
    nv, na = (8, 768), (1, D)
    sends = 80
    rp, om, oq, ov, oa = call(
        kmain, "sublayer_backward",
        [
            pole_mask, maps, rel_bias, attn_gain.reshape(1, D), merge_gain.reshape(1, 4 * D),
            latent.reshape(TOK, D), coarse_grad.reshape(144, 512), qkv_weight.transpose(1, 0, 2),
            proj_weight, merge_weight,
        ],
        [((608, D), BF), ((16, 512), F32), ((8, 512), F32), (nv, F32), (na, F32)],
        [
            vm((TOK, D), BF), vm((144, 512), BF), vm((4 * D, 512), BF), vm((2, 3, D, DA), BF),
            vm((2, DA, D), BF), vm((2, 8, 768), F32), vm((WLON * WTOK, 512), BF),
            vm((2, nb, WTOK), F32), vm((48, 512), F32), vm((2, nb, 128), F32),
            vm((608, D), BF), vm((224, 512), BF), vm((608, D), BF), vm((224, 512), BF),
            vm((192, 512), BF), vm((192, 4 * D), BF), vm((192, 4 * D), BF),
            vm((TOK, D), BF), vm((TOK, D), BF), vm((TOK, D), BF), vm((2, TOK, 3 * DA), BF),
            vm((2, NWIN, nb, WTOK), F32), vm((2, TOK, DA), BF), vm((TOK, D), BF),
            vm((2, 96, D), BF), vm((144, 4 * D), BF), vm((TOK, D), BF), vm((1, 4 * D), F32),
            vm((NZ, 2, NY, 32, 512), F32), vm((TOK, D), BF), vm((TOK, D), BF),
            vm((2, TOK, DA), BF),
            vm((2, 3, TOK, DA), BF), vm((nb, WTOK), F32), vm((48, 768), F32),
            vm((2, 2, NY, 32, 1024), F32), vm((608, D), BF), vm(nv, F32), vm(na, F32),
            vm((NY, NZ, 32, 512), BF), vm((2, NY, 32, 1024), BF),
            vm((NY, NZ, 32, 512), BF), vm((2, NY, 32, 1024), BF), vm((2,) + nv, F32),
            vm((2,) + na, F32),
            vm((NZ, 32, 512), F32), vm((NY - 1, NZ, 32, 512), BF), vm((NY - 1, NZ, 32, 512), BF),
            vm((NZ, 32, 512), F32), vm((NZ - 1, 32, 512), BF), vm((NZ - 1, 32, 512), BF),
            vm((2, 16, 512), F32), vm((16, 512), F32),
            vm((NY, 32, 1024), F32), vm((NY, 32, 1024), BF), vm((NY, 32, 1024), BF),
            vm((32, 1024), F32), vm((NY - 1, 32, 1024), BF), vm((NY - 1, 32, 1024), BF),
            vm((NZ, 8, 512), F32), vm((NZ - 1, 8, 512), F32),
            vm((NZ,) + nv, F32), vm((2,) + na, F32), vm((2,) + nv, F32), vm((NY,) + na, F32),
            vm((NY,) + nv, F32), vm((NZ,) + na, F32),
            dma((5,)), dma((sends,)), dma((sends,)),
        ],
        cid=1, mib=58, smem=1, hbm=5,
    )
    lg, ag, gw, gp, gb, mgg, gmm = call(
        kend, "finish", [maps, rp, om, oq, ov, oa],
        [
            ((TOK, D), BF), ((1, D), F32), ((3, 4, DA), F32), ((4, DA), F32),
            ((HEADS, NREL), F32), ((1, 4 * D), F32), ((16, 512), F32),
        ],
        mib=58,
    )
    return (
        lg.reshape(latent.shape),
        ag.reshape(D),
        gw.transpose(1, 0, 2),
        gp.T,
        gb,
        mgg.reshape(4 * D),
        gmm,
    )


def solution(mesh):
    placed = (
        P(None, "lat", "lon", None),
        P(),
        P(),
        P(None, None, "tp"),
        P("tp", None),
        P("tp", None),
        P(),
        P(None, "tp"),
        P(None, "lat", "lon", "tp"),
    )
    return jax.shard_map(
        local,
        mesh=mesh,
        in_specs=placed,
        out_specs=(
            P(None, "lat", "lon", None),
            P(),
            P(("lon", "lat"), None, "tp"),
            P("tp", ("lon", "lat")),
            P("tp", None),
            P(),
            P(("lon", "lat"), "tp"),
        ),
        check_vma=False,
    )
```

```python
import functools

import jax
import jax.numpy as jnp
import numpy as np
from jax import lax
from jax.experimental import pallas as pl
from jax.experimental.pallas import tpu as pltpu
from jax.sharding import PartitionSpec as P

EPS = 1e-05
NEG = -1e30
MESH = pl.DeviceIdType.MESH
BF = jnp.bfloat16
F32 = jnp.float32

LEV, ROWS, COLS, D = 2, 6, 48, 512
WLON = 12
NWIN = COLS // WLON
WTOK = LEV * ROWS * WLON
TOK = LEV * ROWS * COLS
HEADS = 4
HD = 64
DA = HEADS * HD
NREL = 759
NZ, NY = 8, 4


(QL, QL2, QC, QC2, PC, PXM, PXW, PWM, PMW, PPO, PF, FP, E0) = range(13)
MAPW = 768
OUT_PADS = (256, 48, 256, 48)
COARSE_PADS = (96, 16, 96, 16)


def pieces(row_sets, near, far, pads):
    base, out = 0, []
    parts = ((row_sets[0], near), (row_sets[0], far), (row_sets[1], near), (row_sets[1], far))
    for n, ((rows, cols), pad) in enumerate(zip(parts, pads)):
        p = base
        for l in range(LEV):
            for r in rows:
                for c in cols:
                    out.append((p, n, l, r, c))
                    p += 1
        base += pad
    return out


@functools.lru_cache(None)
def index_maps():
    t = np.full((32, MAPW), -1, np.int32)
    near, far = range(0, 42), range(42, 48)

    def merge_at(l, rr, sc):
        return ((rr * 2 + sc % 2) * LEV + l) * 24 + sc // 2

    def window_at(l, rr, sc):
        return (sc // WLON) * WTOK + (l * ROWS + rr - 1) * WLON + sc % WLON

    def seen(n, r, c):
        return (r + 4 if n < 2 else r - 2), (c + 6 if n % 2 == 0 else c - 42)

    for l in range(LEV):
        for rr in range(1, 7):
            for sc in range(COLS):
                t[PWM, window_at(l, rr, sc)] = merge_at(l, rr, sc) - 96
                t[PMW, merge_at(l, rr, sc) - 96] = window_at(l, rr, sc)
    for p, n, l, r, c in pieces((range(0, 3), range(3, 6)), near, far, OUT_PADS):
        rr, sc = seen(n, r, c)
        t[QL if n < 2 else QL2, (l * ROWS + r) * COLS + c] = p
        t[PXM, p] = merge_at(l, rr, sc) - 96
        t[PXW, p] = window_at(l, rr, sc)
        t[PPO, window_at(l, rr, sc)] = p
        t[PF, p] = (l * ROWS + r) * COLS + c
    for p, n, l, r, c in pieces((range(0, 2), range(1, 3)), range(0, 21), range(21, 24), COARSE_PADS):
        t[QC if n < 2 else QC2, (l * 3 + r) * 24 + c] = p
        cr = r + 2 if n < 2 else r - 1
        cc = c + 3 if n % 2 == 0 else c - 21
        t[PC, p] = (cr * LEV + l) * 24 + cc
    order = np.arange(D).reshape(NZ, 2, NY, 2, 4).transpose(1, 3, 2, 0, 4)
    t[FP, 0:D] = order.reshape(-1)
    for c in range(WLON):
        for j in range(WTOK):
            l2, r2, c2 = j // 72, j // 12 % 6, j % 12
            t[E0 + c, ((1 - l2) * 11 + 5 - r2) * 23 + c - c2 + 11] = j
    return t


def pick(maps, n, rows, cols, base=0):
    at = lax.broadcasted_iota(jnp.int32, (rows, cols), 0) + base
    return jnp.where(at == maps[n : n + 1, 0:cols], 1.0, 0.0).astype(BF)


def mm(a, b):
    return lax.dot_general(a, b, (((1,), (0,)), ((), ())), preferred_element_type=F32)


def mm_nt(a, b):
    return lax.dot_general(a, b, (((1,), (1,)), ((), ())), preferred_element_type=F32)


def mm_tn(a, b):
    return lax.dot_general(a, b, (((0,), (0,)), ((), ())), preferred_element_type=F32)


def layer_stats(x):
    center = x - jnp.mean(x, -1, keepdims=True)
    inverse = lax.rsqrt(jnp.mean(center * center, -1, keepdims=True) + EPS)
    return center * inverse, inverse


def norm_back(up, gain, normed, inverse):
    s = up * gain
    return inverse * (
        s - jnp.mean(s, -1, keepdims=True) - normed * jnp.mean(s * normed, -1, keepdims=True)
    )


def head_mask(h, rows):
    lane = lax.broadcasted_iota(jnp.int32, (rows, DA), 1)
    return (lane >= h * HD) & (lane < (h + 1) * HD)


def stack_heads(x):
    zero = jnp.zeros_like(x)
    return jnp.concatenate(
        [jnp.where(head_mask(h, x.shape[0]), x, zero) for h in range(HEADS)], 0
    )


def vspec():
    return pl.BlockSpec(memory_space=pltpu.VMEM)


def call(kernel, name, ins, outs, scratch=(), cid=None, smem=0, hbm=0, mib=16):
    params = dict(vmem_limit_bytes=mib << 20)
    if cid is not None:
        params.update(collective_id=cid, has_side_effects=True)
    specs = [pl.BlockSpec(memory_space=pltpu.SMEM)] * smem
    specs += [vspec()] * (len(ins) - smem - hbm) + [pl.BlockSpec(memory_space=pl.ANY)] * hbm
    return pl.pallas_call(
        kernel,
        out_shape=[jax.ShapeDtypeStruct(s, d) for s, d in outs],
        in_specs=specs,
        out_specs=[vspec()] * len(outs),
        scratch_shapes=list(scratch),
        compiler_params=pltpu.CompilerParams(**params),
        name=name,
    )(*ins)


def device(dlon, dlat, dtp):
    nlon, nlat = lax.axis_size("lon"), lax.axis_size("lat")
    return (
        lax.rem(lax.axis_index("lon") + dlon + nlon, nlon),
        lax.rem(lax.axis_index("lat") + dlat + nlat, nlat),
        lax.rem(lax.axis_index("tp") + dtp, 2),
    )


def remote(src, dst, ss, rs, n, dev):
    return pltpu.make_async_remote_copy(
        src, dst, ss.at[n], rs.at[n], device_id=dev, device_id_type=MESH
    )


class Links:
    def __init__(self, ss, rs):
        self.ss, self.rs, self.n = ss, rs, 0

    def send(self, src, dst, dev):
        c = remote(src, dst, self.ss, self.rs, self.n, dev)
        self.n += 1
        c.start()
        return c


def wait(copies):
    for c in copies:
        c.wait()


def kmain(
    pole_ref, maps, tab_ref, gain_ref, mgain_ref, lat_hbm, cg_hbm, w_hbm, proj_hbm, mw_hbm,
    rp_ref, om_ref, oq_ref, ov_ref, oa_ref,
    lat, cg, mw, wf, pf, tabs, et, bm, u, wide,
    sp, sc, pc, cc, cmt, dmo, dmp,
    xw, hn, hnp, qkv, pr, ao, y, yh, mb, dyt, mg,
    gm, dyw, dyp, do, dqkv, dst, t, gq, lp, sv, av,
    sm1, sq1, rm1, rq1, sv1, av1,
    am, sm2, rm2, bmm, sm3, rm3, cm, rm4,
    aq, sq2, rq2, bq, sq3, rq3, cq, rq4,
    sv2, sv3, sv4, av2, ls, ss, rs,
):
    lon, band, tp = lax.axis_index("lon"), lax.axis_index("lat"), lax.axis_index("tp")
    z, core = lax.div(lon, 2), lax.rem(lon, 2)
    yy, xx = lax.div(band, 2), lax.rem(band, 2)
    peer = device(0, 0, 1)
    core_dev = (z * 2 + 1 - core, band, tp)
    x_dev = (lon, yy * 2 + 1 - xx, tp)
    y_devs = [(lon, lax.rem(yy + k, NY) * 2 + xx, tp) for k in range(1, NY)]
    z_devs = [(lax.rem(z + k, NZ) * 2 + core, band, tp) for k in range(1, NZ)]
    near = [device(s * o, s * a, 0) for s in (1, -1) for o, a in ((1, 0), (0, 1), (1, 1))]
    group = [
        (z * 2 + lax.rem(core + a, 2), lax.rem(yy + c, NY) * 2 + lax.rem(xx + b, 2), tp)
        for a in range(2)
        for b in range(2)
        for c in range(NY)
    ][1:]
    partners = [peer] + group + z_devs + near
    barrier = pltpu.get_barrier_semaphore()
    for dev in partners:
        pl.semaphore_signal(barrier, inc=1, device_id=dev, device_id_type=MESH)
    links = Links(ss, rs)
    scale = HD**-0.5
    other = 1 - tp

    loads = []
    for n, (src, into) in enumerate(
        ((lat_hbm, lat), (cg_hbm, cg), (w_hbm, wf.at[tp]), (proj_hbm, pf.at[tp]), (mw_hbm, mw))
    ):
        loads.append(pltpu.make_async_copy(src, into, ls.at[n]))
        loads[-1].start()

    nrows = pole_ref.shape[0]
    i = lax.broadcasted_iota(jnp.int32, (WTOK, WTOK), 0)
    j = lax.broadcasted_iota(jnp.int32, (WTOK, WTOK), 1)
    ri, rj = lax.rem(lax.div(i, WLON), ROWS), lax.rem(lax.div(j, WLON), ROWS)
    valid = jnp.zeros((WTOK, WTOK), jnp.int32)
    for r in range(ROWS):
        flag = pole_ref[lax.rem(band * ROWS + (r - 3 + nrows), nrows)]
        valid = jnp.where(rj == r, flag, valid)
    cut = jnp.where(band == 0, 3, 0)
    same = jnp.where(ri < cut, 1, 0) == jnp.where(rj < cut, 1, 0)
    allowed = (valid > 0) & same

    def build_bias(g):
        for l in range(LEV):
            for r in range(ROWS):
                shift = (l * 11 + r) * 23
                row = tabs[g]
                if shift:
                    row = pltpu.roll(row, 768 - shift, 1)
                for h in range(HEADS):
                    n = h * 12 + l * ROWS + r
                    u[n : n + 1, :] = row[h : h + 1, :512]
        t0 = u[...]
        hi = t0.astype(BF)
        rest = t0 - hi.astype(F32)
        mid = rest.astype(BF)
        low = (rest - mid.astype(F32)).astype(BF)
        split = jnp.concatenate([hi, mid, low], 0)
        for c in range(WLON):
            v = mm_nt(split, et[c * WTOK : (c + 1) * WTOK, :])
            v = v[0:48] + v[48:96] + v[96:144]
            wide[0, pl.ds(c, 48, stride=WLON), :] = v[:, 0:128]
            wide[1, pl.ds(c, 48, stride=WLON), :] = jnp.concatenate(
                [v[:, 128:WTOK], jnp.zeros((48, 256 - WTOK), F32)], 1
            )
        for h in range(HEADS):
            rows = slice(h * WTOK, (h + 1) * WTOK)
            both = jnp.concatenate([wide[0, rows, :], wide[1, rows, 0 : WTOK - 128]], 1)
            bm[g, rows, :] = jnp.where(allowed, both, NEG)

    tabs[tp] = jnp.zeros((8, 768), F32)
    tabs[tp, 0:HEADS, 0:NREL] = tab_ref[...]
    loads[0].wait()
    loads[1].wait()
    for m, lo, hi in ((QL2, 304, 608), (QL, 256, 304)):
        sp[lo:hi, :] = mm(pick(maps, m, hi - lo, TOK, lo), lat[...]).astype(BF)
    for m, lo, hi in ((QC2, 112, 224), (QC, 96, 112)):
        sc[lo:hi, :] = mm(pick(maps, m, hi - lo, 144, lo), cg[...]).astype(BF)
    loads[2].wait()
    loads[3].wait()
    at = pl.ds(pl.multiple_of(core * 256 + yy * 64, 64), 64)
    pat = pl.ds(pl.multiple_of(core * 128 + yy * 32, 32), 32)
    half = pl.ds(pl.multiple_of(core * 256, 256), 256)
    phalf = pl.ds(pl.multiple_of(core * 128, 128), 128)
    pl.semaphore_wait(barrier, len(partners))
    chalo = [links.send(sc.at[112:208], cc.at[112:208], device(0, 1, 0))]
    halo = [links.send(sp.at[304:560], pc.at[304:560], device(0, 1, 0))]
    chalo.append(links.send(sc.at[208:224], cc.at[208:224], device(1, 1, 0)))
    chalo.append(links.send(sc.at[96:112], cc.at[96:112], device(1, 0, 0)))
    first = [
        links.send(wf.at[tp, :, at], wf.at[tp, :, at], peer),
        links.send(pf.at[tp, pat], pf.at[tp, pat], peer),
    ]
    halo.append(links.send(sp.at[560:608], pc.at[560:608], device(1, 1, 0)))
    halo.append(links.send(sp.at[256:304], pc.at[256:304], device(1, 0, 0)))
    tabc = [links.send(tabs.at[tp], tabs.at[tp], peer)]
    pc[0:256, :] = mm(pick(maps, QL, 256, TOK), lat[...]).astype(BF)
    cc[0:96, :] = mm(pick(maps, QC, 96, 144), cg[...]).astype(BF)
    for c in range(WLON):
        et[c * WTOK : (c + 1) * WTOK, :] = pick(maps, E0 + c, WTOK, 512)
    loads[4].wait()
    wait(chalo)
    cmt[...] = mm(pick(maps, PC, 192, 224), cc[...]).astype(BF)
    for n in range(4):
        cols = slice(n * 512, (n + 1) * 512)
        dmo[:, cols] = mm_nt(cmt[...], mw[cols, :]).astype(BF)
    dmc = [links.send(dmo.at[48:144], dmp.at[48:144], peer)]
    dmh = [
        links.send(dmo.at[0:48], dmp.at[0:48], peer),
        links.send(dmo.at[144:192], dmp.at[144:192], peer),
    ]
    wait(first)
    ring = []
    for dev in y_devs:
        for ref in (wf.at[other, :, at], pf.at[other, pat]):
            ring.append(links.send(ref, ref, dev))
    build_bias(tp)
    wait(halo)

    x = mm(pick(maps, PXW, TOK, 608), pc[...])
    xw[...] = x.astype(BF)
    normed, _ = layer_stats(x)
    hn[...] = (normed * gain_ref[...]).astype(BF)

    def forward(g):
        for n in range(3):
            qkv[g, :, n * DA : (n + 1) * DA] = mm(hn[...], wf[g, n]).astype(BF)

        def window(w, carry):
            rows = pl.ds(pl.multiple_of(w * WTOK, 16), WTOK)
            q = qkv[g, rows, 0:DA]
            k = qkv[g, rows, DA : 2 * DA]
            v = qkv[g, rows, 2 * DA : 3 * DA]
            s = mm_nt(stack_heads(q), k) * scale + bm[g]
            e = jnp.exp(s - jnp.max(s, -1, keepdims=True))
            p = e / jnp.sum(e, -1, keepdims=True)
            pr[g, w] = p
            pb = p.astype(BF)
            vs = stack_heads(v)
            o = jnp.zeros((WTOK, DA), F32)
            for h in range(HEADS):
                hs = slice(h * WTOK, (h + 1) * WTOK)
                o = o + mm(pb[hs], vs[hs])
            ao[g, rows, :] = o.astype(BF)
            return carry

        lax.fori_loop(0, NWIN, window, 0)

    forward(tp)
    features = pick(maps, FP, D, D)
    hnp[...] = mm(hn[...], features).astype(BF)
    wait(ring)
    pair = [links.send(r, r, core_dev) for r in (wf.at[other, :, half], pf.at[other, phalf])]
    wait(tabc)
    build_bias(other)
    wait(pair)
    forward(other)
    def residual(lo, hi):
        to_merge = pick(maps, PWM, hi - lo, TOK, lo)
        x = mm(pick(maps, PXM, hi - lo, 608, lo), pc[...])
        for g in range(2):
            x = x + mm(mm(to_merge, ao[g]).astype(BF), pf[g])
        y[lo:hi, :] = x.astype(BF)

    residual(0, 96)
    yhc = [links.send(y.at[0:96], yh.at[1], device(0, -1, 0))]
    residual(480, 576)
    yhc.append(links.send(y.at[480:576], yh.at[0], device(0, 1, 0)))
    residual(96, 480)

    wait(dmc)
    mgain = mgain_ref[...]
    acc = jnp.zeros((1, 4 * D), F32)

    def slab(r, cp):
        lo = cp * 48
        if r == 0:
            return yh[0, lo : lo + 48, :]
        if r == 7:
            return yh[1, lo : lo + 48, :]
        lo += (r - 1) * 96
        return y[lo : lo + 48, :]

    for cr in (1, 2, 0, 3):
        if cr == 0:
            wait(yhc)
            wait(dmh)
        slabs = [slab(2 * cr + rp, cp) for rp in (0, 1) for cp in (0, 1)]
        hat, inv = layer_stats(jnp.concatenate(slabs, 1).astype(F32))
        rows = slice(cr * 48, (cr + 1) * 48)
        dm = dmo[rows, :].astype(F32) + dmp[rows, :].astype(F32)
        if cr > 0:
            acc = acc + jnp.sum(dm * hat, 0, keepdims=True)
            mb[(cr - 1) * 48 : cr * 48, :] = (hat * mgain).astype(BF)
        dy = norm_back(dm, mgain, hat, inv).astype(BF)
        for q in range(4):
            r = 2 * cr + q // 2
            if 1 <= r <= 6:
                lo = (r - 1) * 96 + (q % 2) * 48
                dyt[lo : lo + 48, :] = dy[:, q * D : (q + 1) * D]
    mg[...] = acc

    for iz in range(NZ):
        part = mm_tn(mb[:, iz * 256 : (iz + 1) * 256], cmt[48:192, :])
        gm[iz] = part.reshape(2, NY, 32, 512)
    turns = [lax.rem(yy + k, NY) for k in (1, 2, 3, 0)]
    m1 = []
    for iy in turns:
        for iz in range(NZ):
            sm1[iy, iz] = gm[iz, 1 - core, iy].astype(BF)
        m1.append(links.send(sm1.at[iy], rm1.at[iy], core_dev))

    dyw[...] = mm(pick(maps, PMW, TOK, TOK), dyt[...]).astype(BF)
    for g in range(2):
        do[g] = mm_nt(dyw[...], pf[g]).astype(BF)
    dst[...] = jnp.zeros_like(dst)

    def backward(g, mine, lo=0, hi=NWIN):
        def window(w, carry):
            rows = pl.ds(pl.multiple_of(w * WTOK, 16), WTOK)
            q = qkv[g, rows, 0:DA]
            k = qkv[g, rows, DA : 2 * DA]
            v = qkv[g, rows, 2 * DA : 3 * DA]
            p = pr[g, w]
            dos = stack_heads(do[g, rows, :])
            dp = mm_nt(dos, v)
            dv = mm_tn(p.astype(BF), dos)
            ds = p * (dp - jnp.sum(dp * p, -1, keepdims=True))
            if mine:
                dst[...] = dst[...] + ds
            dsb = ds.astype(BF)
            dk = mm_tn(dsb, stack_heads(q)) * scale
            ks = stack_heads(k)
            dq = jnp.zeros((WTOK, DA), F32)
            for h in range(HEADS):
                hs = slice(h * WTOK, (h + 1) * WTOK)
                dq = dq + mm(dsb[hs], ks[hs])
            dqkv[g, 0, rows, :] = (dq * scale).astype(BF)
            dqkv[g, 1, rows, :] = dk.astype(BF)
            dqkv[g, 2, rows, :] = dv.astype(BF)
            return carry

        lax.fori_loop(lo, hi, window, 0)

    m2 = []
    for k in range(1, NY):
        wait(m1[k - 1 : k])
        iy = turns[k - 1]
        for iz in range(NZ):
            sm2[k - 1, iz] = (gm[iz, core, iy] + rm1[iy, iz].astype(F32)).astype(BF)
        m2.append(links.send(sm2.at[k - 1], rm2.at[k - 1], y_devs[k - 1]))
    wait(m1[3:])

    backward(tp, True)

    dyp[...] = mm(dyw[...], features).astype(BF)
    for n in range(4):
        part = mm_tn(hnp[...], dqkv[tp, n]) if n < 3 else mm_tn(dyp[...], ao[tp])
        gq[:, :, :, :, n * DA : (n + 1) * DA] = part.reshape(2, 2, NY, 32, DA)
    sq1[...] = gq[1 - core].astype(BF)
    q1 = [links.send(sq1, rq1, core_dev)]
    for iz in range(NZ):
        am[iz] = gm[iz, core, yy] + rm1[yy, iz].astype(F32)

    wide[0] = dst[:, 0:128]
    wide[1, :, 0 : WTOK - 128] = dst[:, 128:WTOK]
    acc = jnp.zeros((48, 512), F32)
    for c in range(WLON):
        rows = pl.ds(c, 48, stride=WLON)
        x = jnp.concatenate([wide[0, rows, :], wide[1, rows, :][:, 0 : WTOK - 128]], 1)
        hi = x.astype(BF)
        low = (x - hi.astype(F32)).astype(BF)
        v = mm(jnp.concatenate([hi, low], 0), et[c * WTOK : (c + 1) * WTOK, :])
        acc = acc + v[0:48] + v[48:96]
    t[:, 0:512] = acc
    t[:, 512:768] = jnp.zeros((48, 256), F32)
    for h in range(HEADS):
        out = jnp.zeros((1, 768), F32)
        for g in range(12):
            row = t[h * 12 + g : h * 12 + g + 1, :]
            shift = (g // ROWS * 11 + g % ROWS) * 23
            out = out + (pltpu.roll(row, shift, 1) if shift else row)
        sv[h : h + 1, :] = out
    sv[4:5, :] = mg[:, 0:768]
    sv[5:6, :] = mg[:, 768:1536]
    sv[6:7, 0:512] = mg[:, 1536:2048]
    sv[6:7, 512:768] = jnp.zeros((1, 256), F32)
    sv[7:8, :] = jnp.zeros((1, 768), F32)
    sv1[core] = sv[...]
    v1 = [links.send(sv1.at[core], sv1.at[core], core_dev)]

    wait(q1)
    sq2[...] = (gq[core, 1 - xx] + rq1[1 - xx].astype(F32)).astype(BF)
    q2 = [links.send(sq2, rq2, x_dev)]
    aq[...] = gq[core, xx] + rq1[xx].astype(F32)
    wait(v1)
    sv2[z] = sv1[0] + sv1[1]
    v2 = [links.send(sv2.at[z], sv2.at[z], dev) for dev in z_devs]

    backward(other, False)

    wait(q2)
    q3 = []
    for k in range(1, NY):
        iy = lax.rem(yy + k, NY)
        sq3[k - 1] = (aq[iy] + rq2[iy].astype(F32)).astype(BF)
        q3.append(links.send(sq3.at[k - 1], rq3.at[k - 1], y_devs[k - 1]))
    bq[...] = aq[yy] + rq2[yy].astype(F32)

    wait(m2)
    for iz in range(NZ):
        acc = am[iz]
        for k in range(NY - 1):
            acc = acc + rm2[k, iz].astype(F32)
        bmm[iz] = acc
    m3 = []
    for k in range(1, NZ):
        sm3[k - 1] = bmm[lax.rem(z + k, NZ)].astype(BF)
        m3.append(links.send(sm3.at[k - 1], rm3.at[k - 1], z_devs[k - 1]))

    dh = jnp.zeros((TOK, D), F32)
    for g in range(2):
        for n in range(3):
            dh = dh + mm_nt(dqkv[g, n], wf[g, n])
    normed, inv = layer_stats(xw[...].astype(F32))
    av[...] = jnp.sum(dh * normed, 0, keepdims=True)
    me = (core * 2 + xx) * NY + yy
    av1[me] = av[...]
    a1 = [links.send(av1.at[me], av1.at[me], dev) for dev in group]
    branch = norm_back(dh, gain_ref[...], normed, inv).astype(BF)
    lg = (dyw[...].astype(F32) + branch.astype(F32)).astype(BF)
    lp[...] = mm(pick(maps, PPO, 608, TOK), lg).astype(BF)
    ro = [
        links.send(lp.at[304:560], rp_ref.at[304:560], device(0, -1, 0)),
        links.send(lp.at[256:304], rp_ref.at[256:304], device(-1, 0, 0)),
        links.send(lp.at[560:608], rp_ref.at[560:608], device(-1, -1, 0)),
    ]
    rp_ref[0:256, :] = lp[0:256, :]
    wait(v2)
    acc = sv2[0]
    for k in range(1, NZ):
        acc = acc + sv2[k]
    sv3[xx] = acc
    v3 = [links.send(sv3.at[xx], sv3.at[xx], x_dev)]
    wait(q3)
    acc = bq[...]
    for k in range(NY - 1):
        acc = acc + rq3[k].astype(F32)
    for iz in range(NZ):
        rows = slice(iz * 4, iz * 4 + 4)
        cq[iz] = jnp.concatenate([acc[rows, 0:512], acc[rows, 512:1024]], 0)
    q4 = []
    for k in range(1, NZ):
        q4.append(links.send(cq.at[lax.rem(z + k, NZ)], rq4.at[k - 1], z_devs[k - 1]))

    wait(a1)
    acc = av1[0]
    for k in range(1, 4 * NY):
        acc = acc + av1[k]
    av2[z] = acc
    a2 = [links.send(av2.at[z], av2.at[z], dev) for dev in z_devs]
    wait(v3)
    sv4[yy] = sv3[0] + sv3[1]
    v4 = [links.send(sv4.at[yy], sv4.at[yy], dev) for dev in y_devs]

    wait(m3)
    acc = bmm[z]
    for k in range(NZ - 1):
        acc = acc + rm3[k].astype(F32)
    cm[0] = acc[0:16]
    cm[1] = acc[16:32]
    m4 = [links.send(cm.at[1 - xx], rm4, x_dev)]
    wait(m4)
    om_ref[...] = cm[xx] + rm4[...]
    wait(q4)
    acc = cq[z]
    for k in range(NZ - 1):
        acc = acc + rq4[k]
    oq_ref[...] = acc
    wait(v4)
    ov_ref[...] = sv4[0] + sv4[1] + sv4[2] + sv4[3]
    wait(a2)
    acc = av2[0]
    for k in range(1, NZ):
        acc = acc + av2[k]
    oa_ref[...] = acc
    wait(ro)


def kend(
    maps, rp_ref, om_ref, oq_ref, ov_ref, oa_ref, lg_ref, ag_ref, gw_ref, gp_ref, gb_ref, mg_ref,
    gm_ref,
):
    lg_ref[...] = mm(pick(maps, PF, TOK, 608), rp_ref[...]).astype(BF)
    gm_ref[...] = om_ref[...]
    gw_ref[0] = oq_ref[0:4, 0:DA]
    gw_ref[1] = oq_ref[0:4, DA : 2 * DA]
    gw_ref[2] = oq_ref[4:8, 0:DA]
    gp_ref[...] = oq_ref[4:8, DA : 2 * DA]
    gb_ref[...] = ov_ref[0:HEADS, 0:NREL]
    mg_ref[:, 0:768] = ov_ref[4:5, :]
    mg_ref[:, 768:1536] = ov_ref[5:6, :]
    mg_ref[:, 1536:2048] = ov_ref[6:7, 0:512]
    ag_ref[...] = oa_ref[...]


def local(
    latent, pole_mask, attn_gain, qkv_weight, proj_weight, rel_bias, merge_gain, merge_weight,
    coarse_grad,
):
    maps = jnp.asarray(index_maps())
    dma = pltpu.SemaphoreType.DMA
    vm = pltpu.VMEM
    nb = HEADS * WTOK
    nv, na = (8, 768), (1, D)
    sends = 96
    rp, om, oq, ov, oa = call(
        kmain, "sublayer_backward",
        [
            pole_mask, maps, rel_bias, attn_gain.reshape(1, D), merge_gain.reshape(1, 4 * D),
            latent.reshape(TOK, D), coarse_grad.reshape(144, 512), qkv_weight.transpose(1, 0, 2),
            proj_weight, merge_weight,
        ],
        [((608, D), BF), ((16, 512), F32), ((8, 512), F32), (nv, F32), (na, F32)],
        [
            vm((TOK, D), BF), vm((144, 512), BF), vm((4 * D, 512), BF), vm((2, 3, D, DA), BF),
            vm((2, DA, D), BF), vm((2, 8, 768), F32), vm((WLON * WTOK, 512), BF),
            vm((2, nb, WTOK), F32), vm((48, 512), F32), vm((2, nb, 128), F32),
            vm((608, D), BF), vm((224, 512), BF), vm((608, D), BF), vm((224, 512), BF),
            vm((192, 512), BF), vm((192, 4 * D), BF), vm((192, 4 * D), BF),
            vm((TOK, D), BF), vm((TOK, D), BF), vm((TOK, D), BF), vm((2, TOK, 3 * DA), BF),
            vm((2, NWIN, nb, WTOK), F32), vm((2, TOK, DA), BF), vm((TOK, D), BF),
            vm((2, 96, D), BF), vm((144, 4 * D), BF), vm((TOK, D), BF), vm((1, 4 * D), F32),
            vm((NZ, 2, NY, 32, 512), F32), vm((TOK, D), BF), vm((TOK, D), BF),
            vm((2, TOK, DA), BF),
            vm((2, 3, TOK, DA), BF), vm((nb, WTOK), F32), vm((48, 768), F32),
            vm((2, 2, NY, 32, 1024), F32), vm((608, D), BF), vm(nv, F32), vm(na, F32),
            vm((NY, NZ, 32, 512), BF), vm((2, NY, 32, 1024), BF),
            vm((NY, NZ, 32, 512), BF), vm((2, NY, 32, 1024), BF), vm((2,) + nv, F32),
            vm((4 * NY,) + na, F32),
            vm((NZ, 32, 512), F32), vm((NY - 1, NZ, 32, 512), BF), vm((NY - 1, NZ, 32, 512), BF),
            vm((NZ, 32, 512), F32), vm((NZ - 1, 32, 512), BF), vm((NZ - 1, 32, 512), BF),
            vm((2, 16, 512), F32), vm((16, 512), F32),
            vm((NY, 32, 1024), F32), vm((NY, 32, 1024), BF), vm((NY, 32, 1024), BF),
            vm((32, 1024), F32), vm((NY - 1, 32, 1024), BF), vm((NY - 1, 32, 1024), BF),
            vm((NZ, 8, 512), F32), vm((NZ - 1, 8, 512), F32),
            vm((NZ,) + nv, F32), vm((2,) + nv, F32), vm((NY,) + nv, F32), vm((NZ,) + na, F32),
            dma((5,)), dma((sends,)), dma((sends,)),
        ],
        cid=1, mib=58, smem=1, hbm=5,
    )
    lg, ag, gw, gp, gb, mgg, gmm = call(
        kend, "finish", [maps, rp, om, oq, ov, oa],
        [
            ((TOK, D), BF), ((1, D), F32), ((3, 4, DA), F32), ((4, DA), F32),
            ((HEADS, NREL), F32), ((1, 4 * D), F32), ((16, 512), F32),
        ],
        mib=58,
    )
    return (
        lg.reshape(latent.shape),
        ag.reshape(D),
        gw.transpose(1, 0, 2),
        gp.T,
        gb,
        mgg.reshape(4 * D),
        gmm,
    )


def solution(mesh):
    placed = (
        P(None, "lat", "lon", None),
        P(),
        P(),
        P(None, None, "tp"),
        P("tp", None),
        P("tp", None),
        P(),
        P(None, "tp"),
        P(None, "lat", "lon", "tp"),
    )
    return jax.shard_map(
        local,
        mesh=mesh,
        in_specs=placed,
        out_specs=(
            P(None, "lat", "lon", None),
            P(),
            P(("lon", "lat"), None, "tp"),
            P("tp", ("lon", "lat")),
            P("tp", None),
            P(),
            P(("lon", "lat"), "tp"),
        ),
        check_vma=False,
    )
```

```python
import functools

import jax
import jax.numpy as jnp
import numpy as np
from jax import lax
from jax.experimental import pallas as pl
from jax.experimental.pallas import tpu as pltpu
from jax.sharding import PartitionSpec as P

EPS = 1e-05
NEG = -1e30
MESH = pl.DeviceIdType.MESH
BF = jnp.bfloat16
F32 = jnp.float32

LEV, ROWS, COLS, D = 2, 6, 48, 512
WLON = 12
NWIN = COLS // WLON
WTOK = LEV * ROWS * WLON
TOK = LEV * ROWS * COLS
HEADS = 4
HD = 64
DA = HEADS * HD
NREL = 759
NZ, NY = 8, 4
FAR_Y = (2, 1, 3)
FAR_Z = (4, 3, 5, 2, 6, 1, 7)


(QL, QL2, QC, QC2, PC, PXM, PXW, PWM, PMW, PPO, PF, FP, E0) = range(13)
MAPW = 768
OUT_PADS = (256, 48, 256, 48)
COARSE_PADS = (96, 16, 96, 16)


def pieces(row_sets, near, far, pads):
    base, out = 0, []
    parts = ((row_sets[0], near), (row_sets[0], far), (row_sets[1], near), (row_sets[1], far))
    for n, ((rows, cols), pad) in enumerate(zip(parts, pads)):
        p = base
        for l in range(LEV):
            for r in rows:
                for c in cols:
                    out.append((p, n, l, r, c))
                    p += 1
        base += pad
    return out


@functools.lru_cache(None)
def index_maps():
    t = np.full((32, MAPW), -1, np.int32)
    near, far = range(0, 42), range(42, 48)

    def merge_at(l, rr, sc):
        return ((rr * 2 + sc % 2) * LEV + l) * 24 + sc // 2

    def window_at(l, rr, sc):
        return (sc // WLON) * WTOK + (l * ROWS + rr - 1) * WLON + sc % WLON

    def seen(n, r, c):
        return (r + 4 if n < 2 else r - 2), (c + 6 if n % 2 == 0 else c - 42)

    for l in range(LEV):
        for rr in range(1, 7):
            for sc in range(COLS):
                t[PWM, window_at(l, rr, sc)] = merge_at(l, rr, sc) - 96
                t[PMW, merge_at(l, rr, sc) - 96] = window_at(l, rr, sc)
    for p, n, l, r, c in pieces((range(0, 3), range(3, 6)), near, far, OUT_PADS):
        rr, sc = seen(n, r, c)
        t[QL if n < 2 else QL2, (l * ROWS + r) * COLS + c] = p
        t[PXM, p] = merge_at(l, rr, sc) - 96
        t[PXW, p] = window_at(l, rr, sc)
        t[PPO, window_at(l, rr, sc)] = p
        t[PF, p] = (l * ROWS + r) * COLS + c
    for p, n, l, r, c in pieces((range(0, 2), range(1, 3)), range(0, 21), range(21, 24), COARSE_PADS):
        t[QC if n < 2 else QC2, (l * 3 + r) * 24 + c] = p
        cr = r + 2 if n < 2 else r - 1
        cc = c + 3 if n % 2 == 0 else c - 21
        t[PC, p] = (cr * LEV + l) * 24 + cc
    order = np.arange(D).reshape(NZ, 2, NY, 2, 4).transpose(1, 3, 2, 0, 4)
    t[FP, 0:D] = order.reshape(-1)
    for c in range(WLON):
        for j in range(WTOK):
            l2, r2, c2 = j // 72, j // 12 % 6, j % 12
            t[E0 + c, ((1 - l2) * 11 + 5 - r2) * 23 + c - c2 + 11] = j
    return t


def pick(maps, n, rows, cols, base=0):
    at = lax.broadcasted_iota(jnp.int32, (rows, cols), 0) + base
    return jnp.where(at == maps[n : n + 1, 0:cols], 1.0, 0.0).astype(BF)


def mm(a, b):
    return lax.dot_general(a, b, (((1,), (0,)), ((), ())), preferred_element_type=F32)


def mm_nt(a, b):
    return lax.dot_general(a, b, (((1,), (1,)), ((), ())), preferred_element_type=F32)


def mm_tn(a, b):
    return lax.dot_general(a, b, (((0,), (0,)), ((), ())), preferred_element_type=F32)


def layer_stats(x):
    center = x - jnp.mean(x, -1, keepdims=True)
    inverse = lax.rsqrt(jnp.mean(center * center, -1, keepdims=True) + EPS)
    return center * inverse, inverse


def norm_back(up, gain, normed, inverse):
    s = up * gain
    return inverse * (
        s - jnp.mean(s, -1, keepdims=True) - normed * jnp.mean(s * normed, -1, keepdims=True)
    )


def head_mask(h, rows):
    lane = lax.broadcasted_iota(jnp.int32, (rows, DA), 1)
    return (lane >= h * HD) & (lane < (h + 1) * HD)


def stack_heads(x):
    zero = jnp.zeros_like(x)
    return jnp.concatenate(
        [jnp.where(head_mask(h, x.shape[0]), x, zero) for h in range(HEADS)], 0
    )


def vspec():
    return pl.BlockSpec(memory_space=pltpu.VMEM)


def call(kernel, name, ins, outs, scratch=(), cid=None, smem=0, hbm=0, mib=16):
    params = dict(vmem_limit_bytes=mib << 20)
    if cid is not None:
        params.update(collective_id=cid, has_side_effects=True)
    specs = [pl.BlockSpec(memory_space=pltpu.SMEM)] * smem
    specs += [vspec()] * (len(ins) - smem - hbm) + [pl.BlockSpec(memory_space=pl.ANY)] * hbm
    return pl.pallas_call(
        kernel,
        out_shape=[jax.ShapeDtypeStruct(s, d) for s, d in outs],
        in_specs=specs,
        out_specs=[vspec()] * len(outs),
        scratch_shapes=list(scratch),
        compiler_params=pltpu.CompilerParams(**params),
        name=name,
    )(*ins)


def device(dlon, dlat, dtp):
    nlon, nlat = lax.axis_size("lon"), lax.axis_size("lat")
    return (
        lax.rem(lax.axis_index("lon") + dlon + nlon, nlon),
        lax.rem(lax.axis_index("lat") + dlat + nlat, nlat),
        lax.rem(lax.axis_index("tp") + dtp, 2),
    )


def remote(src, dst, ss, rs, n, dev):
    return pltpu.make_async_remote_copy(
        src, dst, ss.at[n], rs.at[n], device_id=dev, device_id_type=MESH
    )


class Links:
    def __init__(self, ss, rs):
        self.ss, self.rs, self.n = ss, rs, 0

    def send(self, src, dst, dev):
        c = remote(src, dst, self.ss, self.rs, self.n, dev)
        self.n += 1
        c.start()
        return c


def wait(copies):
    for c in copies:
        c.wait()


def kmain(
    pole_ref, maps, tab_ref, gain_ref, mgain_ref, lat_hbm, cg_hbm, w_hbm, proj_hbm, mw_hbm,
    rp_ref, om_ref, oq_ref, ov_ref, oa_ref,
    lat, cg, mw, wf, pf, tabs, et, bm, u, wide,
    sp, sc, pc, cc, cmt, dmo, dmp,
    xw, hn, hnp, qkv, pr, ao, y, yh, mb, dyt, mg,
    gm, dyw, dyp, do, dqkv, dst, t, gq, lp, sv, av,
    sm1, sq1, rm1, rq1, sv1, av1,
    am, sm2, rm2, bmm, sm3, rm3, cm, rm4,
    aq, sq2, rq2, bq, sq3, rq3, cq, rq4,
    sv2, sv3, sv4, av2, ls, ss, rs,
):
    lon, band, tp = lax.axis_index("lon"), lax.axis_index("lat"), lax.axis_index("tp")
    z, core = lax.div(lon, 2), lax.rem(lon, 2)
    yy, xx = lax.div(band, 2), lax.rem(band, 2)
    peer = device(0, 0, 1)
    core_dev = (z * 2 + 1 - core, band, tp)
    x_dev = (lon, yy * 2 + 1 - xx, tp)
    y_devs = [(lon, lax.rem(yy + k, NY) * 2 + xx, tp) for k in range(1, NY)]
    z_devs = [(lax.rem(z + k, NZ) * 2 + core, band, tp) for k in range(1, NZ)]
    near = [device(s * o, s * a, 0) for s in (1, -1) for o, a in ((1, 0), (0, 1), (1, 1))]
    group = [
        (z * 2 + lax.rem(core + a, 2), lax.rem(yy + c, NY) * 2 + lax.rem(xx + b, 2), tp)
        for a in range(2)
        for b in range(2)
        for c in range(NY)
    ][1:]
    partners = [peer] + group + z_devs + near
    barrier = pltpu.get_barrier_semaphore()
    for dev in partners:
        pl.semaphore_signal(barrier, inc=1, device_id=dev, device_id_type=MESH)
    links = Links(ss, rs)
    scale = HD**-0.5
    other = 1 - tp

    loads = []
    for n, (src, into) in enumerate(
        ((lat_hbm, lat), (cg_hbm, cg), (w_hbm, wf.at[tp]), (proj_hbm, pf.at[tp]), (mw_hbm, mw))
    ):
        loads.append(pltpu.make_async_copy(src, into, ls.at[n]))
        loads[-1].start()

    nrows = pole_ref.shape[0]
    i = lax.broadcasted_iota(jnp.int32, (WTOK, WTOK), 0)
    j = lax.broadcasted_iota(jnp.int32, (WTOK, WTOK), 1)
    ri, rj = lax.rem(lax.div(i, WLON), ROWS), lax.rem(lax.div(j, WLON), ROWS)
    valid = jnp.zeros((WTOK, WTOK), jnp.int32)
    for r in range(ROWS):
        flag = pole_ref[lax.rem(band * ROWS + (r - 3 + nrows), nrows)]
        valid = jnp.where(rj == r, flag, valid)
    cut = jnp.where(band == 0, 3, 0)
    same = jnp.where(ri < cut, 1, 0) == jnp.where(rj < cut, 1, 0)
    allowed = (valid > 0) & same

    def build_bias(g):
        for l in range(LEV):
            for r in range(ROWS):
                shift = (l * 11 + r) * 23
                row = tabs[g]
                if shift:
                    row = pltpu.roll(row, 768 - shift, 1)
                for h in range(HEADS):
                    n = h * 12 + l * ROWS + r
                    u[n : n + 1, :] = row[h : h + 1, :512]
        t0 = u[...]
        hi = t0.astype(BF)
        rest = t0 - hi.astype(F32)
        mid = rest.astype(BF)
        low = (rest - mid.astype(F32)).astype(BF)
        split = jnp.concatenate([hi, mid, low], 0)
        for c in range(WLON):
            v = mm_nt(split, et[c * WTOK : (c + 1) * WTOK, :])
            v = v[0:48] + v[48:96] + v[96:144]
            wide[0, pl.ds(c, 48, stride=WLON), :] = v[:, 0:128]
            wide[1, pl.ds(c, 48, stride=WLON), :] = jnp.concatenate(
                [v[:, 128:WTOK], jnp.zeros((48, 256 - WTOK), F32)], 1
            )
        for h in range(HEADS):
            rows = slice(h * WTOK, (h + 1) * WTOK)
            both = jnp.concatenate([wide[0, rows, :], wide[1, rows, 0 : WTOK - 128]], 1)
            bm[g, rows, :] = jnp.where(allowed, both, NEG)

    tabs[tp] = jnp.zeros((8, 768), F32)
    tabs[tp, 0:HEADS, 0:NREL] = tab_ref[...]
    loads[0].wait()
    loads[1].wait()
    for m, lo, hi in ((QL2, 304, 608), (QL, 256, 304)):
        sp[lo:hi, :] = mm(pick(maps, m, hi - lo, TOK, lo), lat[...]).astype(BF)
    for m, lo, hi in ((QC2, 112, 224), (QC, 96, 112)):
        sc[lo:hi, :] = mm(pick(maps, m, hi - lo, 144, lo), cg[...]).astype(BF)
    loads[2].wait()
    loads[3].wait()
    at = pl.ds(pl.multiple_of(core * 256 + yy * 64, 64), 64)
    pat = pl.ds(pl.multiple_of(core * 128 + yy * 32, 32), 32)
    half = pl.ds(pl.multiple_of(core * 256, 256), 256)
    phalf = pl.ds(pl.multiple_of(core * 128, 128), 128)
    pl.semaphore_wait(barrier, len(partners))
    chalo = [links.send(sc.at[112:208], cc.at[112:208], device(0, 1, 0))]
    halo = [links.send(sp.at[304:560], pc.at[304:560], device(0, 1, 0))]
    chalo.append(links.send(sc.at[208:224], cc.at[208:224], device(1, 1, 0)))
    chalo.append(links.send(sc.at[96:112], cc.at[96:112], device(1, 0, 0)))
    first = [
        links.send(wf.at[tp, :, at], wf.at[tp, :, at], peer),
        links.send(pf.at[tp, pat], pf.at[tp, pat], peer),
    ]
    halo.append(links.send(sp.at[560:608], pc.at[560:608], device(1, 1, 0)))
    halo.append(links.send(sp.at[256:304], pc.at[256:304], device(1, 0, 0)))
    tabc = [links.send(tabs.at[tp], tabs.at[tp], peer)]
    pc[0:256, :] = mm(pick(maps, QL, 256, TOK), lat[...]).astype(BF)
    cc[0:96, :] = mm(pick(maps, QC, 96, 144), cg[...]).astype(BF)
    for c in range(WLON):
        et[c * WTOK : (c + 1) * WTOK, :] = pick(maps, E0 + c, WTOK, 512)
    loads[4].wait()
    wait(chalo)
    cmt[...] = mm(pick(maps, PC, 192, 224), cc[...]).astype(BF)
    for n in range(4):
        cols = slice(n * 512, (n + 1) * 512)
        dmo[:, cols] = mm_nt(cmt[...], mw[cols, :]).astype(BF)
    dmc = [links.send(dmo.at[48:144], dmp.at[48:144], peer)]
    dmh = [
        links.send(dmo.at[0:48], dmp.at[0:48], peer),
        links.send(dmo.at[144:192], dmp.at[144:192], peer),
    ]
    wait(first)
    ring = []
    for dev in y_devs:
        for ref in (wf.at[other, :, at], pf.at[other, pat]):
            ring.append(links.send(ref, ref, dev))
    build_bias(tp)
    wait(halo)

    x = mm(pick(maps, PXW, TOK, 608), pc[...])
    xw[...] = x.astype(BF)
    normed, _ = layer_stats(x)
    hn[...] = (normed * gain_ref[...]).astype(BF)

    def forward(g):
        for n in range(3):
            qkv[g, :, n * DA : (n + 1) * DA] = mm(hn[...], wf[g, n]).astype(BF)

        def window(w, carry):
            rows = pl.ds(pl.multiple_of(w * WTOK, 16), WTOK)
            q = qkv[g, rows, 0:DA]
            k = qkv[g, rows, DA : 2 * DA]
            v = qkv[g, rows, 2 * DA : 3 * DA]
            s = mm_nt(stack_heads(q), k) * scale + bm[g]
            e = jnp.exp(s - jnp.max(s, -1, keepdims=True))
            p = e / jnp.sum(e, -1, keepdims=True)
            pr[g, w] = p
            pb = p.astype(BF)
            vs = stack_heads(v)
            o = jnp.zeros((WTOK, DA), F32)
            for h in range(HEADS):
                hs = slice(h * WTOK, (h + 1) * WTOK)
                o = o + mm(pb[hs], vs[hs])
            ao[g, rows, :] = o.astype(BF)
            return carry

        lax.fori_loop(0, NWIN, window, 0)

    forward(tp)
    features = pick(maps, FP, D, D)
    hnp[...] = mm(hn[...], features).astype(BF)
    wait(ring)
    pair = [links.send(r, r, core_dev) for r in (wf.at[other, :, half], pf.at[other, phalf])]
    wait(tabc)
    build_bias(other)
    wait(pair)
    forward(other)
    def residual(lo, hi):
        to_merge = pick(maps, PWM, hi - lo, TOK, lo)
        x = mm(pick(maps, PXM, hi - lo, 608, lo), pc[...])
        for g in range(2):
            x = x + mm(mm(to_merge, ao[g]).astype(BF), pf[g])
        y[lo:hi, :] = x.astype(BF)

    residual(0, 96)
    yhc = [links.send(y.at[0:96], yh.at[1], device(0, -1, 0))]
    residual(480, 576)
    yhc.append(links.send(y.at[480:576], yh.at[0], device(0, 1, 0)))
    residual(96, 480)

    wait(dmc)
    mgain = mgain_ref[...]
    acc = jnp.zeros((1, 4 * D), F32)

    def slab(r, cp):
        lo = cp * 48
        if r == 0:
            return yh[0, lo : lo + 48, :]
        if r == 7:
            return yh[1, lo : lo + 48, :]
        lo += (r - 1) * 96
        return y[lo : lo + 48, :]

    for cr in (1, 2, 0, 3):
        if cr == 0:
            wait(yhc)
            wait(dmh)
        slabs = [slab(2 * cr + rp, cp) for rp in (0, 1) for cp in (0, 1)]
        hat, inv = layer_stats(jnp.concatenate(slabs, 1).astype(F32))
        rows = slice(cr * 48, (cr + 1) * 48)
        dm = dmo[rows, :].astype(F32) + dmp[rows, :].astype(F32)
        if cr > 0:
            acc = acc + jnp.sum(dm * hat, 0, keepdims=True)
            mb[(cr - 1) * 48 : cr * 48, :] = (hat * mgain).astype(BF)
        dy = norm_back(dm, mgain, hat, inv).astype(BF)
        for q in range(4):
            r = 2 * cr + q // 2
            if 1 <= r <= 6:
                lo = (r - 1) * 96 + (q % 2) * 48
                dyt[lo : lo + 48, :] = dy[:, q * D : (q + 1) * D]
    mg[...] = acc

    for iz in range(NZ):
        part = mm_tn(mb[:, iz * 256 : (iz + 1) * 256], cmt[48:192, :])
        gm[iz] = part.reshape(2, NY, 32, 512)
    turns = [lax.rem(yy + k, NY) for k in FAR_Y + (0,)]
    m1 = []
    for iy in turns:
        for iz in range(NZ):
            sm1[iy, iz] = gm[iz, 1 - core, iy].astype(BF)
        m1.append(links.send(sm1.at[iy], rm1.at[iy], core_dev))

    dyw[...] = mm(pick(maps, PMW, TOK, TOK), dyt[...]).astype(BF)
    for g in range(2):
        do[g] = mm_nt(dyw[...], pf[g]).astype(BF)
    dst[...] = jnp.zeros_like(dst)

    def backward(g, mine, lo=0, hi=NWIN):
        def window(w, carry):
            rows = pl.ds(pl.multiple_of(w * WTOK, 16), WTOK)
            q = qkv[g, rows, 0:DA]
            k = qkv[g, rows, DA : 2 * DA]
            v = qkv[g, rows, 2 * DA : 3 * DA]
            p = pr[g, w]
            dos = stack_heads(do[g, rows, :])
            dp = mm_nt(dos, v)
            dv = mm_tn(p.astype(BF), dos)
            ds = p * (dp - jnp.sum(dp * p, -1, keepdims=True))
            if mine:
                dst[...] = dst[...] + ds
            dsb = ds.astype(BF)
            dk = mm_tn(dsb, stack_heads(q)) * scale
            ks = stack_heads(k)
            dq = jnp.zeros((WTOK, DA), F32)
            for h in range(HEADS):
                hs = slice(h * WTOK, (h + 1) * WTOK)
                dq = dq + mm(dsb[hs], ks[hs])
            dqkv[g, 0, rows, :] = (dq * scale).astype(BF)
            dqkv[g, 1, rows, :] = dk.astype(BF)
            dqkv[g, 2, rows, :] = dv.astype(BF)
            return carry

        lax.fori_loop(lo, hi, window, 0)

    m2 = []
    for n, k in enumerate(FAR_Y):
        wait(m1[n : n + 1])
        iy = turns[n]
        for iz in range(NZ):
            sm2[k - 1, iz] = (gm[iz, core, iy] + rm1[iy, iz].astype(F32)).astype(BF)
        m2.append(links.send(sm2.at[k - 1], rm2.at[k - 1], y_devs[k - 1]))
    wait(m1[3:])

    backward(tp, True)

    dyp[...] = mm(dyw[...], features).astype(BF)
    for n in range(4):
        part = mm_tn(hnp[...], dqkv[tp, n]) if n < 3 else mm_tn(dyp[...], ao[tp])
        gq[:, :, :, :, n * DA : (n + 1) * DA] = part.reshape(2, 2, NY, 32, DA)
    sq1[...] = gq[1 - core].astype(BF)
    q1 = [links.send(sq1, rq1, core_dev)]
    for iz in range(NZ):
        am[iz] = gm[iz, core, yy] + rm1[yy, iz].astype(F32)

    wide[0] = dst[:, 0:128]
    wide[1, :, 0 : WTOK - 128] = dst[:, 128:WTOK]
    acc = jnp.zeros((48, 512), F32)
    for c in range(WLON):
        rows = pl.ds(c, 48, stride=WLON)
        x = jnp.concatenate([wide[0, rows, :], wide[1, rows, :][:, 0 : WTOK - 128]], 1)
        hi = x.astype(BF)
        low = (x - hi.astype(F32)).astype(BF)
        v = mm(jnp.concatenate([hi, low], 0), et[c * WTOK : (c + 1) * WTOK, :])
        acc = acc + v[0:48] + v[48:96]
    t[:, 0:512] = acc
    t[:, 512:768] = jnp.zeros((48, 256), F32)
    for h in range(HEADS):
        out = jnp.zeros((1, 768), F32)
        for g in range(12):
            row = t[h * 12 + g : h * 12 + g + 1, :]
            shift = (g // ROWS * 11 + g % ROWS) * 23
            out = out + (pltpu.roll(row, shift, 1) if shift else row)
        sv[h : h + 1, :] = out
    sv[4:5, :] = mg[:, 0:768]
    sv[5:6, :] = mg[:, 768:1536]
    sv[6:7, 0:512] = mg[:, 1536:2048]
    sv[6:7, 512:768] = jnp.zeros((1, 256), F32)
    sv[7:8, :] = jnp.zeros((1, 768), F32)
    sv1[core] = sv[...]
    v1 = [links.send(sv1.at[core], sv1.at[core], core_dev)]

    wait(q1)
    sq2[...] = (gq[core, 1 - xx] + rq1[1 - xx].astype(F32)).astype(BF)
    q2 = [links.send(sq2, rq2, x_dev)]
    aq[...] = gq[core, xx] + rq1[xx].astype(F32)
    wait(v1)
    sv2[z] = sv1[0] + sv1[1]
    v2 = [links.send(sv2.at[z], sv2.at[z], dev) for dev in z_devs]

    backward(other, False)

    wait(q2)
    q3 = []
    for k in FAR_Y:
        iy = lax.rem(yy + k, NY)
        sq3[k - 1] = (aq[iy] + rq2[iy].astype(F32)).astype(BF)
        q3.append(links.send(sq3.at[k - 1], rq3.at[k - 1], y_devs[k - 1]))
    bq[...] = aq[yy] + rq2[yy].astype(F32)

    wait(m2)
    for iz in range(NZ):
        acc = am[iz]
        for k in range(NY - 1):
            acc = acc + rm2[k, iz].astype(F32)
        bmm[iz] = acc
    m3 = []
    for k in FAR_Z:
        sm3[k - 1] = bmm[lax.rem(z + k, NZ)].astype(BF)
        m3.append(links.send(sm3.at[k - 1], rm3.at[k - 1], z_devs[k - 1]))

    dh = jnp.zeros((TOK, D), F32)
    for g in range(2):
        for n in range(3):
            dh = dh + mm_nt(dqkv[g, n], wf[g, n])
    normed, inv = layer_stats(xw[...].astype(F32))
    av[...] = jnp.sum(dh * normed, 0, keepdims=True)
    me = (core * 2 + xx) * NY + yy
    av1[me] = av[...]
    a1 = [links.send(av1.at[me], av1.at[me], dev) for dev in group]
    branch = norm_back(dh, gain_ref[...], normed, inv).astype(BF)
    lg = (dyw[...].astype(F32) + branch.astype(F32)).astype(BF)
    lp[...] = mm(pick(maps, PPO, 608, TOK), lg).astype(BF)
    ro = [
        links.send(lp.at[304:560], rp_ref.at[304:560], device(0, -1, 0)),
        links.send(lp.at[256:304], rp_ref.at[256:304], device(-1, 0, 0)),
        links.send(lp.at[560:608], rp_ref.at[560:608], device(-1, -1, 0)),
    ]
    rp_ref[0:256, :] = lp[0:256, :]
    wait(v2)
    acc = sv2[0]
    for k in range(1, NZ):
        acc = acc + sv2[k]
    sv3[xx] = acc
    v3 = [links.send(sv3.at[xx], sv3.at[xx], x_dev)]
    wait(q3)
    acc = bq[...]
    for k in range(NY - 1):
        acc = acc + rq3[k].astype(F32)
    for iz in range(NZ):
        rows = slice(iz * 4, iz * 4 + 4)
        cq[iz] = jnp.concatenate([acc[rows, 0:512], acc[rows, 512:1024]], 0)
    q4 = []
    for k in FAR_Z:
        q4.append(links.send(cq.at[lax.rem(z + k, NZ)], rq4.at[k - 1], z_devs[k - 1]))

    wait(a1)
    acc = av1[0]
    for k in range(1, 4 * NY):
        acc = acc + av1[k]
    av2[z] = acc
    a2 = [links.send(av2.at[z], av2.at[z], dev) for dev in z_devs]
    wait(v3)
    sv4[yy] = sv3[0] + sv3[1]
    v4 = [links.send(sv4.at[yy], sv4.at[yy], dev) for dev in y_devs]

    wait(m3)
    acc = bmm[z]
    for k in range(NZ - 1):
        acc = acc + rm3[k].astype(F32)
    cm[0] = acc[0:16]
    cm[1] = acc[16:32]
    m4 = [links.send(cm.at[1 - xx], rm4, x_dev)]
    wait(m4)
    om_ref[...] = cm[xx] + rm4[...]
    wait(q4)
    acc = cq[z]
    for k in range(NZ - 1):
        acc = acc + rq4[k]
    oq_ref[...] = acc
    wait(v4)
    ov_ref[...] = sv4[0] + sv4[1] + sv4[2] + sv4[3]
    wait(a2)
    acc = av2[0]
    for k in range(1, NZ):
        acc = acc + av2[k]
    oa_ref[...] = acc
    wait(ro)


def kend(
    maps, rp_ref, om_ref, oq_ref, ov_ref, oa_ref, lg_ref, ag_ref, gw_ref, gp_ref, gb_ref, mg_ref,
    gm_ref,
):
    lg_ref[...] = mm(pick(maps, PF, TOK, 608), rp_ref[...]).astype(BF)
    gm_ref[...] = om_ref[...]
    gw_ref[0] = oq_ref[0:4, 0:DA]
    gw_ref[1] = oq_ref[0:4, DA : 2 * DA]
    gw_ref[2] = oq_ref[4:8, 0:DA]
    gp_ref[...] = oq_ref[4:8, DA : 2 * DA]
    gb_ref[...] = ov_ref[0:HEADS, 0:NREL]
    mg_ref[:, 0:768] = ov_ref[4:5, :]
    mg_ref[:, 768:1536] = ov_ref[5:6, :]
    mg_ref[:, 1536:2048] = ov_ref[6:7, 0:512]
    ag_ref[...] = oa_ref[...]


def local(
    latent, pole_mask, attn_gain, qkv_weight, proj_weight, rel_bias, merge_gain, merge_weight,
    coarse_grad,
):
    maps = jnp.asarray(index_maps())
    dma = pltpu.SemaphoreType.DMA
    vm = pltpu.VMEM
    nb = HEADS * WTOK
    nv, na = (8, 768), (1, D)
    sends = 96
    rp, om, oq, ov, oa = call(
        kmain, "sublayer_backward",
        [
            pole_mask, maps, rel_bias, attn_gain.reshape(1, D), merge_gain.reshape(1, 4 * D),
            latent.reshape(TOK, D), coarse_grad.reshape(144, 512), qkv_weight.transpose(1, 0, 2),
            proj_weight, merge_weight,
        ],
        [((608, D), BF), ((16, 512), F32), ((8, 512), F32), (nv, F32), (na, F32)],
        [
            vm((TOK, D), BF), vm((144, 512), BF), vm((4 * D, 512), BF), vm((2, 3, D, DA), BF),
            vm((2, DA, D), BF), vm((2, 8, 768), F32), vm((WLON * WTOK, 512), BF),
            vm((2, nb, WTOK), F32), vm((48, 512), F32), vm((2, nb, 128), F32),
            vm((608, D), BF), vm((224, 512), BF), vm((608, D), BF), vm((224, 512), BF),
            vm((192, 512), BF), vm((192, 4 * D), BF), vm((192, 4 * D), BF),
            vm((TOK, D), BF), vm((TOK, D), BF), vm((TOK, D), BF), vm((2, TOK, 3 * DA), BF),
            vm((2, NWIN, nb, WTOK), F32), vm((2, TOK, DA), BF), vm((TOK, D), BF),
            vm((2, 96, D), BF), vm((144, 4 * D), BF), vm((TOK, D), BF), vm((1, 4 * D), F32),
            vm((NZ, 2, NY, 32, 512), F32), vm((TOK, D), BF), vm((TOK, D), BF),
            vm((2, TOK, DA), BF),
            vm((2, 3, TOK, DA), BF), vm((nb, WTOK), F32), vm((48, 768), F32),
            vm((2, 2, NY, 32, 1024), F32), vm((608, D), BF), vm(nv, F32), vm(na, F32),
            vm((NY, NZ, 32, 512), BF), vm((2, NY, 32, 1024), BF),
            vm((NY, NZ, 32, 512), BF), vm((2, NY, 32, 1024), BF), vm((2,) + nv, F32),
            vm((4 * NY,) + na, F32),
            vm((NZ, 32, 512), F32), vm((NY - 1, NZ, 32, 512), BF), vm((NY - 1, NZ, 32, 512), BF),
            vm((NZ, 32, 512), F32), vm((NZ - 1, 32, 512), BF), vm((NZ - 1, 32, 512), BF),
            vm((2, 16, 512), F32), vm((16, 512), F32),
            vm((NY, 32, 1024), F32), vm((NY, 32, 1024), BF), vm((NY, 32, 1024), BF),
            vm((32, 1024), F32), vm((NY - 1, 32, 1024), BF), vm((NY - 1, 32, 1024), BF),
            vm((NZ, 8, 512), F32), vm((NZ - 1, 8, 512), F32),
            vm((NZ,) + nv, F32), vm((2,) + nv, F32), vm((NY,) + nv, F32), vm((NZ,) + na, F32),
            dma((5,)), dma((sends,)), dma((sends,)),
        ],
        cid=1, mib=58, smem=1, hbm=5,
    )
    lg, ag, gw, gp, gb, mgg, gmm = call(
        kend, "finish", [maps, rp, om, oq, ov, oa],
        [
            ((TOK, D), BF), ((1, D), F32), ((3, 4, DA), F32), ((4, DA), F32),
            ((HEADS, NREL), F32), ((1, 4 * D), F32), ((16, 512), F32),
        ],
        mib=58,
    )
    return (
        lg.reshape(latent.shape),
        ag.reshape(D),
        gw.transpose(1, 0, 2),
        gp.T,
        gb,
        mgg.reshape(4 * D),
        gmm,
    )


def solution(mesh):
    placed = (
        P(None, "lat", "lon", None),
        P(),
        P(),
        P(None, None, "tp"),
        P("tp", None),
        P("tp", None),
        P(),
        P(None, "tp"),
        P(None, "lat", "lon", "tp"),
    )
    return jax.shard_map(
        local,
        mesh=mesh,
        in_specs=placed,
        out_specs=(
            P(None, "lat", "lon", None),
            P(),
            P(("lon", "lat"), None, "tp"),
            P("tp", ("lon", "lat")),
            P("tp", None),
            P(),
            P(("lon", "lat"), "tp"),
        ),
        check_vma=False,
    )
```
